256 devices in a mesh: gx: 16 (over y_hi, x, core), gy: 16 (over z, y_lo).
Axes of the slice: x: 4, y: 4 (y_hi: 2, y_lo: 2; y = y_hi * 2 + y_lo), z: 8, core: 2. Of those that a mesh axis runs over, the one named last changes fastest.
Arguments:
- block_ids: int32 [2, 1024, 4096], P(None, 'gx', 'gy'), may hold values from 0 to 31
- block_power: float32 [32], replicated, may hold values from 0.2 to 5
- layer_class: int32 [2, 4], replicated, may hold values from 0 to 3
- power_share: float32 [4], replicated, may hold values from 0.1 to 1
- lateral_k: float32 [4], replicated, may hold values from 0.3 to 3
- vertical_k: float32 [4], replicated, may hold values from 0.3 to 3
- sink_conductance: float32 [2], replicated, may hold values from 0.5 to 3
- bond_conductance: float32 [1024, 4096], P('gx', 'gy'), may hold values from 0.5 to 4
- peak_heat_factors_flipped: float32 [2, 4, 1024, 4096], P(None, None, 'gx', 'gy'), may hold values from 0.1 to 2
- sensor_weight: float32 [2, 4, 1024, 4096], P(None, None, 'gx', 'gy'), may hold values from -6 to 6
Outputs:
- thermal_excess: float32 [2, 4, 1024, 4096], P(None, None, 'gx', 'gy')
- peak_heat_sensitivity: float32 [2, 4, 1024, 4096], P(None, None, 'gx', 'gy')
- sensor_heat_sensitivity: float32 [2, 4, 1024, 4096], P(None, None, 'gx', 'gy')
The draws below stay inside these ranges and needn't reach their ends.
All inputs are finite; a program needn't handle non-finite values.
Results may differ from the reference program's by a relative error of at most 0.00002.
Values sent between devices are 32-bit elements; how exact they have to be, the bound alone decides.
No kernel may reach another device: no remote copies, remote signals or barrier semaphores. Data moves between devices by JAX's collectives and lax.ppermute only.
A program may use at most 64 MiB of HBM per device.

```python
import math
import jax
import jax.numpy as jnp

LAYERS = 4
SWEEPS = 4
BLOCKS = 32
CLASSES = 4
NX = 1024
NY = 4096


def place_ends(values, stream_key, least, top_value):
    spot = [jax.random.randint(jax.random.fold_in(stream_key, axis), (), 0, length) for axis, length in enumerate(values.shape)]
    longest = values.shape.index(max(values.shape))
    neighbour = spot[:longest] + [(spot[longest] + 1) % values.shape[longest]] + spot[longest + 1:]
    return values.at[tuple(spot)].set(least).at[tuple(neighbour)].set(top_value)


def levels(rng, shape, cuts, smallest, top_value):
    level = 1.0
    for dim, shards_of in cuts:
        draws = jax.random.uniform(jax.random.fold_in(jax.random.fold_in(rng, 6), dim), (shards_of,), jnp.float32, smallest / len(cuts), top_value / len(cuts))
        level = level * jnp.repeat(jnp.exp(draws), shape[dim] // shards_of).reshape((-1,) + (1,) * (len(shape) - 1 - dim))
    return level


def noise(own_key, dims, spread, most, pieces=(), kind=jnp.bfloat16):
    values = jax.random.normal(own_key, dims, jnp.float32) * spread
    if len(pieces) > 0:
        values = levels(own_key, dims, pieces, -0.22, 0.18) * values
    return jnp.clip(values, min=-most, max=most).astype(kind)


def setup_inputs(seed: int = 0) -> dict:
    streams_of = jax.random.split(jax.random.key(seed), 11)
    block_ids = place_ends(jax.random.randint(streams_of[0], (2, NX, NY), 0, BLOCKS), jax.random.fold_in(streams_of[0], 1), 0, BLOCKS - 1).astype(jnp.int32)
    block_power = jnp.clip(jnp.exp(jax.random.uniform(streams_of[1], (BLOCKS,), jnp.float32, math.log(0.2), math.log(5.0))), 0.2, 5.0)
    layer_class = place_ends(jax.random.randint(streams_of[2], (2, LAYERS), 0, CLASSES), jax.random.fold_in(streams_of[2], 1), 0, CLASSES - 1).astype(jnp.int32)
    power_share = jnp.clip(jnp.exp(jax.random.uniform(streams_of[3], (CLASSES,), jnp.float32, math.log(0.1), math.log(1.0))), 0.1, 1.0)
    lateral_k = jnp.clip(jnp.exp(jax.random.uniform(streams_of[4], (CLASSES,), jnp.float32, math.log(0.3), math.log(3.0))), 0.3, 3.0)
    vertical_k = jnp.clip(jnp.exp(jax.random.uniform(streams_of[5], (CLASSES,), jnp.float32, math.log(0.3), math.log(3.0))), 0.3, 3.0)
    sink_conductance = jnp.clip(jnp.exp(jax.random.uniform(streams_of[6], (2,), jnp.float32, math.log(0.5), math.log(3.0))), 0.5, 3.0)
    bond_conductance = jnp.clip(jnp.exp(math.log(4.0) - 2.0794415 * jax.random.uniform(streams_of[7], (NX, NY), jnp.float32) ** levels(streams_of[7], (NX, NY), ((0, 16), (1, 16)), -0.2, 0.2)), 0.5, 4.0)
    peak_heat_factors_flipped = jnp.clip(jnp.exp(math.log(2.0) - 2.9957323 * jax.random.uniform(streams_of[8], (2, LAYERS, NX, NY), jnp.float32) ** levels(streams_of[8], (2, LAYERS, NX, NY), ((2, 16), (3, 16)), -0.2, 0.2)), 0.1, 2.0)
    sensor_weight = noise(streams_of[9], (2, LAYERS, NX, NY), 1.0, 6.0, ((2, 16), (3, 16)), jnp.float32)
    return {"block_ids": block_ids, "block_power": block_power, "layer_class": layer_class, "power_share": power_share, "lateral_k": lateral_k, "vertical_k": vertical_k, "sink_conductance": sink_conductance, "bond_conductance": bond_conductance, "peak_heat_factors_flipped": peak_heat_factors_flipped, "sensor_weight": sensor_weight}


def flip_upper_layer(array):
    return jnp.stack([array[0], jnp.flip(array[1], axis=-2)])


def reference(block_ids, block_power, layer_class, power_share, lateral_k, vertical_k, sink_conductance, bond_conductance, peak_heat_factors_flipped, sensor_weight):
    cell_blocks = flip_upper_layer(block_ids)
    share = power_share[layer_class]
    heating_rate_field = block_power[cell_blocks][:, None] * share[:, :, None, None]
    level = jnp.arange(LAYERS)
    lateral_g = lateral_k[layer_class][:, :, None, None]
    upper_g = jnp.where(level[None, :] < LAYERS - 1, vertical_k[layer_class], 0.0)
    lower_g = jnp.concatenate([jnp.zeros((2, 1), jnp.float32), upper_g[:, :-1]], axis=1)
    upper_g = upper_g[:, :, None, None]
    lower_g = lower_g[:, :, None, None]
    face_mask = (level == LAYERS - 1).astype(jnp.float32)[None, :, None, None]
    sink_mask = (level == 0).astype(jnp.float32)[None, :, None, None]
    matrix_main_line = 4.0 * lateral_g + upper_g + lower_g + face_mask * bond_conductance[None, None] + sink_mask * sink_conductance[:, None, None, None]

    def neighbours(values):
        padded = jnp.pad(values, ((0, 0), (0, 0), (1, 1), (1, 1)))
        lateral = padded[:, :, 2:, 1:-1] + padded[:, :, :-2, 1:-1] + padded[:, :, 1:-1, 2:] + padded[:, :, 1:-1, :-2]
        zero_layer = jnp.zeros_like(values[:, :1])
        upper = jnp.concatenate([values[:, 1:], zero_layer], axis=1)
        lower = jnp.concatenate([zero_layer, values[:, :-1]], axis=1)
        other_die = values[::-1, LAYERS - 1][:, None]
        return lateral_g * lateral + upper_g * upper + lower_g * lower + face_mask * bond_conductance[None, None] * other_die

    def pointwise_iterative_update(source):
        values = jnp.zeros_like(source)
        for sweep_index in range(SWEEPS):
            values = (source + neighbours(values)) / matrix_main_line
        return values

    thermal_excess = pointwise_iterative_update(heating_rate_field)
    peak_heat_sensitivity = pointwise_iterative_update(flip_upper_layer(peak_heat_factors_flipped) * thermal_excess)
    sensor_heat_sensitivity = pointwise_iterative_update(flip_upper_layer(sensor_weight))
    return flip_upper_layer(thermal_excess), flip_upper_layer(peak_heat_sensitivity), flip_upper_layer(sensor_heat_sensitivity)
```

```python
import functools

import jax
import jax.numpy as jnp
from jax import lax
from jax.experimental import pallas as pl
from jax.experimental.pallas import tpu as pltpu
from jax.sharding import PartitionSpec as P


BLOCKS = 32
ROWS = 80
DEEP = 6
NEAR = 3
F32 = jnp.float32

VMEM = pl.BlockSpec(memory_space=pltpu.VMEM)
SMEM = pl.BlockSpec(memory_space=pltpu.SMEM)

STRIP_H = [DEEP] * 3 + [NEAR] * 16
STRIP_AT = [sum(STRIP_H[:n]) for n in range(19)]
PART_H = [DEEP] * 3 + [2, 1] * 4
PART_AT = [2 * sum(PART_H[:n]) for n in range(11)]


def lanes():
    return lax.broadcasted_iota(jnp.int32, (8, 128), 1)


def sublanes():
    return lax.broadcasted_iota(jnp.int32, (8, 128), 0)


def rolled(x, shift, axis):
    size = x.shape[axis]
    shift %= size
    return x if shift == 0 else pltpu.roll(x, shift, axis)


def mirrored(x):
    return jnp.take_along_axis(x, 7 - sublanes(), axis=0)


def field_tile(refs, n, rows, t):
    power, bond, sensor, peak = refs
    if n < 2:
        return power[n, t, rows, :]
    cut = slice(128 * t, 128 * t + 128)
    if n == 2:
        return bond[rows, cut]
    field = sensor if n < 11 else peak
    m = (n - 3) % 8
    return field[m // 4, m % 4, rows, cut]


def ring_tile(from_right, from_left, n):
    h, at = STRIP_H[n], STRIP_AT[n]
    lane = lanes()
    return jnp.where(
        lane < h,
        rolled(from_right, -at, 1),
        jnp.where(lane >= 128 - h, rolled(from_left, 128 - h - at, 1), 0.0),
    )


def flip_layers_kernel(field, out):
    for d in range(2):
        for l in range(3):
            for t in range(2):
                for k in range(8):
                    out[d, l, t, 8 * (7 - k) : 8 * (8 - k), :] = mirrored(
                        field[d, l + 1, 8 * k : 8 * k + 8, 128 * t : 128 * t + 128]
                    )


def column_kernel(place, block_power, ids, bond, sensor, peak, power, to_a, to_b):
    values = [block_power[n] for n in range(BLOCKS)]

    def look_up(k, _):
        rows = pl.ds(pl.multiple_of(8 * k, 8), 8)
        for d in range(2):
            for t in range(2):
                index = ids[d, rows, 128 * t : 128 * t + 128]
                level = values
                bit = 1
                while len(level) > 1:
                    odd = (index & bit) != 0
                    level = [
                        jnp.where(odd, level[2 * n + 1], level[2 * n])
                        for n in range(len(level) // 2)
                    ]
                    bit *= 2
                power[d, t, rows, :] = level[0]
        return 0

    lax.fori_loop(0, 8, look_up, 0)
    even = (place[1] & 1) == 0
    refs = (power, bond, sensor, peak)

    def pack(k, _):
        rows = pl.ds(pl.multiple_of(8 * k, 8), 8)
        lane = lanes()
        right_edge = jnp.zeros((8, 128), F32)
        left_edge = jnp.zeros((8, 128), F32)
        for n in range(19):
            h, at = STRIP_H[n], STRIP_AT[n]
            here = (lane >= at) & (lane < at + h)
            left_edge = jnp.where(here, rolled(field_tile(refs, n, rows, 0), at, 1), left_edge)
            right_edge = jnp.where(
                here, rolled(field_tile(refs, n, rows, 1), at - (128 - h), 1), right_edge
            )
        to_a[rows, :] = jnp.where(even, right_edge, left_edge)
        to_b[rows, :] = jnp.where(even, left_edge, right_edge)
        return 0

    lax.fori_loop(0, 8, pack, 0)


def sides(place, axis, from_a, from_b, rows):
    even = (place[axis] & 1) == 0
    a, b = from_a[rows, :], from_b[rows, :]
    return jnp.where(even, a, b), jnp.where(even, b, a)


def row_kernel(place, power, bond, sensor, peak, col_a, col_b, to_a, to_b):
    even = (place[0] & 1) == 0
    refs = (power, bond, sensor, peak)
    row = sublanes()
    strips = []
    for first in (0, 56):
        rows = slice(first, first + 8)
        right, left = sides(place, 1, col_a, col_b, rows)

        def tile(n, t):
            return field_tile(refs, n, rows, t) if t < 2 else ring_tile(right, left, n)

        strip = []
        for t in range(3):
            for n in range(3):
                strip.append(tile(n, t))
            for m in range(8):
                x, y = tile(3 + 2 * m, t), tile(4 + 2 * m, t)
                if first == 0:
                    strip.append(jnp.where(row < 4, x, rolled(y, 4, 0)))
                else:
                    strip.append(jnp.where(row >= 4, x, rolled(y, -4, 0)))
        strips.append(strip)
    top, bottom = strips
    for n in range(33):
        rows = slice(8 * n, 8 * n + 8)
        to_a[rows, :] = jnp.where(even, bottom[n], top[n])
        to_b[rows, :] = jnp.where(even, top[n], bottom[n])


def build_kernel(place, power, bond, sensor, peak, col_a, col_b, row_a, row_b, own, message):
    refs = (power, bond, sensor, peak)

    def core(k, _):
        rows = pl.ds(pl.multiple_of(8 * k, 8), 8)
        to = pl.ds(pl.multiple_of(8 * k + 8, 8), 8)
        right, left = sides(place, 1, col_a, col_b, rows)
        for n in range(19):
            own[n, 0, to, :] = field_tile(refs, n, rows, 0)
            own[n, 1, to, :] = field_tile(refs, n, rows, 1)
            own[n, 2, to, :] = ring_tile(right, left, n)
        return 0

    lax.fori_loop(0, 8, core, 0)
    for t in range(3):
        for n in range(11):
            at = 8 * (11 * t + n)
            below, above = sides(place, 0, row_a, row_b, slice(at, at + 8))
            if n < 3:
                own[n, t, 0:8, :] = above
                own[n, t, 72:80, :] = below
            else:
                m = 3 + 2 * (n - 3)
                own[m, t, 0:8, :] = above
                own[m, t, 72:80, :] = below
                own[m + 1, t, 0:8, :] = rolled(above, 4, 0)
                own[m + 1, t, 72:80, :] = rolled(below, -4, 0)

    def pack(k, _):
        rows = pl.ds(pl.multiple_of(8 * k, 8), 8)
        back = 8 * (9 - k)
        lane = lanes()
        for n in range(3):
            for t in range(2):
                to = pl.ds(pl.multiple_of(80 * (2 * n + t) + back, 8), 8)
                message[to, :] = mirrored(own[n, t, rows, :])
        column = jnp.zeros((8, 128), F32)
        planes = [0, 1, 2]
        for field in range(2):
            for d in range(2):
                planes += [3 + 8 * field + 4 * d + 3, 3 + 8 * field + 4 * d + 2]
        for slot, n in enumerate(planes):
            h, at = PART_H[slot], PART_AT[slot]
            here = (lane >= at) & (lane < at + 2 * h)
            column = jnp.where(here, rolled(own[n, 2, rows, :], at + h, 1), column)
        message[pl.ds(pl.multiple_of(480 + back, 8), 8), :] = mirrored(column)
        return 0

    lax.fori_loop(0, 10, pack, 0)
    row = sublanes()
    for field in range(2):
        for d in range(2):
            n = 3 + 8 * field + 4 * d
            for t in range(2):
                above = jnp.where(
                    row >= 4, own[n + 3, t, 0:8, :], rolled(own[n + 2, t, 0:8, :], 4, 0)
                )
                below = jnp.where(
                    row < 4, own[n + 3, t, 72:80, :], rolled(own[n + 2, t, 72:80, :], 4, 0)
                )
                at = 560 + 16 * (4 * field + 2 * d + t)
                message[at : at + 8, :] = mirrored(below)
                message[at + 8 : at + 16, :] = mirrored(above)


def partner_ring(message, slot, rows):
    h, at = PART_H[slot], PART_AT[slot]
    lane = lanes()
    return jnp.where(
        (lane < h) | (lane >= 128 - h), rolled(message[rows, :], -(at + h), 1), 0.0
    )


class Solver:
    def __init__(self, place, tables, d, v, cond, v_scalars=None):
        self.place, self.d, self.v, self.cond = place, d, v, cond
        layer_class, share, lateral, vertical, sink = tables
        self.coef = []
        for side in range(2):
            die = d if side == 0 else 1 - d
            classes = [layer_class[die, l] for l in range(4)]
            coefs = []
            for l in range(4):
                g = lateral[classes[l]]
                up = vertical[classes[l]] if l < 3 else jnp.float32(0)
                down = vertical[classes[l - 1]] if l > 0 else jnp.float32(0)
                diagonal = 4 * g + up + down
                if l == 0:
                    diagonal = diagonal + sink[die]
                part = share[classes[l]] if share is not None else None
                if l < 3:
                    inverse = 1.0 / jnp.full((8, 128), diagonal, F32)
                    coefs.append(
                        (
                            inverse if part is None else inverse * part,
                            g * inverse,
                            up * inverse,
                            down * inverse,
                        )
                    )
                else:
                    coefs.append((diagonal, g, down, part))
            self.coef.append(coefs)

    def prepare(self, bond_tile):
        def body(k, _):
            rows = pl.ds(pl.multiple_of(8 * k, 8), 8)
            for t in range(3):
                bond = bond_tile(k, rows, t)
                self.cond[0, t, rows, :] = bond
                for side in range(2):
                    self.cond[1 + side, t, rows, :] = 1.0 / (self.coef[side][3][0] + bond)
            return 0

        lax.fori_loop(0, 10, body, 0)

    def masks(self, k):
        gx, gy = self.place[0], self.place[1]
        outside = ((k == 0) & (gx == 0)) | ((k == 9) & (gx == 15))
        row = jnp.where(outside, 0.0, 1.0).astype(F32)
        lane = lanes()
        right = jnp.where(gy == 15, 0.0, 1.0).astype(F32)
        left = jnp.where(gy == 0, 0.0, 1.0).astype(F32)
        ring = jnp.where(lane < 64, right, left)
        return row, row * ring

    def first(self, side, layers, source):
        def body(k, _):
            rows = pl.ds(pl.multiple_of(8 * k, 8), 8)
            to = pl.ds(pl.multiple_of(8 * k + 8, 8), 8)
            row, ring = self.masks(k)
            for t in range(3):
                mask = ring if t == 2 else row
                shared = {}
                for l in layers:
                    s = source(l, t, rows, shared)
                    coef = self.coef[side][l]
                    if l < 3:
                        s = s * coef[0]
                    else:
                        if coef[3] is not None:
                            s = s * coef[3]
                        s = s * self.cond[1 + side, t, rows, :]
                    self.v[0, side, l, t, to, :] = s * mask
            return 0

        lax.fori_loop(0, 10, body, 0)

    def sweep(self, b, side, layers, source, emit=None, core_only=False):
        v = self.v

        def body(k, _):
            rows = pl.ds(pl.multiple_of(8 * k, 8), 8)
            to = pl.ds(pl.multiple_of(8 * k + 8, 8), 8)
            row, ring = self.masks(k)
            lane = lanes()
            shared = {}
            for l in layers:
                coef = self.coef[side][l]
                centre = [v[b, side, l, t, to, :] for t in range(3)]
                forward = [pltpu.roll(c, 1, 1) for c in centre]
                backward = [pltpu.roll(c, 127, 1) for c in centre]
                for t in range(2 if core_only else 3):
                    left = jnp.where(lane == 0, forward[t - 1], forward[t])
                    right = jnp.where(lane == 127, backward[(t + 1) % 3], backward[t])
                    lateral = (left + right) + (
                        v[b, side, l, t, pl.ds(8 * k + 7, 8), :]
                        + v[b, side, l, t, pl.ds(8 * k + 9, 8), :]
                    )
                    s = source(l, t, rows, shared)
                    if l < 3:
                        total = s * coef[0] + coef[1] * lateral
                        total = total + coef[2] * v[b, side, l + 1, t, to, :]
                        if l > 0:
                            total = total + coef[3] * v[b, side, l - 1, t, to, :]
                    else:
                        if coef[3] is not None:
                            s = s * coef[3]
                        total = s + coef[1] * lateral
                        total = total + coef[2] * v[b, side, 2, t, to, :]
                        total = total + self.cond[0, t, rows, :] * v[b, 1 - side, 3, t, to, :]
                        total = total * self.cond[1 + side, t, rows, :]
                    if not core_only:
                        total = total * (ring if t == 2 else row)
                    if emit is None:
                        v[1 - b, side, l, t, to, :] = total
                    else:
                        emit(l, t, k, rows, total)
            return 0

        if core_only:
            lax.fori_loop(1, 9, body, 0)
        else:
            lax.fori_loop(0, 10, body, 0)

    def partial_solve(self, own_source, other_source, emit):
        self.first(0, (0, 1, 2, 3), own_source)
        self.first(1, (1, 2, 3), other_source)
        self.sweep(0, 0, (0, 1, 2, 3), own_source)
        self.sweep(0, 1, (2, 3), other_source)
        self.sweep(1, 0, (0, 1, 2, 3), own_source)
        self.sweep(1, 1, (3,), other_source)
        self.sweep(0, 0, (0, 1, 2, 3), own_source, emit, core_only=True)


def clear_pads(v):
    zero = jnp.zeros((8, 128), F32)
    for b in range(2):
        for side in range(2):
            for l in range(4):
                for t in range(3):
                    v[b, side, l, t, 0:8, :] = zero
                    v[b, side, l, t, 88:96, :] = zero


def place_other(planes, layers_in, message, field, d):
    other = 1 - d
    zero = jnp.zeros((8, 128), F32)

    def body(k, _):
        rows = pl.ds(pl.multiple_of(8 * k, 8), 8)
        to = pl.ds(pl.multiple_of(8 * k + 8, 8), 8)
        for l in range(3):
            for t in range(2):
                planes[l, t, to, :] = layers_in[other, l, t, rows, :]
        return 0

    lax.fori_loop(0, 8, body, 0)

    def ring(k, _):
        rows = pl.ds(pl.multiple_of(8 * k, 8), 8)
        column = message[pl.ds(pl.multiple_of(480 + 8 * k, 8), 8), :]
        lane = lanes()
        planes[0, 2, rows, :] = zero
        for slot_in, l, h in ((0, 2, 2), (1, 1, 1)):
            ats = [PART_AT[3 + 4 * field + 2 * die + slot_in] + h for die in range(2)]
            picked = jnp.where(other == 0, rolled(column, -ats[0], 1), rolled(column, -ats[1], 1))
            planes[l, 2, rows, :] = jnp.where((lane < h) | (lane >= 128 - h), picked, 0.0)
        return 0

    lax.fori_loop(0, 10, ring, 0)
    for t in range(2):
        planes[0, t, 0:8, :] = zero
        planes[0, t, 72:80, :] = zero
        at = 560 + 64 * field + 32 * other + 16 * t
        above = message[pl.ds(pl.multiple_of(at, 8), 8), :]
        below = message[pl.ds(pl.multiple_of(at + 8, 8), 8), :]
        planes[2, t, 0:8, :] = above
        planes[2, t, 72:80, :] = below
        planes[1, t, 0:8, :] = rolled(above, 4, 0)
        planes[1, t, 72:80, :] = rolled(below, -4, 0)


def thermal_sensor_kernel(
    place, layer_class, share, lateral, vertical, sink, own, layers_in, message,
    thermal, sensed, heat, v, cond, power, planes,
):
    clear_pads(v)

    def frame(d, _):
        solver = Solver(place, (layer_class, share, lateral, vertical, sink), d, v, cond)

        def bond_tile(k, rows, t):
            if t < 2:
                theirs = message[pl.ds(pl.multiple_of(80 * (4 + t) + 8 * k, 8), 8), :]
            else:
                theirs = partner_ring(message, 2, pl.ds(pl.multiple_of(480 + 8 * k, 8), 8))
            return jnp.where(d == 0, own[2, t, rows, :], theirs)

        solver.prepare(bond_tile)

        def other_power(k, _):
            rows = pl.ds(pl.multiple_of(8 * k, 8), 8)
            column = message[pl.ds(pl.multiple_of(480 + 8 * k, 8), 8), :]
            lane = lanes()
            for t in range(2):
                at = 160 * (1 - d) + 80 * t + 8 * k
                power[t, rows, :] = message[pl.ds(pl.multiple_of(at, 8), 8), :]
            picked = jnp.where(
                d == 1,
                rolled(column, -(PART_AT[0] + DEEP), 1),
                rolled(column, -(PART_AT[1] + DEEP), 1),
            )
            power[2, rows, :] = jnp.where((lane < DEEP) | (lane >= 128 - DEEP), picked, 0.0)
            return 0

        lax.fori_loop(0, 10, other_power, 0)

        def own_power(l, t, rows, shared):
            if t not in shared:
                shared[t] = own[d, t, rows, :]
            return shared[t]

        def their_power(l, t, rows, shared):
            if t not in shared:
                shared[t] = power[t, rows, :]
            return shared[t]

        every = (0, 1, 2, 3)
        solver.first(0, every, own_power)
        solver.first(1, every, their_power)
        for b in (0, 1):
            solver.sweep(b, 0, every, own_power)
            solver.sweep(b, 1, every, their_power)

        def emit_own(l, t, k, rows, total):
            heat[d, l, t, rows, :] = total

        def emit_other(l, t, k, rows, total):
            heat[d, 3 + l, t, rows, :] = total

        solver.sweep(0, 0, every, own_power, emit_own)
        solver.sweep(0, 1, (1, 2, 3), their_power, emit_other)

        def write(k, _):
            rows = pl.ds(pl.multiple_of(8 * k, 8), 8)
            at = pl.ds(pl.multiple_of(8 * k + 8, 8), 8)
            for l in range(4):
                for t in range(2):
                    thermal[d, l, rows, 128 * t : 128 * t + 128] = heat[d, l, t, at, :]
            return 0

        lax.fori_loop(0, 8, write, 0)

        place_other(planes, layers_in, message, 0, d)
        plain = Solver(place, (layer_class, None, lateral, vertical, sink), d, v, cond)

        def own_sensor(l, t, rows, shared):
            return own[3 + 4 * d + l, t, rows, :]

        def their_sensor(l, t, rows, shared):
            return planes[l - 1, t, rows, :]

        def emit(l, t, k, rows, total):
            at = pl.ds(pl.multiple_of(8 * k - 8, 8), 8)
            sensed[d, l, at, 128 * t : 128 * t + 128] = total

        plain.partial_solve(own_sensor, their_sensor, emit)
        return 0

    lax.fori_loop(0, 2, frame, 0)


def peak_kernel(
    place, layer_class, lateral, vertical, sink, own, layers_in, message, heat,
    out, v, cond, planes,
):
    clear_pads(v)

    def frame(d, _):
        solver = Solver(place, (layer_class, None, lateral, vertical, sink), d, v, cond)

        def bond_tile(k, rows, t):
            if t < 2:
                theirs = message[pl.ds(pl.multiple_of(80 * (4 + t) + 8 * k, 8), 8), :]
            else:
                theirs = partner_ring(message, 2, pl.ds(pl.multiple_of(480 + 8 * k, 8), 8))
            return jnp.where(d == 0, own[2, t, rows, :], theirs)

        solver.prepare(bond_tile)
        place_other(planes, layers_in, message, 1, d)

        def own_peak(l, t, rows, shared):
            return own[11 + 4 * d + l, t, rows, :] * heat[d, l, t, rows, :]

        def their_peak(l, t, rows, shared):
            return planes[l - 1, t, rows, :] * heat[d, 3 + l, t, rows, :]

        def emit(l, t, k, rows, total):
            at = pl.ds(pl.multiple_of(8 * k - 8, 8), 8)
            out[d, l, at, 128 * t : 128 * t + 128] = total

        solver.partial_solve(own_peak, their_peak, emit)
        return 0

    lax.fori_loop(0, 2, frame, 0)


def call(kernel, tables, arrays, outs, scratch=(), flops=0, name=None):
    shapes = [jax.ShapeDtypeStruct(shape, F32) for shape in outs]
    return pl.pallas_call(
        kernel,
        out_shape=shapes,
        in_specs=[SMEM] * len(tables) + [VMEM] * len(arrays),
        out_specs=[VMEM] * len(shapes),
        scratch_shapes=[pltpu.VMEM(shape, F32) for shape in scratch],
        compiler_params=pltpu.CompilerParams(vmem_limit_bytes=48 << 20),
        cost_estimate=pl.CostEstimate(flops=flops, bytes_accessed=4 << 20, transcendentals=0),
        name=name,
    )(*tables, *arrays)


def pairs(count, odd):
    if odd:
        return [(i, ((i - 1) ^ 1) + 1) for i in range(1, count - 1)]
    return [(i, i ^ 1) for i in range(count)]


def local(
    block_ids,
    block_power,
    layer_class,
    power_share,
    lateral_k,
    vertical_k,
    sink_conductance,
    bond_conductance,
    peak_factors,
    sensor_weight,
):
    nx, ny = lax.axis_size("gx"), lax.axis_size("gy")
    facing = [(i, nx - 1 - i) for i in range(nx)]
    place = jnp.stack([lax.axis_index("gx"), lax.axis_index("gy")]).astype(jnp.int32)
    layers = (2, 3, 2, 64, 128)

    (sensor_out,) = call(flip_layers_kernel, (), (sensor_weight,), [layers], name="flip_sensor")
    sensor_in = lax.ppermute(sensor_out, "gx", facing)

    power, col_a, col_b = call(
        column_kernel,
        (place, block_power),
        (block_ids, bond_conductance, sensor_weight, peak_factors),
        [(2, 2, 64, 128), (64, 128), (64, 128)],
        name="columns",
    )
    (peak_out,) = call(flip_layers_kernel, (), (peak_factors,), [layers], name="flip_peak")
    col_a = lax.ppermute(col_a, "gy", pairs(ny, False))
    col_b = lax.ppermute(col_b, "gy", pairs(ny, True))
    fields = (power, bond_conductance, sensor_weight, peak_factors)
    row_a, row_b = call(
        row_kernel, (place,), fields + (col_a, col_b), [(264, 128), (264, 128)], name="rows"
    )
    row_a = lax.ppermute(row_a, "gx", pairs(nx, False))
    row_b = lax.ppermute(row_b, "gx", pairs(nx, True))
    own, message = call(
        build_kernel,
        (place,),
        fields + (col_a, col_b, row_a, row_b),
        [(19, 3, ROWS, 128), (688, 128)],
        name="build",
    )
    message = lax.ppermute(message, "gx", facing)
    peak_in = lax.ppermute(peak_out, "gx", facing)
    planes = (3, 3, ROWS, 128)
    v = (2, 2, 4, 3, ROWS + 16, 128)
    thermal, sensed, heat = call(
        thermal_sensor_kernel,
        (place, layer_class, power_share, lateral_k, vertical_k, sink_conductance),
        (own, sensor_in, message),
        [(2, 4, 64, 256), (2, 4, 64, 256), (2, 7, 3, ROWS, 128)],
        [v, planes, (3, ROWS, 128), planes],
        name="thermal_sensor",
    )
    (peak,) = call(
        peak_kernel,
        (place, layer_class, lateral_k, vertical_k, sink_conductance),
        (own, peak_in, message, heat),
        [(2, 4, 64, 256)],
        [v, planes, planes],
        name="peak",
    )
    return thermal, peak, sensed


def solution(mesh):
    return jax.shard_map(
        local,
        mesh=mesh,
        in_specs=(
            P(None, "gx", "gy"),
            P(),
            P(),
            P(),
            P(),
            P(),
            P(),
            P("gx", "gy"),
            P(None, None, "gx", "gy"),
            P(None, None, "gx", "gy"),
        ),
        out_specs=(P(None, None, "gx", "gy"),) * 3,
        check_vma=False,
    )
```

```python
import functools

import jax
import jax.numpy as jnp
from jax import lax
from jax.experimental import pallas as pl
from jax.experimental.pallas import tpu as pltpu
from jax.sharding import PartitionSpec as P


BLOCKS = 32
ROWS = 80
DEEP = 6
NEAR = 3
F32 = jnp.float32

VMEM = pl.BlockSpec(memory_space=pltpu.VMEM)
SMEM = pl.BlockSpec(memory_space=pltpu.SMEM)

STRIP_H = [DEEP] * 3 + [NEAR] * 16
STRIP_AT = [sum(STRIP_H[:n]) for n in range(19)]
PART_H = [DEEP] * 3 + [2, 1] * 4
PART_AT = [2 * sum(PART_H[:n]) for n in range(11)]


def lanes():
    return lax.broadcasted_iota(jnp.int32, (8, 128), 1)


def sublanes():
    return lax.broadcasted_iota(jnp.int32, (8, 128), 0)


def rolled(x, shift, axis):
    size = x.shape[axis]
    shift %= size
    return x if shift == 0 else pltpu.roll(x, shift, axis)


def mirrored(x):
    return jnp.take_along_axis(x, 7 - sublanes(), axis=0)


def field_tile(refs, n, rows, t):
    power, bond, sensor, peak = refs
    if n < 2:
        return power[n, t, rows, :]
    cut = slice(128 * t, 128 * t + 128)
    if n == 2:
        return bond[rows, cut]
    field = sensor if n < 11 else peak
    m = (n - 3) % 8
    return field[m // 4, m % 4, rows, cut]


def ring_tile(from_right, from_left, n):
    h, at = STRIP_H[n], STRIP_AT[n]
    lane = lanes()
    return jnp.where(
        lane < h,
        rolled(from_right, -at, 1),
        jnp.where(lane >= 128 - h, rolled(from_left, 128 - h - at, 1), 0.0),
    )


def flip_layers_kernel(field, out):
    for d in range(2):
        for l in range(3):
            for t in range(2):
                for k in range(8):
                    out[d, l, t, 8 * (7 - k) : 8 * (8 - k), :] = mirrored(
                        field[d, l + 1, 8 * k : 8 * k + 8, 128 * t : 128 * t + 128]
                    )


def flip_own_kernel(own, out):
    for d in range(2):
        for l in range(3):
            for t in range(2):
                for k in range(8):
                    out[d, l, t, 8 * (7 - k) : 8 * (8 - k), :] = mirrored(
                        own[12 + 4 * d + l, t, 8 * k + 8 : 8 * k + 16, :]
                    )


def column_kernel(place, block_power, ids, bond, sensor, peak, power, to_a, to_b):
    values = [block_power[n] for n in range(BLOCKS)]

    def look_up(k, _):
        rows = pl.ds(pl.multiple_of(8 * k, 8), 8)
        for d in range(2):
            for t in range(2):
                index = ids[d, rows, 128 * t : 128 * t + 128]
                level = values
                bit = 1
                while len(level) > 1:
                    odd = (index & bit) != 0
                    level = [
                        jnp.where(odd, level[2 * n + 1], level[2 * n])
                        for n in range(len(level) // 2)
                    ]
                    bit *= 2
                power[d, t, rows, :] = level[0]
        return 0

    lax.fori_loop(0, 8, look_up, 0)
    even = (place[1] & 1) == 0
    refs = (power, bond, sensor, peak)

    def pack(k, _):
        rows = pl.ds(pl.multiple_of(8 * k, 8), 8)
        lane = lanes()
        right_edge = jnp.zeros((8, 128), F32)
        left_edge = jnp.zeros((8, 128), F32)
        for n in range(19):
            h, at = STRIP_H[n], STRIP_AT[n]
            here = (lane >= at) & (lane < at + h)
            left_edge = jnp.where(here, rolled(field_tile(refs, n, rows, 0), at, 1), left_edge)
            right_edge = jnp.where(
                here, rolled(field_tile(refs, n, rows, 1), at - (128 - h), 1), right_edge
            )
        to_a[rows, :] = jnp.where(even, right_edge, left_edge)
        to_b[rows, :] = jnp.where(even, left_edge, right_edge)
        return 0

    lax.fori_loop(0, 8, pack, 0)


def sides(place, axis, from_a, from_b, rows):
    even = (place[axis] & 1) == 0
    a, b = from_a[rows, :], from_b[rows, :]
    return jnp.where(even, a, b), jnp.where(even, b, a)


def row_kernel(place, power, bond, sensor, peak, col_a, col_b, to_a, to_b):
    even = (place[0] & 1) == 0
    refs = (power, bond, sensor, peak)
    row = sublanes()
    strips = []
    for first in (0, 56):
        rows = slice(first, first + 8)
        right, left = sides(place, 1, col_a, col_b, rows)

        def tile(n, t):
            return field_tile(refs, n, rows, t) if t < 2 else ring_tile(right, left, n)

        strip = []
        for t in range(3):
            for n in range(3):
                strip.append(tile(n, t))
            for m in range(8):
                x, y = tile(3 + 2 * m, t), tile(4 + 2 * m, t)
                if first == 0:
                    strip.append(jnp.where(row < 4, x, rolled(y, 4, 0)))
                else:
                    strip.append(jnp.where(row >= 4, x, rolled(y, -4, 0)))
        strips.append(strip)
    top, bottom = strips
    for n in range(33):
        rows = slice(8 * n, 8 * n + 8)
        to_a[rows, :] = jnp.where(even, bottom[n], top[n])
        to_b[rows, :] = jnp.where(even, top[n], bottom[n])


def build_kernel(place, power, bond, sensor, peak, col_a, col_b, row_a, row_b, own, message):
    refs = (power, bond, sensor, peak)

    def core(k, _):
        rows = pl.ds(pl.multiple_of(8 * k, 8), 8)
        to = pl.ds(pl.multiple_of(8 * k + 8, 8), 8)
        right, left = sides(place, 1, col_a, col_b, rows)
        for n in range(19):
            own[n, 0, to, :] = field_tile(refs, n, rows, 0)
            own[n, 1, to, :] = field_tile(refs, n, rows, 1)
            own[n, 2, to, :] = ring_tile(right, left, n)
        return 0

    lax.fori_loop(0, 8, core, 0)
    for t in range(3):
        for n in range(11):
            at = 8 * (11 * t + n)
            below, above = sides(place, 0, row_a, row_b, slice(at, at + 8))
            if n < 3:
                own[n, t, 0:8, :] = above
                own[n, t, 72:80, :] = below
            else:
                m = 3 + 2 * (n - 3)
                own[m, t, 0:8, :] = above
                own[m, t, 72:80, :] = below
                own[m + 1, t, 0:8, :] = rolled(above, 4, 0)
                own[m + 1, t, 72:80, :] = rolled(below, -4, 0)

    def pack(k, _):
        rows = pl.ds(pl.multiple_of(8 * k, 8), 8)
        back = 8 * (9 - k)
        lane = lanes()
        for n in range(3):
            for t in range(2):
                to = pl.ds(pl.multiple_of(80 * (2 * n + t) + back, 8), 8)
                message[to, :] = mirrored(own[n, t, rows, :])
        column = jnp.zeros((8, 128), F32)
        planes = [0, 1, 2]
        for field in range(2):
            for d in range(2):
                planes += [3 + 8 * field + 4 * d + 3, 3 + 8 * field + 4 * d + 2]
        for slot, n in enumerate(planes):
            h, at = PART_H[slot], PART_AT[slot]
            here = (lane >= at) & (lane < at + 2 * h)
            column = jnp.where(here, rolled(own[n, 2, rows, :], at + h, 1), column)
        message[pl.ds(pl.multiple_of(480 + back, 8), 8), :] = mirrored(column)
        return 0

    lax.fori_loop(0, 10, pack, 0)
    row = sublanes()
    for field in range(2):
        for d in range(2):
            n = 3 + 8 * field + 4 * d
            for t in range(2):
                above = jnp.where(
                    row >= 4, own[n + 3, t, 0:8, :], rolled(own[n + 2, t, 0:8, :], 4, 0)
                )
                below = jnp.where(
                    row < 4, own[n + 3, t, 72:80, :], rolled(own[n + 2, t, 72:80, :], 4, 0)
                )
                at = 560 + 16 * (4 * field + 2 * d + t)
                message[at : at + 8, :] = mirrored(below)
                message[at + 8 : at + 16, :] = mirrored(above)


def partner_ring(message, slot, rows):
    h, at = PART_H[slot], PART_AT[slot]
    lane = lanes()
    return jnp.where(
        (lane < h) | (lane >= 128 - h), rolled(message[rows, :], -(at + h), 1), 0.0
    )


class Solver:
    def __init__(self, place, tables, d, v, cond, v_scalars=None):
        self.place, self.d, self.v, self.cond = place, d, v, cond
        layer_class, share, lateral, vertical, sink = tables
        self.coef = []
        for side in range(2):
            die = d if side == 0 else 1 - d
            classes = [layer_class[die, l] for l in range(4)]
            coefs = []
            for l in range(4):
                g = lateral[classes[l]]
                up = vertical[classes[l]] if l < 3 else jnp.float32(0)
                down = vertical[classes[l - 1]] if l > 0 else jnp.float32(0)
                diagonal = 4 * g + up + down
                if l == 0:
                    diagonal = diagonal + sink[die]
                part = share[classes[l]] if share is not None else None
                if l < 3:
                    inverse = 1.0 / jnp.full((8, 128), diagonal, F32)
                    coefs.append(
                        (
                            inverse if part is None else inverse * part,
                            g * inverse,
                            up * inverse,
                            down * inverse,
                        )
                    )
                else:
                    coefs.append((diagonal, g, down, part))
            self.coef.append(coefs)

    def prepare(self, bond_tile):
        def body(k, _):
            rows = pl.ds(pl.multiple_of(8 * k, 8), 8)
            for t in range(3):
                bond = bond_tile(k, rows, t)
                self.cond[0, t, rows, :] = bond
                for side in range(2):
                    self.cond[1 + side, t, rows, :] = 1.0 / (self.coef[side][3][0] + bond)
            return 0

        lax.fori_loop(0, 10, body, 0)

    def masks(self, k):
        gx, gy = self.place[0], self.place[1]
        outside = ((k == 0) & (gx == 0)) | ((k == 9) & (gx == 15))
        row = jnp.where(outside, 0.0, 1.0).astype(F32)
        lane = lanes()
        right = jnp.where(gy == 15, 0.0, 1.0).astype(F32)
        left = jnp.where(gy == 0, 0.0, 1.0).astype(F32)
        ring = jnp.where(lane < 64, right, left)
        return row, row * ring

    def first(self, side, layers, source):
        def body(k, _):
            rows = pl.ds(pl.multiple_of(8 * k, 8), 8)
            to = pl.ds(pl.multiple_of(8 * k + 8, 8), 8)
            row, ring = self.masks(k)
            for t in range(3):
                mask = ring if t == 2 else row
                shared = {}
                for l in layers:
                    s = source(l, t, rows, shared)
                    coef = self.coef[side][l]
                    if l < 3:
                        s = s * coef[0]
                    else:
                        if coef[3] is not None:
                            s = s * coef[3]
                        s = s * self.cond[1 + side, t, rows, :]
                    self.v[0, side, l, t, to, :] = s * mask
            return 0

        lax.fori_loop(0, 10, body, 0)

    def sweep(self, b, work, core_only=False, unroll=2):
        v = self.v

        def one(k, stores):
            rows = pl.ds(pl.multiple_of(8 * k, 8), 8)
            to = pl.ds(pl.multiple_of(8 * k + 8, 8), 8)
            row, ring = self.masks(k)
            lane = lanes()
            first_lane, last_lane = lane == 0, lane == 127
            for side, layers, source, emit in work:
                shared = {}
                for l in layers:
                    coef = self.coef[side][l]
                    centre = [v[b, side, l, t, to, :] for t in range(3)]
                    forward = [pltpu.roll(c, 1, 1) for c in centre]
                    backward = [pltpu.roll(c, 127, 1) for c in centre]
                    for t in range(2 if core_only else 3):
                        left = jnp.where(first_lane, forward[t - 1], forward[t])
                        right = jnp.where(last_lane, backward[(t + 1) % 3], backward[t])
                        lateral = (left + right) + (
                            v[b, side, l, t, pl.ds(8 * k + 7, 8), :]
                            + v[b, side, l, t, pl.ds(8 * k + 9, 8), :]
                        )
                        s = source(l, t, rows, shared)
                        if l < 3:
                            total = s * coef[0] + coef[1] * lateral
                            total = total + coef[2] * v[b, side, l + 1, t, to, :]
                            if l > 0:
                                total = total + coef[3] * v[b, side, l - 1, t, to, :]
                        else:
                            if coef[3] is not None:
                                s = s * coef[3]
                            total = s + coef[1] * lateral
                            total = total + coef[2] * v[b, side, 2, t, to, :]
                            total = total + self.cond[0, t, rows, :] * v[b, 1 - side, 3, t, to, :]
                            total = total * self.cond[1 + side, t, rows, :]
                        if not core_only:
                            total = total * (ring if t == 2 else row)
                        stores.append((emit, side, l, t, k, rows, to, total))

        def body(j, _):
            stores = []
            for u in range(unroll):
                one(j * unroll + u + (1 if core_only else 0), stores)
            for emit, side, l, t, k, rows, to, total in stores:
                if emit is None:
                    v[1 - b, side, l, t, to, :] = total
                else:
                    emit(l, t, k, rows, total)
            return 0

        lax.fori_loop(0, (8 if core_only else 10) // unroll, body, 0)

    def partial_solve(self, own_source, other_source, emit):
        self.first(0, (0, 1, 2, 3), own_source)
        self.first(1, (1, 2, 3), other_source)
        every = (0, 1, 2, 3)
        self.sweep(0, [(0, every, own_source, None), (1, (2, 3), other_source, None)])
        self.sweep(1, [(0, every, own_source, None), (1, (3,), other_source, None)])
        self.sweep(0, [(0, every, own_source, emit)], core_only=True)


def clear_pads(v):
    zero = jnp.zeros((8, 128), F32)
    for b in range(2):
        for side in range(2):
            for l in range(4):
                for t in range(3):
                    v[b, side, l, t, 0:8, :] = zero
                    v[b, side, l, t, 88:96, :] = zero


def place_other(planes, layers_in, message, field, d):
    other = 1 - d
    zero = jnp.zeros((8, 128), F32)

    def body(k, _):
        rows = pl.ds(pl.multiple_of(8 * k, 8), 8)
        to = pl.ds(pl.multiple_of(8 * k + 8, 8), 8)
        for l in range(3):
            for t in range(2):
                planes[l, t, to, :] = layers_in[other, l, t, rows, :]
        return 0

    lax.fori_loop(0, 8, body, 0)

    def ring(k, _):
        rows = pl.ds(pl.multiple_of(8 * k, 8), 8)
        column = message[pl.ds(pl.multiple_of(480 + 8 * k, 8), 8), :]
        lane = lanes()
        planes[0, 2, rows, :] = zero
        for slot_in, l, h in ((0, 2, 2), (1, 1, 1)):
            ats = [PART_AT[3 + 4 * field + 2 * die + slot_in] + h for die in range(2)]
            picked = jnp.where(other == 0, rolled(column, -ats[0], 1), rolled(column, -ats[1], 1))
            planes[l, 2, rows, :] = jnp.where((lane < h) | (lane >= 128 - h), picked, 0.0)
        return 0

    lax.fori_loop(0, 10, ring, 0)
    for t in range(2):
        planes[0, t, 0:8, :] = zero
        planes[0, t, 72:80, :] = zero
        at = 560 + 64 * field + 32 * other + 16 * t
        above = message[pl.ds(pl.multiple_of(at, 8), 8), :]
        below = message[pl.ds(pl.multiple_of(at + 8, 8), 8), :]
        planes[2, t, 0:8, :] = above
        planes[2, t, 72:80, :] = below
        planes[1, t, 0:8, :] = rolled(above, 4, 0)
        planes[1, t, 72:80, :] = rolled(below, -4, 0)


def thermal_sensor_kernel(
    place, layer_class, share, lateral, vertical, sink, own, layers_in, message,
    thermal, sensed, heat, v, cond, power, planes,
):
    clear_pads(v)

    def frame(d, _):
        solver = Solver(place, (layer_class, share, lateral, vertical, sink), d, v, cond)

        def bond_tile(k, rows, t):
            if t < 2:
                theirs = message[pl.ds(pl.multiple_of(80 * (4 + t) + 8 * k, 8), 8), :]
            else:
                theirs = partner_ring(message, 2, pl.ds(pl.multiple_of(480 + 8 * k, 8), 8))
            return jnp.where(d == 0, own[2, t, rows, :], theirs)

        solver.prepare(bond_tile)

        def other_power(k, _):
            rows = pl.ds(pl.multiple_of(8 * k, 8), 8)
            column = message[pl.ds(pl.multiple_of(480 + 8 * k, 8), 8), :]
            lane = lanes()
            for t in range(2):
                at = 160 * (1 - d) + 80 * t + 8 * k
                power[t, rows, :] = message[pl.ds(pl.multiple_of(at, 8), 8), :]
            picked = jnp.where(
                d == 1,
                rolled(column, -(PART_AT[0] + DEEP), 1),
                rolled(column, -(PART_AT[1] + DEEP), 1),
            )
            power[2, rows, :] = jnp.where((lane < DEEP) | (lane >= 128 - DEEP), picked, 0.0)
            return 0

        lax.fori_loop(0, 10, other_power, 0)

        def own_power(l, t, rows, shared):
            if t not in shared:
                shared[t] = own[d, t, rows, :]
            return shared[t]

        def their_power(l, t, rows, shared):
            if t not in shared:
                shared[t] = power[t, rows, :]
            return shared[t]

        every = (0, 1, 2, 3)
        solver.first(0, every, own_power)
        solver.first(1, every, their_power)
        for b in (0, 1):
            solver.sweep(b, [(0, every, own_power, None), (1, every, their_power, None)])

        def emit_own(l, t, k, rows, total):
            heat[d, l, t, rows, :] = total

        def emit_other(l, t, k, rows, total):
            heat[d, 3 + l, t, rows, :] = total

        solver.sweep(0, [(0, every, own_power, emit_own), (1, (1, 2, 3), their_power, emit_other)])

        def write(k, _):
            rows = pl.ds(pl.multiple_of(8 * k, 8), 8)
            at = pl.ds(pl.multiple_of(8 * k + 8, 8), 8)
            for l in range(4):
                for t in range(2):
                    thermal[d, l, rows, 128 * t : 128 * t + 128] = heat[d, l, t, at, :]
            return 0

        lax.fori_loop(0, 8, write, 0)

        place_other(planes, layers_in, message, 0, d)
        plain = Solver(place, (layer_class, None, lateral, vertical, sink), d, v, cond)

        def own_sensor(l, t, rows, shared):
            return own[3 + 4 * d + l, t, rows, :]

        def their_sensor(l, t, rows, shared):
            return planes[l - 1, t, rows, :]

        def emit(l, t, k, rows, total):
            at = pl.ds(pl.multiple_of(8 * k - 8, 8), 8)
            sensed[d, l, at, 128 * t : 128 * t + 128] = total

        plain.partial_solve(own_sensor, their_sensor, emit)
        return 0

    lax.fori_loop(0, 2, frame, 0)


def peak_kernel(
    place, layer_class, lateral, vertical, sink, own, layers_in, message, heat,
    out, v, cond, planes,
):
    clear_pads(v)

    def frame(d, _):
        solver = Solver(place, (layer_class, None, lateral, vertical, sink), d, v, cond)

        def bond_tile(k, rows, t):
            if t < 2:
                theirs = message[pl.ds(pl.multiple_of(80 * (4 + t) + 8 * k, 8), 8), :]
            else:
                theirs = partner_ring(message, 2, pl.ds(pl.multiple_of(480 + 8 * k, 8), 8))
            return jnp.where(d == 0, own[2, t, rows, :], theirs)

        solver.prepare(bond_tile)
        place_other(planes, layers_in, message, 1, d)

        def own_peak(l, t, rows, shared):
            return own[11 + 4 * d + l, t, rows, :] * heat[d, l, t, rows, :]

        def their_peak(l, t, rows, shared):
            return planes[l - 1, t, rows, :] * heat[d, 3 + l, t, rows, :]

        def emit(l, t, k, rows, total):
            at = pl.ds(pl.multiple_of(8 * k - 8, 8), 8)
            out[d, l, at, 128 * t : 128 * t + 128] = total

        solver.partial_solve(own_peak, their_peak, emit)
        return 0

    lax.fori_loop(0, 2, frame, 0)


def call(kernel, tables, arrays, outs, scratch=(), flops=0, cost=1024, name=None):
    shapes = [jax.ShapeDtypeStruct(shape, F32) for shape in outs]
    return pl.pallas_call(
        kernel,
        out_shape=shapes,
        in_specs=[SMEM] * len(tables) + [VMEM] * len(arrays),
        out_specs=[VMEM] * len(shapes),
        scratch_shapes=[pltpu.VMEM(shape, F32) for shape in scratch],
        compiler_params=pltpu.CompilerParams(vmem_limit_bytes=16 << 20),
        cost_estimate=pl.CostEstimate(flops=flops, bytes_accessed=cost, transcendentals=0),
        name=name,
    )(*tables, *arrays)


def pairs(count, odd):
    if odd:
        return [(i, ((i - 1) ^ 1) + 1) for i in range(1, count - 1)]
    return [(i, i ^ 1) for i in range(count)]


def local(
    block_ids,
    block_power,
    layer_class,
    power_share,
    lateral_k,
    vertical_k,
    sink_conductance,
    bond_conductance,
    peak_factors,
    sensor_weight,
):
    nx, ny = lax.axis_size("gx"), lax.axis_size("gy")
    facing = [(i, nx - 1 - i) for i in range(nx)]
    place = jnp.stack([lax.axis_index("gx"), lax.axis_index("gy")]).astype(jnp.int32)
    layers = (2, 3, 2, 64, 128)

    (sensor_out,) = call(flip_layers_kernel, (), (sensor_weight,), [layers], name="flip_sensor")
    sensor_in = lax.ppermute(sensor_out, "gx", facing)

    power, col_a, col_b = call(
        column_kernel,
        (place, block_power),
        (block_ids, bond_conductance, sensor_weight, peak_factors),
        [(2, 2, 64, 128), (64, 128), (64, 128)],
        name="columns",
    )
    col_a = lax.ppermute(col_a, "gy", pairs(ny, False))
    col_b = lax.ppermute(col_b, "gy", pairs(ny, True))
    fields = (power, bond_conductance, sensor_weight, peak_factors)
    row_a, row_b = call(
        row_kernel, (place,), fields + (col_a, col_b), [(264, 128), (264, 128)], name="rows"
    )
    row_a = lax.ppermute(row_a, "gx", pairs(nx, False))
    row_b = lax.ppermute(row_b, "gx", pairs(nx, True))
    row_a, row_b, sensor_in = lax.optimization_barrier((row_a, row_b, sensor_in))
    own, message = call(
        build_kernel,
        (place,),
        fields + (col_a, col_b, row_a, row_b),
        [(19, 3, ROWS, 128), (688, 128)],
        name="build",
    )
    message = lax.ppermute(message, "gx", facing)
    (peak_out,) = call(flip_own_kernel, (), (own,), [layers], flops=10**11, cost=64 << 20, name="flip_peak")
    peak_in = lax.ppermute(peak_out, "gx", facing)
    planes = (3, 3, ROWS, 128)
    v = (2, 2, 4, 3, ROWS + 16, 128)
    thermal, sensed, heat = call(
        thermal_sensor_kernel,
        (place, layer_class, power_share, lateral_k, vertical_k, sink_conductance),
        (own, sensor_in, message),
        [(2, 4, 64, 256), (2, 4, 64, 256), (2, 7, 3, ROWS, 128)],
        [v, planes, (3, ROWS, 128), planes],
        cost=64 << 20, flops=10**11,
        name="thermal_sensor",
    )
    (peak,) = call(
        peak_kernel,
        (place, layer_class, lateral_k, vertical_k, sink_conductance),
        (own, peak_in, message, heat),
        [(2, 4, 64, 256)],
        [v, planes, planes],
        name="peak",
    )
    return thermal, peak, sensed


def solution(mesh):
    return jax.shard_map(
        local,
        mesh=mesh,
        in_specs=(
            P(None, "gx", "gy"),
            P(),
            P(),
            P(),
            P(),
            P(),
            P(),
            P("gx", "gy"),
            P(None, None, "gx", "gy"),
            P(None, None, "gx", "gy"),
        ),
        out_specs=(P(None, None, "gx", "gy"),) * 3,
        check_vma=False,
    )
```

```python
import jax
import jax.numpy as jnp
from jax import lax
from jax.experimental import pallas as pl
from jax.experimental.pallas import tpu as pltpu
from jax.sharding import PartitionSpec as P


BLOCKS = 32
ROWS = 80
DEEP = 6
NEAR = 3
F32 = jnp.float32

VMEM = pl.BlockSpec(memory_space=pltpu.VMEM)
SMEM = pl.BlockSpec(memory_space=pltpu.SMEM)

STRIP_H = [DEEP] * 3 + [NEAR] * 16
STRIP_AT = [sum(STRIP_H[:n]) for n in range(19)]
PART_H = [DEEP] * 3 + [2, 1] * 4
PART_AT = [2 * sum(PART_H[:n]) for n in range(11)]


def lanes():
    return lax.broadcasted_iota(jnp.int32, (8, 128), 1)


def sublanes():
    return lax.broadcasted_iota(jnp.int32, (8, 128), 0)


def rolled(x, shift, axis):
    size = x.shape[axis]
    shift %= size
    return x if shift == 0 else pltpu.roll(x, shift, axis)


def mirrored(x):
    return jnp.take_along_axis(x, 7 - sublanes(), axis=0)


def ring_tile(from_right, from_left, n):
    h, at = STRIP_H[n], STRIP_AT[n]
    lane = lanes()
    return jnp.where(
        lane < h,
        rolled(from_right, -at, 1),
        jnp.where(lane >= 128 - h, rolled(from_left, 128 - h - at, 1), 0.0),
    )


def gather_kernel(
    place, block_power, ids, bond, sensor, peak, own, first_out, to_a, to_b, table, blocks, sems
):
    copies = [
        pltpu.make_async_copy(block_power, table, sems.at[0]),
        pltpu.make_async_copy(ids, blocks, sems.at[1]),
    ]
    for n in range(2, 19):
        for t in range(2):
            cut = pl.ds(128 * t, 128)
            if n == 2:
                source = bond.at[:, cut]
            else:
                field, m = (sensor, n - 3) if n < 11 else (peak, n - 11)
                source = field.at[m // 4, m % 4, :, cut]
            copies.append(
                pltpu.make_async_copy(source, own.at[n, t, pl.ds(8, 64), :], sems.at[len(copies)])
            )
    for copy in copies:
        copy.start()
    copies[0].wait()
    copies[1].wait()
    values = [table[n] for n in range(BLOCKS)]

    def look_up(k):
        stores = []
        for d in range(2):
            for t in range(2):
                index = blocks[d, tile_rows(k), 128 * t : 128 * t + 128]
                level = values
                bit = 1
                while len(level) > 1:
                    odd = (index & bit) != 0
                    level = [
                        jnp.where(odd, level[2 * n + 1], level[2 * n])
                        for n in range(len(level) // 2)
                    ]
                    bit *= 2
                stores.append((own, (d, t, tile_rows(k, 8)), level[0]))
                stores.append((first_out, (6 + d, t, tile_rows(7 - k)), mirrored(level[0])))
        return stores

    tile_loop(0, 8, 1, look_up)
    for copy in copies[2:]:
        copy.wait()
    even = (place[1] & 1) == 0

    def pack(k):
        lane = lanes()
        stores = []
        right_edge = jnp.zeros((8, 128), F32)
        left_edge = jnp.zeros((8, 128), F32)
        for n in range(19):
            h, at = STRIP_H[n], STRIP_AT[n]
            here = (lane >= at) & (lane < at + h)
            tiles = [own[n, t, tile_rows(k, 8), :] for t in range(2)]
            left_edge = jnp.where(here, rolled(tiles[0], at, 1), left_edge)
            right_edge = jnp.where(here, rolled(tiles[1], at - (128 - h), 1), right_edge)
            slot = 8 if n == 2 else 3 * ((n - 3) // 4) + (n - 3) % 4 - 1
            if n == 2 or (3 <= n < 11 and (n - 3) % 4 > 0):
                for t in range(2):
                    stores.append((first_out, (slot, t, tile_rows(7 - k)), mirrored(tiles[t])))
        stores.append((to_a, (tile_rows(k),), jnp.where(even, right_edge, left_edge)))
        stores.append((to_b, (tile_rows(k),), jnp.where(even, left_edge, right_edge)))
        return stores

    tile_loop(0, 8, 2, pack)


def sides(place, axis, from_a, from_b, rows):
    even = (place[axis] & 1) == 0
    a, b = from_a[rows, :], from_b[rows, :]
    return jnp.where(even, a, b), jnp.where(even, b, a)


def row_kernel(place, own, col_a, col_b, to_a, to_b, peak_out):
    even = (place[0] & 1) == 0
    row = sublanes()
    strips = []
    for first in (0, 56):
        rows = slice(first, first + 8)
        right, left = sides(place, 1, col_a, col_b, rows)

        def tile(n, t):
            if t < 2:
                return own[n, t, first + 8 : first + 16, :]
            return ring_tile(right, left, n)

        strip = []
        for t in range(3):
            for n in range(3):
                strip.append(tile(n, t))
            for m in range(8):
                x, y = tile(3 + 2 * m, t), tile(4 + 2 * m, t)
                if first == 0:
                    strip.append(jnp.where(row < 4, x, rolled(y, 4, 0)))
                else:
                    strip.append(jnp.where(row >= 4, x, rolled(y, -4, 0)))
        strips.append(strip)
    top, bottom = strips
    for n in range(33):
        rows = slice(8 * n, 8 * n + 8)
        to_a[rows, :] = jnp.where(even, bottom[n], top[n])
        to_b[rows, :] = jnp.where(even, top[n], bottom[n])

    def flip(k):
        return [
            (peak_out, (3 * d + l, t, tile_rows(7 - k)), mirrored(own[12 + 4 * d + l, t, tile_rows(k, 8), :]))
            for d in range(2)
            for l in range(3)
            for t in range(2)
        ]

    tile_loop(0, 8, 2, flip)


def build_kernel(place, start, col_a, col_b, row_a, row_b, own, message):
    def core(k):
        right, left = sides(place, 1, col_a, col_b, tile_rows(k))
        return [(own, (n, 2, tile_rows(k, 8)), ring_tile(right, left, n)) for n in range(19)]

    tile_loop(0, 8, 2, core)
    for t in range(3):
        for n in range(11):
            at = 8 * (11 * t + n)
            below, above = sides(place, 0, row_a, row_b, slice(at, at + 8))
            if n < 3:
                own[n, t, 0:8, :] = above
                own[n, t, 72:80, :] = below
            else:
                m = 3 + 2 * (n - 3)
                own[m, t, 0:8, :] = above
                own[m, t, 72:80, :] = below
                own[m + 1, t, 0:8, :] = rolled(above, 4, 0)
                own[m + 1, t, 72:80, :] = rolled(below, -4, 0)

    planes = [0, 1, 2]
    for field in range(2):
        for d in range(2):
            planes += [3 + 8 * field + 4 * d + 3, 3 + 8 * field + 4 * d + 2]

    def pack(k):
        lane = lanes()
        column = jnp.zeros((8, 128), F32)
        for slot, n in enumerate(planes):
            h, at = PART_H[slot], PART_AT[slot]
            here = (lane >= at) & (lane < at + 2 * h)
            column = jnp.where(here, rolled(own[n, 2, tile_rows(k), :], at + h, 1), column)
        return [(message, (tile_rows(9 - k),), mirrored(column))]

    tile_loop(0, 10, 5, pack)
    row = sublanes()
    for n in range(3):
        for t in range(2):
            at = 80 + 16 * (2 * n + t)
            message[at : at + 8, :] = mirrored(own[n, t, 72:80, :])
            message[at + 8 : at + 16, :] = mirrored(own[n, t, 0:8, :])
    for field in range(2):
        for d in range(2):
            n = 3 + 8 * field + 4 * d
            for t in range(2):
                above = jnp.where(
                    row >= 4, own[n + 3, t, 0:8, :], rolled(own[n + 2, t, 0:8, :], 4, 0)
                )
                below = jnp.where(
                    row < 4, own[n + 3, t, 72:80, :], rolled(own[n + 2, t, 72:80, :], 4, 0)
                )
                at = 176 + 16 * (4 * field + 2 * d + t)
                message[at : at + 8, :] = mirrored(below)
                message[at + 8 : at + 16, :] = mirrored(above)


def partner_ring(message, slot, rows):
    h, at = PART_H[slot], PART_AT[slot]
    lane = lanes()
    return jnp.where(
        (lane < h) | (lane >= 128 - h), rolled(message[rows, :], -(at + h), 1), 0.0
    )


def tile_loop(start, stop, unroll, body):
    def step(j, _):
        stores = []
        for u in range(unroll):
            stores += body(start + unroll * j + u)
        for ref, index, value in stores:
            ref[index] = value
        return 0

    lax.fori_loop(0, (stop - start) // unroll, step, 0)


def tile_rows(k, add=0):
    return pl.ds(pl.multiple_of(8 * k + add, 8), 8)


class Solver:
    def __init__(self, place, tables, d, v, cond):
        self.place, self.d, self.v, self.cond = place, d, v, cond
        layer_class, share, lateral, vertical, sink = tables
        self.coef = []
        for side in range(2):
            die = d if side == 0 else 1 - d
            classes = [layer_class[die, l] for l in range(4)]
            coefs = []
            for l in range(4):
                g = lateral[classes[l]]
                up = vertical[classes[l]] if l < 3 else jnp.float32(0)
                down = vertical[classes[l - 1]] if l > 0 else jnp.float32(0)
                diagonal = 4 * g + up + down
                if l == 0:
                    diagonal = diagonal + sink[die]
                part = share[classes[l]] if share is not None else None
                if l < 3:
                    inverse = 1.0 / jnp.full((8, 128), diagonal, F32)
                    scale = inverse if part is None else inverse * part
                    coefs.append((scale, g * inverse, up * inverse, down * inverse))
                else:
                    coefs.append((diagonal, g, down, part))
            self.coef.append(coefs)
        gy = place[1]
        right = jnp.where(gy == 15, 0.0, 1.0).astype(F32)
        left = jnp.where(gy == 0, 0.0, 1.0).astype(F32)
        self.ring = jnp.where(lanes() < 64, right, left)

    def prepare(self, bond_tile):
        def body(k):
            stores = []
            for t in range(3):
                bond = bond_tile(k, t)
                stores.append((self.cond, (self.d, 0, t, tile_rows(k)), bond))
                for side in range(2):
                    value = 1.0 / (self.coef[side][3][0] + bond)
                    stores.append((self.cond, (self.d, 1 + side, t, tile_rows(k)), value))
            return stores

        tile_loop(0, 10, 5, body)

    def zero_outside(self, b, planes):
        zero = jnp.zeros((8, 128), F32)
        for here, first in ((self.place[0] == 0, 8), (self.place[0] == 15, 80)):

            @pl.when(here)
            def _():
                for side, l in planes:
                    for t in range(3):
                        self.v[side][self.d, b, l, t, first : first + 8, :] = zero

    def first(self, work, unroll=2):
        def body(k):
            stores = []
            for side, layers, source in work:
                for t in range(3):
                    shared = {}
                    for l in layers:
                        s = source(l, t, tile_rows(k), shared)
                        coef = self.coef[side][l]
                        if l < 3:
                            s = s * coef[0]
                        else:
                            if coef[3] is not None:
                                s = s * coef[3]
                            s = s * self.cond[self.d, 1 + side, t, tile_rows(k)]
                        if t == 2:
                            s = s * self.ring
                        stores.append((self.v[side], (self.d, 0, l, t, tile_rows(k, 8)), s))
            return stores

        tile_loop(0, 10, unroll, body)
        self.zero_outside(0, [(side, l) for side, layers, _ in work for l in layers])

    def sweep(self, b, work, core_only=False, unroll=2):
        v, d = self.v, self.d

        def body(k):
            stores = []
            rows, to = tile_rows(k), tile_rows(k, 8)
            lane = lanes()
            first_lane, last_lane = lane == 0, lane == 127
            seen = {}

            def value(side, l, t):
                if (side, l, t) not in seen:
                    seen[side, l, t] = v[side][d, b, l, t, to, :]
                return seen[side, l, t]

            for side, layers, source, emit in work:
                shared = {}
                for l in layers:
                    coef = self.coef[side][l]
                    forward = [pltpu.roll(value(side, l, t), 1, 1) for t in range(3)]
                    backward = [pltpu.roll(value(side, l, t), 127, 1) for t in range(3)]
                    for t in range(2 if core_only else 3):
                        left = jnp.where(first_lane, forward[t - 1], forward[t])
                        right = jnp.where(last_lane, backward[(t + 1) % 3], backward[t])
                        around = (left + right) + (
                            v[side][d, b, l, t, pl.ds(8 * k + 7, 8), :]
                            + v[side][d, b, l, t, pl.ds(8 * k + 9, 8), :]
                        )
                        s = source(l, t, rows, shared)
                        if l < 3:
                            total = s * coef[0] + coef[1] * around
                            total = total + coef[2] * value(side, l + 1, t)
                            if l > 0:
                                total = total + coef[3] * value(side, l - 1, t)
                        else:
                            if coef[3] is not None:
                                s = s * coef[3]
                            total = (s + coef[1] * around) + coef[2] * value(side, 2, t)
                            total = total + self.cond[d, 0, t, rows] * value(1 - side, 3, t)
                            total = total * self.cond[d, 1 + side, t, rows]
                        if t == 2:
                            total = total * self.ring
                        if emit is None:
                            stores.append((v[side], (d, 1 - b, l, t, to), total))
                        else:
                            stores += emit(l, t, k, total)
            return stores

        if core_only:
            tile_loop(1, 9, unroll, body)
        else:
            tile_loop(0, 10, unroll, body)
            kept = [(side, l) for side, layers, _, emit in work if emit is None for l in layers]
            self.zero_outside(1 - b, kept)

    def solve_own(self, own_source, other_source, emit):
        every = (0, 1, 2, 3)
        self.first([(0, every, own_source), (1, (1, 2, 3), other_source)])
        self.sweep(0, [(0, every, own_source, None), (1, (2, 3), other_source, None)])
        self.sweep(1, [(0, every, own_source, None), (1, (3,), other_source, None)])
        self.sweep(0, [(0, every, own_source, emit)], core_only=True)

    def solve_before(self, own_source, emit):
        self.first([(0, (0, 1, 2, 3), own_source)])
        self.sweep(0, [(0, (0, 1, 2), own_source, None)])
        self.sweep(1, [(0, (0, 1), own_source, None)])
        self.sweep(0, [(0, (0,), own_source, emit)], core_only=True, unroll=4)

    def solve_after(self, own_source, other_source, emit):
        self.first([(1, (1, 2, 3), other_source)])
        self.sweep(0, [(0, (3,), own_source, None), (1, (2, 3), other_source, None)])
        self.sweep(1, [(0, (2, 3), own_source, None), (1, (3,), other_source, None)])
        self.sweep(0, [(0, (1, 2, 3), own_source, emit)], core_only=True)


def clear_pads(v):
    zero = jnp.zeros((8, 128), F32)
    for d in range(2):
        for b in range(2):
            for l in range(4):
                for t in range(3):
                    v[d, b, l, t, 0:8, :] = zero
                    v[d, b, l, t, 88:96, :] = zero


def place_other(planes, layers_in, message, field, d):
    other = 1 - d
    zero = jnp.zeros((8, 128), F32)

    def body(k):
        return [
            (planes, (l, t, tile_rows(k, 8)), layers_in(3 * other + l, t, tile_rows(k)))
            for l in range(3)
            for t in range(2)
        ]

    tile_loop(0, 8, 4, body)

    def ring(k):
        column = message[tile_rows(k), :]
        lane = lanes()
        stores = [(planes, (0, 2, tile_rows(k)), zero)]
        for slot_in, l, h in ((0, 2, 2), (1, 1, 1)):
            ats = [PART_AT[3 + 4 * field + 2 * die + slot_in] + h for die in range(2)]
            picked = jnp.where(other == 0, rolled(column, -ats[0], 1), rolled(column, -ats[1], 1))
            inside = (lane < h) | (lane >= 128 - h)
            stores.append((planes, (l, 2, tile_rows(k)), jnp.where(inside, picked, 0.0)))
        return stores

    tile_loop(0, 10, 5, ring)
    for t in range(2):
        planes[0, t, 0:8, :] = zero
        planes[0, t, 72:80, :] = zero
        at = 176 + 64 * field + 32 * other + 16 * t
        above = message[pl.ds(pl.multiple_of(at, 8), 8), :]
        below = message[pl.ds(pl.multiple_of(at + 8, 8), 8), :]
        planes[2, t, 0:8, :] = above
        planes[2, t, 72:80, :] = below
        planes[1, t, 0:8, :] = rolled(above, 4, 0)
        planes[1, t, 72:80, :] = rolled(below, -4, 0)


def place_deep(planes, first_in, message):
    def body(k):
        return [
            (planes, (n, t, tile_rows(k, 8)), first_in[6 + n, t, tile_rows(k), :])
            for n in range(3)
            for t in range(2)
        ]

    tile_loop(0, 8, 4, body)

    def ring(k):
        return [
            (planes, (n, 2, tile_rows(k)), partner_ring(message, n, tile_rows(k)))
            for n in range(3)
        ]

    tile_loop(0, 10, 5, ring)
    for n in range(3):
        for t in range(2):
            at = 80 + 16 * (2 * n + t)
            planes[n, t, 0:8, :] = message[at : at + 8, :]
            planes[n, t, 72:80, :] = message[at + 8 : at + 16, :]


def thermal_sensor_kernel(
    place, layer_class, share, lateral, vertical, sink, own, first_in, message,
    thermal, sensed, heat, weighted, early, cond, v_peak, v_own, v_other, planes, deep,
):
    for v in (v_own, v_other, v_peak):
        clear_pads(v)
    place_deep(deep, first_in, message)

    def frame(d, _):
        v = (v_own, v_other)
        solver = Solver(place, (layer_class, share, lateral, vertical, sink), d, v, cond)
        solver.prepare(
            lambda k, t: jnp.where(d == 0, own[2, t, tile_rows(k), :], deep[2, t, tile_rows(k), :])
        )

        def own_power(l, t, rows, shared):
            if t not in shared:
                shared[t] = own[d, t, rows, :]
            return shared[t]

        def their_power(l, t, rows, shared):
            if t not in shared:
                shared[t] = deep[1 - d, t, rows, :]
            return shared[t]

        every = (0, 1, 2, 3)
        solver.first([(0, every, own_power), (1, every, their_power)])
        for b in (0, 1):
            solver.sweep(b, [(0, every, own_power, None), (1, every, their_power, None)])

        def emit_own(l, t, k, total):
            peak = own[11 + 4 * d + l, t, tile_rows(k), :]
            stores = [(weighted, (d, l, t, tile_rows(k)), total * peak)]
            if t < 2:
                stores.append((v_own, (d, 1, l, t, tile_rows(k, 8)), total))
            return stores

        def emit_other(l, t, k, total):
            return [(heat, (d, l - 1, t, tile_rows(k)), total)]

        solver.sweep(
            0, [(0, every, own_power, emit_own), (1, (1, 2, 3), their_power, emit_other)]
        )

        def write(k):
            return [
                (
                    thermal,
                    (d, l, tile_rows(k), slice(128 * t, 128 * t + 128)),
                    v_own[d, 1, l, t, tile_rows(k, 16), :],
                )
                for l in range(4)
                for t in range(2)
            ]

        tile_loop(0, 8, 4, write)

        plain = (layer_class, None, lateral, vertical, sink)

        def layers_in(n, t, rows):
            return first_in[n, t, rows, :]

        place_other(planes, layers_in, message, 0, d)

        def own_sensor(l, t, rows, shared):
            return own[3 + 4 * d + l, t, rows, :]

        def their_sensor(l, t, rows, shared):
            return planes[l - 1, t, rows, :]

        def emit(l, t, k, total):
            return [(sensed, (d, l, tile_rows(k, -8), slice(128 * t, 128 * t + 128)), total)]

        Solver(place, plain, d, v, cond).solve_own(own_sensor, their_sensor, emit)

        def own_peak(l, t, rows, shared):
            return weighted[d, l, t, rows, :]

        def emit_early(l, t, k, total):
            return [(early, (d, t, tile_rows(k, -8)), total)]

        Solver(place, plain, d, (v_peak, None), cond).solve_before(own_peak, emit_early)
        return 0

    lax.fori_loop(0, 2, frame, 0)


def peak_kernel(
    place, layer_class, lateral, vertical, sink, layers_in, message, heat, weighted, early, cond,
    v_start, out, v_peak, v_other, planes,
):
    clear_pads(v_other)

    def frame(d, _):
        plain = (layer_class, None, lateral, vertical, sink)
        solver = Solver(place, plain, d, (v_peak, v_other), cond)

        def layers(n, t, rows):
            return layers_in[n, t, rows, :]

        place_other(planes, layers, message, 1, d)

        def own_peak(l, t, rows, shared):
            return weighted[d, l, t, rows, :]

        def their_peak(l, t, rows, shared):
            return planes[l - 1, t, rows, :] * heat[d, l - 1, t, rows, :]

        def emit(l, t, k, total):
            return [(out, (d, l, tile_rows(k, -8), slice(128 * t, 128 * t + 128)), total)]

        solver.solve_after(own_peak, their_peak, emit)

        def write(k):
            return [
                (
                    out,
                    (d, 0, tile_rows(k), slice(128 * t, 128 * t + 128)),
                    early[d, t, tile_rows(k), :],
                )
                for t in range(2)
            ]

        tile_loop(0, 8, 8, write)
        return 0

    lax.fori_loop(0, 2, frame, 0)


PLANES = (19, 3, ROWS, 128)
FIELD = (2, 4, 64, 256)
V = (2, 2, 4, 3, ROWS + 16, 128)
OTHER = (3, 3, ROWS, 128)
KEPT = [
    (2, 3, 3, ROWS, 128),
    (2, 4, 3, ROWS, 128),
    (2, 2, 64, 128),
    (2, 3, 3, ROWS, 128),
    V,
]


def call(kernel, tables, arrays, outs, scratch=(), flops=0, aliases={}, hbm=0, name=None):
    shapes = [jax.ShapeDtypeStruct(shape, F32) for shape in outs]
    arrays = [
        pltpu.with_memory_space_constraint(x, pltpu.HBM) if i < hbm else x
        for i, x in enumerate(arrays)
    ]
    anywhere = pl.BlockSpec(memory_space=pltpu.HBM)
    return pl.pallas_call(
        kernel,
        out_shape=shapes,
        in_specs=[SMEM] * len(tables) + [anywhere] * hbm + [VMEM] * (len(arrays) - hbm),
        out_specs=[VMEM] * len(shapes),
        scratch_shapes=[pltpu.VMEM(x, F32) if isinstance(x, tuple) else x for x in scratch],
        input_output_aliases={len(tables) + i: o for i, o in aliases.items()},
        compiler_params=pltpu.CompilerParams(vmem_limit_bytes=16 << 20),
        cost_estimate=pl.CostEstimate(flops=flops, bytes_accessed=1024, transcendentals=0),
        name=name,
    )(*tables, *arrays)


def pairs(count, odd):
    if odd:
        return [(i, ((i - 1) ^ 1) + 1) for i in range(1, count - 1)]
    return [(i, i ^ 1) for i in range(count)]


def local(
    block_ids,
    block_power,
    layer_class,
    power_share,
    lateral_k,
    vertical_k,
    sink_conductance,
    bond_conductance,
    peak_factors,
    sensor_weight,
):
    nx, ny = lax.axis_size("gx"), lax.axis_size("gy")
    facing = [(i, nx - 1 - i) for i in range(nx)]
    place = jnp.stack([lax.axis_index("gx"), lax.axis_index("gy")]).astype(jnp.int32)
    own, first_out, col_a, col_b = call(
        gather_kernel,
        (place,),
        (block_power, block_ids, bond_conductance, sensor_weight, peak_factors),
        [PLANES, (9, 2, 64, 128), (64, 128), (64, 128)],
        [
            pltpu.SMEM((BLOCKS,), F32),
            pltpu.VMEM((2, 64, 256), jnp.int32),
            pltpu.SemaphoreType.DMA((36,)),
        ],
        hbm=5,
        name="gather",
    )
    first_in = lax.ppermute(first_out, "gx", facing)
    col_a = lax.ppermute(col_a, "gy", pairs(ny, False))
    col_b = lax.ppermute(col_b, "gy", pairs(ny, True))
    row_a, row_b, peak_out = call(
        row_kernel,
        (place,),
        (own, col_a, col_b),
        [(264, 128), (264, 128), (6, 2, 64, 128)],
        name="rows",
    )
    row_a = lax.ppermute(row_a, "gx", pairs(nx, False))
    row_b = lax.ppermute(row_b, "gx", pairs(nx, True))
    peak_in = lax.ppermute(peak_out, "gx", facing)
    own, message = call(
        build_kernel,
        (place,),
        (own, col_a, col_b, row_a, row_b),
        [PLANES, (304, 128)],
        aliases={0: 0},
        name="build",
    )
    message = lax.ppermute(message, "gx", facing)
    state = call(
        thermal_sensor_kernel,
        (place, layer_class, power_share, lateral_k, vertical_k, sink_conductance),
        (own, first_in, message),
        [FIELD, FIELD] + KEPT,
        [V, V, OTHER, OTHER],
        flops=10**11,
        name="thermal_sensor",
    )
    thermal, sensed, *kept = state
    peak, _ = call(
        peak_kernel,
        (place, layer_class, lateral_k, vertical_k, sink_conductance),
        (peak_in, message, *kept),
        [FIELD, V],
        [V, OTHER],
        aliases={6: 1},
        name="peak",
    )
    return thermal, peak, sensed


def solution(mesh):
    return jax.shard_map(
        local,
        mesh=mesh,
        in_specs=(
            P(None, "gx", "gy"),
            P(),
            P(),
            P(),
            P(),
            P(),
            P(),
            P("gx", "gy"),
            P(None, None, "gx", "gy"),
            P(None, None, "gx", "gy"),
        ),
        out_specs=(P(None, None, "gx", "gy"),) * 3,
        check_vma=False,
    )
```

```python
import jax
import jax.numpy as jnp
from jax import lax
from jax.experimental import pallas as pl
from jax.experimental.pallas import tpu as pltpu
from jax.sharding import PartitionSpec as P


BLOCKS = 32
ROWS = 80
DEEP = 6
NEAR = 3
F32 = jnp.float32

VMEM = pl.BlockSpec(memory_space=pltpu.VMEM)
SMEM = pl.BlockSpec(memory_space=pltpu.SMEM)

STRIP_H = [DEEP] * 3 + [NEAR] * 16
STRIP_AT = [sum(STRIP_H[:n]) for n in range(19)]
PART_H = [DEEP] * 3 + [2, 1] * 4
PART_AT = [2 * sum(PART_H[:n]) for n in range(11)]


def lanes():
    return lax.broadcasted_iota(jnp.int32, (8, 128), 1)


def sublanes():
    return lax.broadcasted_iota(jnp.int32, (8, 128), 0)


def rolled(x, shift, axis):
    size = x.shape[axis]
    shift %= size
    return x if shift == 0 else pltpu.roll(x, shift, axis)


def mirrored(x):
    return jnp.take_along_axis(x, 7 - sublanes(), axis=0)


def ring_tile(from_right, from_left, n):
    h, at = STRIP_H[n], STRIP_AT[n]
    lane = lanes()
    return jnp.where(
        lane < h,
        rolled(from_right, -at, 1),
        jnp.where(lane >= 128 - h, rolled(from_left, 128 - h - at, 1), 0.0),
    )


def gather_kernel(
    place, block_power, ids, bond, sensor, peak, own, to_a, to_b, table, blocks, sems
):
    copies = [
        pltpu.make_async_copy(block_power, table, sems.at[0]),
        pltpu.make_async_copy(ids, blocks, sems.at[1]),
    ]
    for n in range(2, 19):
        for t in range(2):
            cut = pl.ds(128 * t, 128)
            if n == 2:
                source = bond.at[:, cut]
            else:
                field, m = (sensor, n - 3) if n < 11 else (peak, n - 11)
                source = field.at[m // 4, m % 4, :, cut]
            copies.append(
                pltpu.make_async_copy(source, own.at[n, t, pl.ds(8, 64), :], sems.at[len(copies)])
            )
    for copy in copies:
        copy.start()
    copies[0].wait()
    copies[1].wait()
    values = [table[n] for n in range(BLOCKS)]

    def look_up(k):
        stores = []
        for d in range(2):
            for t in range(2):
                index = blocks[d, tile_rows(k), 128 * t : 128 * t + 128]
                level = values
                bit = 1
                while len(level) > 1:
                    odd = (index & bit) != 0
                    level = [
                        jnp.where(odd, level[2 * n + 1], level[2 * n])
                        for n in range(len(level) // 2)
                    ]
                    bit *= 2
                stores.append((own, (d, t, tile_rows(k, 8)), level[0]))
        return stores

    tile_loop(0, 8, 1, look_up)
    for copy in copies[2:]:
        copy.wait()
    even = (place[1] & 1) == 0

    def pack(k):
        lane = lanes()
        stores = []
        right_edge = jnp.zeros((8, 128), F32)
        left_edge = jnp.zeros((8, 128), F32)
        for n in range(19):
            h, at = STRIP_H[n], STRIP_AT[n]
            here = (lane >= at) & (lane < at + h)
            tiles = [own[n, t, tile_rows(k, 8), :] for t in range(2)]
            left_edge = jnp.where(here, rolled(tiles[0], at, 1), left_edge)
            right_edge = jnp.where(here, rolled(tiles[1], at - (128 - h), 1), right_edge)
        stores.append((to_a, (tile_rows(k),), jnp.where(even, right_edge, left_edge)))
        stores.append((to_b, (tile_rows(k),), jnp.where(even, left_edge, right_edge)))
        return stores

    tile_loop(0, 8, 2, pack)


def sides(place, axis, from_a, from_b, rows):
    even = (place[axis] & 1) == 0
    a, b = from_a[rows, :], from_b[rows, :]
    return jnp.where(even, a, b), jnp.where(even, b, a)


def mirror_into(out, own, planes):
    def flip(k):
        return [
            (out, (slot, t, tile_rows(7 - k)), mirrored(own[n, t, tile_rows(k, 8), :]))
            for slot, n in enumerate(planes)
            for t in range(2)
        ]

    tile_loop(0, 8, 2, flip)


def deep_kernel(own, out):
    mirror_into(out, own, (0, 1, 2))


def layers_kernel(own, row_a, deep_in, sensor_out, peak_out):
    mirror_into(sensor_out, own, (4, 5, 6, 8, 9, 10))
    mirror_into(peak_out, own, (12, 13, 14, 16, 17, 18))


def row_kernel(place, own, col_a, col_b, deep_out, to_a, to_b):
    even = (place[0] & 1) == 0
    row = sublanes()
    strips = []
    for first in (0, 56):
        rows = slice(first, first + 8)
        right, left = sides(place, 1, col_a, col_b, rows)

        def tile(n, t):
            if t < 2:
                return own[n, t, first + 8 : first + 16, :]
            return ring_tile(right, left, n)

        strip = []
        for t in range(3):
            for n in range(3):
                strip.append(tile(n, t))
            for m in range(8):
                x, y = tile(3 + 2 * m, t), tile(4 + 2 * m, t)
                if first == 0:
                    strip.append(jnp.where(row < 4, x, rolled(y, 4, 0)))
                else:
                    strip.append(jnp.where(row >= 4, x, rolled(y, -4, 0)))
        strips.append(strip)
    top, bottom = strips
    for n in range(33):
        rows = slice(8 * n, 8 * n + 8)
        to_a[rows, :] = jnp.where(even, bottom[n], top[n])
        to_b[rows, :] = jnp.where(even, top[n], bottom[n])


def build_kernel(place, start, col_a, col_b, row_a, row_b, own, message):
    def core(k):
        right, left = sides(place, 1, col_a, col_b, tile_rows(k))
        return [(own, (n, 2, tile_rows(k, 8)), ring_tile(right, left, n)) for n in range(19)]

    tile_loop(0, 8, 2, core)
    for t in range(3):
        for n in range(11):
            at = 8 * (11 * t + n)
            below, above = sides(place, 0, row_a, row_b, slice(at, at + 8))
            if n < 3:
                own[n, t, 0:8, :] = above
                own[n, t, 72:80, :] = below
            else:
                m = 3 + 2 * (n - 3)
                own[m, t, 0:8, :] = above
                own[m, t, 72:80, :] = below
                own[m + 1, t, 0:8, :] = rolled(above, 4, 0)
                own[m + 1, t, 72:80, :] = rolled(below, -4, 0)

    planes = [0, 1, 2]
    for field in range(2):
        for d in range(2):
            planes += [3 + 8 * field + 4 * d + 3, 3 + 8 * field + 4 * d + 2]

    def pack(k):
        lane = lanes()
        column = jnp.zeros((8, 128), F32)
        for slot, n in enumerate(planes):
            h, at = PART_H[slot], PART_AT[slot]
            here = (lane >= at) & (lane < at + 2 * h)
            column = jnp.where(here, rolled(own[n, 2, tile_rows(k), :], at + h, 1), column)
        return [(message, (tile_rows(9 - k),), mirrored(column))]

    tile_loop(0, 10, 5, pack)
    row = sublanes()
    for n in range(3):
        for t in range(2):
            at = 80 + 16 * (2 * n + t)
            message[at : at + 8, :] = mirrored(own[n, t, 72:80, :])
            message[at + 8 : at + 16, :] = mirrored(own[n, t, 0:8, :])
    for field in range(2):
        for d in range(2):
            n = 3 + 8 * field + 4 * d
            for t in range(2):
                above = jnp.where(
                    row >= 4, own[n + 3, t, 0:8, :], rolled(own[n + 2, t, 0:8, :], 4, 0)
                )
                below = jnp.where(
                    row < 4, own[n + 3, t, 72:80, :], rolled(own[n + 2, t, 72:80, :], 4, 0)
                )
                at = 176 + 16 * (4 * field + 2 * d + t)
                message[at : at + 8, :] = mirrored(below)
                message[at + 8 : at + 16, :] = mirrored(above)


def partner_ring(message, slot, rows):
    h, at = PART_H[slot], PART_AT[slot]
    lane = lanes()
    return jnp.where(
        (lane < h) | (lane >= 128 - h), rolled(message[rows, :], -(at + h), 1), 0.0
    )


class Stores(list):
    def append(self, store):
        ref, index, value = store
        ref[index] = value

    def __iadd__(self, stores):
        for store in stores:
            self.append(store)
        return self


def tile_loop(start, stop, unroll, body):
    def step(j, _):
        stores = []
        for u in range(unroll):
            stores += body(start + unroll * j + u)
        for ref, index, value in stores:
            ref[index] = value
        return 0

    lax.fori_loop(0, (stop - start) // unroll, step, 0)


def tile_rows(k, add=0):
    return pl.ds(pl.multiple_of(8 * k + add, 8), 8)


class Solver:
    def __init__(self, place, tables, d, v, cond):
        self.place, self.d, self.v, self.cond = place, d, v, cond
        layer_class, share, lateral, vertical, sink = tables
        self.coef = []
        for side in range(2):
            die = d if side == 0 else 1 - d
            classes = [layer_class[die, l] for l in range(4)]
            coefs = []
            for l in range(4):
                g = lateral[classes[l]]
                up = vertical[classes[l]] if l < 3 else jnp.float32(0)
                down = vertical[classes[l - 1]] if l > 0 else jnp.float32(0)
                diagonal = 4 * g + up + down
                if l == 0:
                    diagonal = diagonal + sink[die]
                part = share[classes[l]] if share is not None else None
                if l < 3:
                    inverse = 1.0 / jnp.full((8, 128), diagonal, F32)
                    scale = inverse if part is None else inverse * part
                    coefs.append((scale, g * inverse, up * inverse, down * inverse))
                else:
                    coefs.append((diagonal, g, down, part))
            self.coef.append(coefs)
        gy = place[1]
        right = jnp.where(gy == 15, 0.0, 1.0).astype(F32)
        left = jnp.where(gy == 0, 0.0, 1.0).astype(F32)
        self.ring = jnp.where(lanes() < 64, right, left)

    def scaled(self, side, l, t, k, s):
        coef = self.coef[side][l]
        if l < 3:
            s = s * coef[0]
        else:
            if coef[3] is not None:
                s = s * coef[3]
            s = s * self.cond[self.d, 1 + side, t, tile_rows(k)]
        return s * self.ring if t == 2 else s


def prepare(solvers, bond_tile):
    def body(k):
        stores = []
        for solver in solvers:
            for t in range(3):
                bond = bond_tile(solver.d, k, t)
                stores.append((solver.cond, (solver.d, 0, t, tile_rows(k)), bond))
                for side in range(2):
                    value = 1.0 / (solver.coef[side][3][0] + bond)
                    stores.append((solver.cond, (solver.d, 1 + side, t, tile_rows(k)), value))
        return stores

    tile_loop(0, 10, 2, body)


def zero_outside(place, written):
    zero = jnp.zeros((8, 128), F32)
    for here, first in ((place[0] == 0, 8), (place[0] == 15, 80)):

        @pl.when(here)
        def _():
            for ref, at in written:
                for t in range(3):
                    ref[(*at, t, slice(first, first + 8))] = zero


def first(work, unroll=5):
    def body(k):
        stores = []
        for solver, side, layers, source in work:
            for t in range(3):
                shared = {}
                for l in layers:
                    value = solver.scaled(side, l, t, k, source(l, t, tile_rows(k), shared))
                    at = (solver.d, 0, l, t, tile_rows(k, 8))
                    stores.append((solver.v[side], at, value))
        return stores

    tile_loop(0, 10, unroll, body)
    written = [(o.v[side], (o.d, 0, l)) for o, side, layers, _ in work for l in layers]
    zero_outside(work[0][0].place, written)


def sweep(b, work, core_only=False, unroll=5):
    def body(k):
        stores = Stores()
        rows, to = tile_rows(k), tile_rows(k, 8)
        lane = lanes()
        first_lane, last_lane = lane == 0, lane == 127
        seen = {}

        for solver, side, layers, source, emit in work:
            v, d, cond = solver.v, solver.d, solver.cond

            def value(side, l, t):
                key = (id(v[side]), d, l, t)
                if key not in seen:
                    seen[key] = v[side][d, b, l, t, to, :]
                return seen[key]

            shared = {}
            for l in layers:
                coef = solver.coef[side][l]
                forward = [pltpu.roll(value(side, l, t), 1, 1) for t in range(3)]
                backward = [pltpu.roll(value(side, l, t), 127, 1) for t in range(3)]
                for t in range(2 if core_only else 3):
                    left = jnp.where(first_lane, forward[t - 1], forward[t])
                    right = jnp.where(last_lane, backward[(t + 1) % 3], backward[t])
                    around = (left + right) + (
                        v[side][d, b, l, t, pl.ds(8 * k + 7, 8), :]
                        + v[side][d, b, l, t, pl.ds(8 * k + 9, 8), :]
                    )
                    s = source(l, t, rows, shared)
                    if l < 3:
                        total = s * coef[0] + coef[1] * around
                        total = total + coef[2] * value(side, l + 1, t)
                        if l > 0:
                            total = total + coef[3] * value(side, l - 1, t)
                    else:
                        if coef[3] is not None:
                            s = s * coef[3]
                        total = (s + coef[1] * around) + coef[2] * value(side, 2, t)
                        total = total + cond[d, 0, t, rows] * value(1 - side, 3, t)
                        total = total * cond[d, 1 + side, t, rows]
                    if t == 2:
                        total = total * solver.ring
                    if emit is None:
                        stores.append((v[side], (d, 1 - b, l, t, to), total))
                    else:
                        stores += emit(l, t, k, total)
        return stores

    if core_only:
        tile_loop(1, 9, unroll, body)
    else:
        tile_loop(0, 10, unroll, body)
        written = [
            (o.v[side], (o.d, 1 - b, l))
            for o, side, layers, _, emit in work
            if emit is None
            for l in layers
        ]
        if written:
            zero_outside(work[0][0].place, written)


def place_other(planes, layers_in, message, field, d):
    other = 1 - d
    zero = jnp.zeros((8, 128), F32)

    def body(k):
        return [
            (planes, (d, l, t, tile_rows(k, 8)), layers_in(3 * other + l, t, tile_rows(k)))
            for l in range(3)
            for t in range(2)
        ]

    tile_loop(0, 8, 4, body)

    def ring(k):
        column = message[tile_rows(k), :]
        lane = lanes()
        stores = [(planes, (d, 0, 2, tile_rows(k)), zero)]
        for slot_in, l, h in ((0, 2, 2), (1, 1, 1)):
            at = PART_AT[3 + 4 * field + 2 * other + slot_in] + h
            inside = (lane < h) | (lane >= 128 - h)
            tile = jnp.where(inside, rolled(column, -at, 1), 0.0)
            stores.append((planes, (d, l, 2, tile_rows(k)), tile))
        return stores

    tile_loop(0, 10, 5, ring)
    for t in range(2):
        planes[d, 0, t, 0:8, :] = zero
        planes[d, 0, t, 72:80, :] = zero
        at = 176 + 64 * field + 32 * other + 16 * t
        above = message[at : at + 8, :]
        below = message[at + 8 : at + 16, :]
        planes[d, 2, t, 0:8, :] = above
        planes[d, 2, t, 72:80, :] = below
        planes[d, 1, t, 0:8, :] = rolled(above, 4, 0)
        planes[d, 1, t, 72:80, :] = rolled(below, -4, 0)


def place_deep(planes, deep_in, message):
    def body(k):
        return [
            (planes, (n, t, tile_rows(k, 8)), deep_in[n, t, tile_rows(k), :])
            for n in range(3)
            for t in range(2)
        ]

    tile_loop(0, 8, 4, body)

    def ring(k):
        return [
            (planes, (n, 2, tile_rows(k)), partner_ring(message, n, tile_rows(k)))
            for n in range(3)
        ]

    tile_loop(0, 10, 5, ring)
    for n in range(3):
        for t in range(2):
            at = 80 + 16 * (2 * n + t)
            planes[n, t, 0:8, :] = message[at : at + 8, :]
            planes[n, t, 72:80, :] = message[at + 8 : at + 16, :]


EVERY = (0, 1, 2, 3)


def shared_source(ref, *at):
    def source(l, t, rows, shared):
        if t not in shared:
            shared[t] = ref[(*at, t, rows)]
        return shared[t]

    return source


def layer_source(ref, first_layer, *at):
    def source(l, t, rows, shared):
        *head, last = at
        return ref[(*head, last + l - first_layer, t, rows)]

    return source


def thermal_sensor_kernel(
    place, layer_class, share, lateral, vertical, sink, own, deep_in, sensor_in, message,
    thermal, sensed, heat, weighted, early, cond, v_peak,
    v_own, v_other, s_own, s_other, planes, deep, block, sems,
):
    place_deep(deep, deep_in, message)
    plain = (layer_class, None, lateral, vertical, sink)
    with_share = (layer_class, share, lateral, vertical, sink)
    both = range(2)
    hot = [Solver(place, with_share, d, (v_own, v_other), cond) for d in both]
    sense = [Solver(place, plain, d, (s_own, s_other), cond) for d in both]
    weigh = [Solver(place, plain, d, (v_peak, None), cond) for d in both]
    prepare(hot, lambda d, k, t: (own if d == 0 else deep)[2, t, tile_rows(k), :])

    def layers_in(n, t, rows):
        return sensor_in[n, t, rows, :]

    for d in both:
        place_other(planes, layers_in, message, 0, d)
    own_power = [shared_source(own, d) for d in both]
    their_power = [shared_source(deep, 1 - d) for d in both]
    own_sensor = [layer_source(own, 0, 3 + 4 * d) for d in both]
    their_sensor = [layer_source(planes, 1, d, 0) for d in both]
    own_peak = [layer_source(weighted, 0, d, 0) for d in both]

    first(
        [(hot[d], 0, EVERY, own_power[d]) for d in both]
        + [(hot[d], 1, EVERY, their_power[d]) for d in both]
        + [(sense[d], 0, EVERY, own_sensor[d]) for d in both]
        + [(sense[d], 1, (1, 2, 3), their_sensor[d]) for d in both]
    )
    for b, reach in ((0, (2, 3)), (1, (3,))):
        sweep(
            b,
            [(hot[d], 0, EVERY, own_power[d], None) for d in both]
            + [(hot[d], 1, EVERY, their_power[d], None) for d in both]
            + [(sense[d], 0, EVERY, own_sensor[d], None) for d in both]
            + [(sense[d], 1, reach, their_sensor[d], None) for d in both],
        )

    def emit_own(d):
        def emit(l, t, k, total):
            peak = own[11 + 4 * d + l, t, tile_rows(k), :]
            stores = [(weighted, (d, l, t, tile_rows(k)), total * peak)]
            if t < 2:
                stores.append((v_own, (d, 1, l, t, tile_rows(k, 8)), total))
            return stores

        return emit

    def emit_other(d):
        return lambda l, t, k, total: [(heat, (d, l - 1, t, tile_rows(k)), total)]

    def emit_block(d):
        return lambda l, t, k, total: [(block, (d, l, t, tile_rows(k, -8)), total)]

    def emit_early(d):
        return lambda l, t, k, total: [(early, (d, t, tile_rows(k, -8)), total)]

    sweep(
        0,
        [(hot[d], 0, EVERY, own_power[d], emit_own(d)) for d in both]
        + [(hot[d], 1, (1, 2, 3), their_power[d], emit_other(d)) for d in both],
    )
    copies = []

    def send(source, out, d, l, t):
        to = out.at[d, l, :, pl.ds(128 * t, 128)]
        copies.append(pltpu.make_async_copy(source, to, sems.at[len(copies)]))
        copies[-1].start()

    for d in both:
        for l in EVERY:
            for t in range(2):
                send(v_own.at[d, 1, l, t, pl.ds(16, 64), :], thermal, d, l, t)
    sweep(
        0,
        [(sense[d], 0, EVERY, own_sensor[d], emit_block(d)) for d in both],
        core_only=True,
        unroll=4,
    )
    for d in both:
        for l in EVERY:
            for t in range(2):
                send(block.at[d, l, t], sensed, d, l, t)
    first([(weigh[d], 0, EVERY, own_peak[d]) for d in both], unroll=5)
    sweep(0, [(weigh[d], 0, (0, 1, 2), own_peak[d], None) for d in both], unroll=5)
    sweep(1, [(weigh[d], 0, (0, 1), own_peak[d], None) for d in both], unroll=5)
    sweep(
        0,
        [(weigh[d], 0, (0,), own_peak[d], emit_early(d)) for d in both],
        core_only=True,
        unroll=4,
    )
    for copy in copies:
        copy.wait()


def peak_kernel(
    place, layer_class, lateral, vertical, sink, peak_in, message, heat, weighted, early, cond,
    v_start, out, v_peak, v_other, planes, block, sems,
):
    plain = (layer_class, None, lateral, vertical, sink)
    both = range(2)
    copies = []

    def send(source, d, l, t):
        to = out.at[d, l, :, pl.ds(128 * t, 128)]
        copies.append(pltpu.make_async_copy(source, to, sems.at[len(copies)]))
        copies[-1].start()

    for d in both:
        for t in range(2):
            send(early.at[d, t], d, 0, t)
    solver = [Solver(place, plain, d, (v_peak, v_other), cond) for d in both]

    def layers_in(n, t, rows):
        return peak_in[n, t, rows, :]

    for d in both:
        place_other(planes, layers_in, message, 1, d)
    own_peak = [layer_source(weighted, 0, d, 0) for d in both]

    def their_peak(d):
        def source(l, t, rows, shared):
            return planes[d, l - 1, t, rows, :] * heat[d, l - 1, t, rows, :]

        return source

    def emit_block(d):
        return lambda l, t, k, total: [(block, (d, l - 1, t, tile_rows(k, -8)), total)]

    first([(solver[d], 1, (1, 2, 3), their_peak(d)) for d in both], unroll=5)
    sweep(
        0,
        [(solver[d], 0, (3,), own_peak[d], None) for d in both]
        + [(solver[d], 1, (2, 3), their_peak(d), None) for d in both],
        unroll=5,
    )
    sweep(
        1,
        [(solver[d], 0, (2, 3), own_peak[d], None) for d in both]
        + [(solver[d], 1, (3,), their_peak(d), None) for d in both],
        unroll=5,
    )
    for d in both:
        sweep(
            0,
            [(solver[d], 0, (1, 2, 3), own_peak[d], emit_block(d))],
            core_only=True,
            unroll=4,
        )
        for l in (1, 2, 3):
            for t in range(2):
                send(block.at[d, l - 1, t], d, l, t)
    for copy in copies:
        copy.wait()


PLANES = (19, 3, ROWS, 128)
FIELD = (2, 4, 64, 256)
V = (2, 2, 4, 3, ROWS + 16, 128)
OTHER = (2, 3, 3, ROWS, 128)
DEEP_PLANES = (3, 3, ROWS, 128)
KEPT = [
    (2, 3, 3, ROWS, 128),
    (2, 4, 3, ROWS, 128),
    (2, 2, 64, 128),
    (2, 3, 3, ROWS, 128),
    V,
]


def call(kernel, tables, arrays, outs, scratch=(), flops=0, aliases={}, hbm=0, hbm_out=0, vmem=16, name=None):
    shapes = [jax.ShapeDtypeStruct(shape, F32) for shape in outs]
    arrays = [
        pltpu.with_memory_space_constraint(x, pltpu.HBM) if i < hbm else x
        for i, x in enumerate(arrays)
    ]
    anywhere = pl.BlockSpec(memory_space=pltpu.HBM)
    return pl.pallas_call(
        kernel,
        out_shape=shapes,
        in_specs=[SMEM] * len(tables) + [anywhere] * hbm + [VMEM] * (len(arrays) - hbm),
        out_specs=[anywhere] * hbm_out + [VMEM] * (len(shapes) - hbm_out),
        scratch_shapes=[pltpu.VMEM(x, F32) if isinstance(x, tuple) else x for x in scratch],
        input_output_aliases={len(tables) + i: o for i, o in aliases.items()},
        compiler_params=pltpu.CompilerParams(vmem_limit_bytes=vmem << 20),
        cost_estimate=pl.CostEstimate(flops=flops, bytes_accessed=1024, transcendentals=0),
        name=name,
    )(*tables, *arrays)


def pairs(count, odd):
    if odd:
        return [(i, ((i - 1) ^ 1) + 1) for i in range(1, count - 1)]
    return [(i, i ^ 1) for i in range(count)]


def local(
    block_ids,
    block_power,
    layer_class,
    power_share,
    lateral_k,
    vertical_k,
    sink_conductance,
    bond_conductance,
    peak_factors,
    sensor_weight,
):
    nx, ny = lax.axis_size("gx"), lax.axis_size("gy")
    facing = [(i, nx - 1 - i) for i in range(nx)]
    place = jnp.stack([lax.axis_index("gx"), lax.axis_index("gy")]).astype(jnp.int32)
    own, col_a, col_b = call(
        gather_kernel,
        (place,),
        (block_power, block_ids, bond_conductance, sensor_weight, peak_factors),
        [PLANES, (64, 128), (64, 128)],
        [
            pltpu.SMEM((BLOCKS,), F32),
            pltpu.VMEM((2, 64, 256), jnp.int32),
            pltpu.SemaphoreType.DMA((36,)),
        ],
        hbm=5,
        name="gather",
    )
    col_a = lax.ppermute(col_a, "gy", pairs(ny, False))
    col_b = lax.ppermute(col_b, "gy", pairs(ny, True))
    (deep_out,) = call(
        deep_kernel, (), (own,), [(3, 2, 64, 128)], flops=10**11, name="deep_out"
    )
    deep_in = lax.ppermute(deep_out, "gx", facing)
    row_a, row_b = call(
        row_kernel, (place,), (own, col_a, col_b, deep_out), [(264, 128), (264, 128)], flops=10**11, name="rows"
    )
    layers = (6, 2, 64, 128)
    sensor_out, peak_out = call(
        layers_kernel, (), (own, row_a, deep_in), [layers, layers], flops=10**11, name="layers_out"
    )
    row_a = lax.ppermute(row_a, "gx", pairs(nx, False))
    row_b = lax.ppermute(row_b, "gx", pairs(nx, True))
    sensor_in = lax.ppermute(sensor_out, "gx", facing)
    own, message = call(
        build_kernel,
        (place,),
        (own, col_a, col_b, row_a, row_b),
        [PLANES, (304, 128)],
        aliases={0: 0},
        flops=10**11,
        name="build",
    )
    peak_out, _ = lax.optimization_barrier((peak_out, message))
    message = lax.ppermute(message, "gx", facing)
    peak_in = lax.ppermute(peak_out, "gx", facing)
    thermal, sensed, *kept = call(
        thermal_sensor_kernel,
        (place, layer_class, power_share, lateral_k, vertical_k, sink_conductance),
        (own, deep_in, sensor_in, message),
        [FIELD, FIELD] + KEPT,
        [V, V, V, V, OTHER, DEEP_PLANES, (2, 4, 2, 64, 128), pltpu.SemaphoreType.DMA((32,))],
        flops=10**11,
        hbm_out=2,
        vmem=24,
        name="thermal_sensor",
    )
    peak, _ = call(
        peak_kernel,
        (place, layer_class, lateral_k, vertical_k, sink_conductance),
        (peak_in, message, *kept),
        [FIELD, V],
        [V, OTHER, (2, 3, 2, 64, 128), pltpu.SemaphoreType.DMA((16,))],
        aliases={6: 1},
        hbm_out=1,
        name="peak",
    )
    return thermal, peak, sensed


def solution(mesh):
    return jax.shard_map(
        local,
        mesh=mesh,
        in_specs=(
            P(None, "gx", "gy"),
            P(),
            P(),
            P(),
            P(),
            P(),
            P(),
            P("gx", "gy"),
            P(None, None, "gx", "gy"),
            P(None, None, "gx", "gy"),
        ),
        out_specs=(P(None, None, "gx", "gy"),) * 3,
        check_vma=False,
    )
```

```python
import jax
import jax.numpy as jnp
from jax import lax
from jax.experimental import pallas as pl
from jax.experimental.pallas import tpu as pltpu
from jax.sharding import PartitionSpec as P


BLOCKS = 32
ROWS = 80
DEEP = 6
NEAR = 3
F32 = jnp.float32

VMEM = pl.BlockSpec(memory_space=pltpu.VMEM)
SMEM = pl.BlockSpec(memory_space=pltpu.SMEM)

STRIP_H = [DEEP] * 3 + [NEAR] * 16
STRIP_AT = [sum(STRIP_H[:n]) for n in range(19)]
PART_H = [DEEP] * 3 + [2, 1] * 4
PART_AT = [2 * sum(PART_H[:n]) for n in range(11)]


def lanes():
    return lax.broadcasted_iota(jnp.int32, (8, 128), 1)


def sublanes():
    return lax.broadcasted_iota(jnp.int32, (8, 128), 0)


def rolled(x, shift, axis):
    size = x.shape[axis]
    shift %= size
    return x if shift == 0 else pltpu.roll(x, shift, axis)


def mirrored(x):
    return jnp.take_along_axis(x, 7 - sublanes(), axis=0)


def ring_tile(from_right, from_left, n):
    h, at = STRIP_H[n], STRIP_AT[n]
    lane = lanes()
    return jnp.where(
        lane < h,
        rolled(from_right, -at, 1),
        jnp.where(lane >= 128 - h, rolled(from_left, 128 - h - at, 1), 0.0),
    )


def gather_kernel(
    place, block_power, ids, bond, sensor, peak, own, to_a, to_b, table, blocks, sems
):
    copies = [
        pltpu.make_async_copy(block_power, table, sems.at[0]),
        pltpu.make_async_copy(ids, blocks, sems.at[1]),
    ]
    for n in range(2, 19):
        for t in range(2):
            cut = pl.ds(128 * t, 128)
            if n == 2:
                source = bond.at[:, cut]
            else:
                field, m = (sensor, n - 3) if n < 11 else (peak, n - 11)
                source = field.at[m // 4, m % 4, :, cut]
            copies.append(
                pltpu.make_async_copy(source, own.at[n, t, pl.ds(8, 64), :], sems.at[len(copies)])
            )
    for copy in copies:
        copy.start()
    copies[0].wait()
    copies[1].wait()
    values = [table[n] for n in range(BLOCKS)]

    def look_up(k):
        stores = []
        for d in range(2):
            for t in range(2):
                index = blocks[d, tile_rows(k), 128 * t : 128 * t + 128]
                level = values
                bit = 1
                while len(level) > 1:
                    odd = (index & bit) != 0
                    level = [
                        jnp.where(odd, level[2 * n + 1], level[2 * n])
                        for n in range(len(level) // 2)
                    ]
                    bit *= 2
                stores.append((own, (d, t, tile_rows(k, 8)), level[0]))
        return stores

    tile_loop(0, 8, 2, look_up)
    for copy in copies[2:]:
        copy.wait()
    even = (place[1] & 1) == 0

    def pack(k):
        lane = lanes()
        stores = []
        right_edge = jnp.zeros((8, 128), F32)
        left_edge = jnp.zeros((8, 128), F32)
        for n in range(19):
            h, at = STRIP_H[n], STRIP_AT[n]
            here = (lane >= at) & (lane < at + h)
            tiles = [own[n, t, tile_rows(k, 8), :] for t in range(2)]
            left_edge = jnp.where(here, rolled(tiles[0], at, 1), left_edge)
            right_edge = jnp.where(here, rolled(tiles[1], at - (128 - h), 1), right_edge)
        stores.append((to_a, (tile_rows(k),), jnp.where(even, right_edge, left_edge)))
        stores.append((to_b, (tile_rows(k),), jnp.where(even, left_edge, right_edge)))
        return stores

    tile_loop(0, 8, 4, pack)


def sides(place, axis, from_a, from_b, rows):
    even = (place[axis] & 1) == 0
    a, b = from_a[rows, :], from_b[rows, :]
    return jnp.where(even, a, b), jnp.where(even, b, a)


def mirror_into(out, own, planes):
    def flip(k):
        return [
            (out, (slot, t, tile_rows(7 - k)), mirrored(own[n, t, tile_rows(k, 8), :]))
            for slot, n in enumerate(planes)
            for t in range(2)
        ]

    tile_loop(0, 8, 2, flip)


def deep_kernel(own, out):
    mirror_into(out, own, (0, 1, 2))


def layers_kernel(own, row_a, sensor_out, peak_out):
    mirror_into(sensor_out, own, (4, 5, 6, 8, 9, 10))
    mirror_into(peak_out, own, (12, 13, 14, 16, 17, 18))


def row_kernel(place, own, col_a, col_b, deep_out, to_a, to_b):
    even = (place[0] & 1) == 0
    row = sublanes()
    strips = []
    for first in (0, 56):
        rows = slice(first, first + 8)
        right, left = sides(place, 1, col_a, col_b, rows)

        def tile(n, t):
            if t < 2:
                return own[n, t, first + 8 : first + 16, :]
            return ring_tile(right, left, n)

        strip = []
        for t in range(3):
            for n in range(3):
                strip.append(tile(n, t))
            for m in range(8):
                x, y = tile(3 + 2 * m, t), tile(4 + 2 * m, t)
                if first == 0:
                    strip.append(jnp.where(row < 4, x, rolled(y, 4, 0)))
                else:
                    strip.append(jnp.where(row >= 4, x, rolled(y, -4, 0)))
        strips.append(strip)
    top, bottom = strips
    for n in range(33):
        rows = slice(8 * n, 8 * n + 8)
        to_a[rows, :] = jnp.where(even, bottom[n], top[n])
        to_b[rows, :] = jnp.where(even, top[n], bottom[n])


def build_kernel(place, start, col_a, col_b, row_a, row_b, deep_in, own, message):
    def core(k):
        right, left = sides(place, 1, col_a, col_b, tile_rows(k))
        return [(own, (n, 2, tile_rows(k, 8)), ring_tile(right, left, n)) for n in range(19)]

    tile_loop(0, 8, 4, core)
    for t in range(3):
        for n in range(11):
            at = 8 * (11 * t + n)
            below, above = sides(place, 0, row_a, row_b, slice(at, at + 8))
            if n < 3:
                own[n, t, 0:8, :] = above
                own[n, t, 72:80, :] = below
            else:
                m = 3 + 2 * (n - 3)
                own[m, t, 0:8, :] = above
                own[m, t, 72:80, :] = below
                own[m + 1, t, 0:8, :] = rolled(above, 4, 0)
                own[m + 1, t, 72:80, :] = rolled(below, -4, 0)

    planes = [0, 1, 2]
    for field in range(2):
        for d in range(2):
            planes += [3 + 8 * field + 4 * d + 3, 3 + 8 * field + 4 * d + 2]

    def pack(k):
        lane = lanes()
        column = jnp.zeros((8, 128), F32)
        for slot, n in enumerate(planes):
            h, at = PART_H[slot], PART_AT[slot]
            here = (lane >= at) & (lane < at + 2 * h)
            column = jnp.where(here, rolled(own[n, 2, tile_rows(k), :], at + h, 1), column)
        return [(message, (tile_rows(9 - k),), mirrored(column))]

    tile_loop(0, 10, 5, pack)
    row = sublanes()
    for n in range(3):
        for t in range(2):
            at = 80 + 16 * (2 * n + t)
            message[at : at + 8, :] = mirrored(own[n, t, 72:80, :])
            message[at + 8 : at + 16, :] = mirrored(own[n, t, 0:8, :])
    for field in range(2):
        for d in range(2):
            n = 3 + 8 * field + 4 * d
            for t in range(2):
                above = jnp.where(
                    row >= 4, own[n + 3, t, 0:8, :], rolled(own[n + 2, t, 0:8, :], 4, 0)
                )
                below = jnp.where(
                    row < 4, own[n + 3, t, 72:80, :], rolled(own[n + 2, t, 72:80, :], 4, 0)
                )
                at = 176 + 16 * (4 * field + 2 * d + t)
                message[at : at + 8, :] = mirrored(below)
                message[at + 8 : at + 16, :] = mirrored(above)


def partner_ring(message, slot, rows):
    h, at = PART_H[slot], PART_AT[slot]
    lane = lanes()
    return jnp.where(
        (lane < h) | (lane >= 128 - h), rolled(message[rows, :], -(at + h), 1), 0.0
    )


class Stores(list):
    def append(self, store):
        ref, index, value = store
        ref[index] = value

    def __iadd__(self, stores):
        for store in stores:
            self.append(store)
        return self


def tile_loop(start, stop, unroll, body):
    def step(j, _):
        stores = []
        for u in range(unroll):
            stores += body(start + unroll * j + u)
        for ref, index, value in stores:
            ref[index] = value
        return 0

    lax.fori_loop(0, (stop - start) // unroll, step, 0)


def tile_rows(k, add=0):
    return pl.ds(pl.multiple_of(8 * k + add, 8), 8)


class Solver:
    def __init__(self, place, tables, d, v, cond):
        self.place, self.d, self.v, self.cond = place, d, v, cond
        layer_class, share, lateral, vertical, sink = tables
        self.coef = []
        for side in range(2):
            die = d if side == 0 else 1 - d
            classes = [layer_class[die, l] for l in range(4)]
            coefs = []
            for l in range(4):
                g = lateral[classes[l]]
                up = vertical[classes[l]] if l < 3 else jnp.float32(0)
                down = vertical[classes[l - 1]] if l > 0 else jnp.float32(0)
                diagonal = 4 * g + up + down
                if l == 0:
                    diagonal = diagonal + sink[die]
                part = share[classes[l]] if share is not None else None
                if l < 3:
                    inverse = 1.0 / jnp.full((8, 128), diagonal, F32)
                    scale = inverse if part is None else inverse * part
                    coefs.append((scale, g * inverse, up * inverse, down * inverse))
                else:
                    coefs.append((diagonal, g, down, part))
            self.coef.append(coefs)
        gy = place[1]
        right = jnp.where(gy == 15, 0.0, 1.0).astype(F32)
        left = jnp.where(gy == 0, 0.0, 1.0).astype(F32)
        self.ring = jnp.where(lanes() < 64, right, left)

    def scaled(self, side, l, t, k, s):
        coef = self.coef[side][l]
        if l < 3:
            s = s * coef[0]
        else:
            if coef[3] is not None:
                s = s * coef[3]
            s = s * self.cond[self.d, 1 + side, t, tile_rows(k)]
        return s * self.ring if t == 2 else s


def prepare(solvers, bond_tile):
    def body(k):
        stores = []
        for solver in solvers:
            for t in range(3):
                bond = bond_tile(solver.d, k, t)
                stores.append((solver.cond, (solver.d, 0, t, tile_rows(k)), bond))
                for side in range(2):
                    value = 1.0 / (solver.coef[side][3][0] + bond)
                    stores.append((solver.cond, (solver.d, 1 + side, t, tile_rows(k)), value))
        return stores

    tile_loop(0, 10, 2, body)


def zero_outside(place, written):
    zero = jnp.zeros((8, 128), F32)
    for here, first in ((place[0] == 0, 8), (place[0] == 15, 80)):

        @pl.when(here)
        def _():
            for ref, at in written:
                for t in range(3):
                    ref[(*at, t, slice(first, first + 8))] = zero


def first(work, unroll=5):
    def body(k):
        stores = []
        for solver, side, layers, source in work:
            for t in range(3):
                shared = {}
                for l in layers:
                    value = solver.scaled(side, l, t, k, source(l, t, tile_rows(k), shared))
                    at = (solver.d, 0, l, t, tile_rows(k, 8))
                    stores.append((solver.v[side], at, value))
        return stores

    tile_loop(0, 10, unroll, body)
    written = [(o.v[side], (o.d, 0, l)) for o, side, layers, _ in work for l in layers]
    zero_outside(work[0][0].place, written)


def sweep(b, work, core_only=False, unroll=5):
    def body(k):
        stores = Stores()
        rows, to = tile_rows(k), tile_rows(k, 8)
        lane = lanes()
        first_lane, last_lane = lane == 0, lane == 127
        seen = {}

        for solver, side, layers, source, emit in work:
            v, d, cond = solver.v, solver.d, solver.cond

            def value(side, l, t):
                key = (id(v[side]), d, l, t)
                if key not in seen:
                    seen[key] = v[side][d, b, l, t, to, :]
                return seen[key]

            shared = {}
            for l in layers:
                coef = solver.coef[side][l]
                forward = [pltpu.roll(value(side, l, t), 1, 1) for t in range(3)]
                backward = [pltpu.roll(value(side, l, t), 127, 1) for t in range(3)]
                for t in range(2 if core_only else 3):
                    left = jnp.where(first_lane, forward[t - 1], forward[t])
                    right = jnp.where(last_lane, backward[(t + 1) % 3], backward[t])
                    around = (left + right) + (
                        v[side][d, b, l, t, pl.ds(8 * k + 7, 8), :]
                        + v[side][d, b, l, t, pl.ds(8 * k + 9, 8), :]
                    )
                    s = source(l, t, rows, shared)
                    if l < 3:
                        total = s * coef[0] + coef[1] * around
                        total = total + coef[2] * value(side, l + 1, t)
                        if l > 0:
                            total = total + coef[3] * value(side, l - 1, t)
                    else:
                        if coef[3] is not None:
                            s = s * coef[3]
                        total = (s + coef[1] * around) + coef[2] * value(side, 2, t)
                        total = total + cond[d, 0, t, rows] * value(1 - side, 3, t)
                        total = total * cond[d, 1 + side, t, rows]
                    if t == 2:
                        total = total * solver.ring
                    if emit is None:
                        stores.append((v[side], (d, 1 - b, l, t, to), total))
                    else:
                        stores += emit(l, t, k, total)
        return stores

    if core_only:
        tile_loop(1, 9, unroll, body)
    else:
        tile_loop(0, 10, unroll, body)
        written = [
            (o.v[side], (o.d, 1 - b, l))
            for o, side, layers, _, emit in work
            if emit is None
            for l in layers
        ]
        if written:
            zero_outside(work[0][0].place, written)


def place_other(planes, layers_in, message, field, d):
    other = 1 - d
    zero = jnp.zeros((8, 128), F32)

    def body(k):
        return [
            (planes, (d, l, t, tile_rows(k, 8)), layers_in(3 * other + l, t, tile_rows(k)))
            for l in range(3)
            for t in range(2)
        ]

    tile_loop(0, 8, 4, body)

    def ring(k):
        column = message[tile_rows(k), :]
        lane = lanes()
        stores = [(planes, (d, 0, 2, tile_rows(k)), zero)]
        for slot_in, l, h in ((0, 2, 2), (1, 1, 1)):
            at = PART_AT[3 + 4 * field + 2 * other + slot_in] + h
            inside = (lane < h) | (lane >= 128 - h)
            tile = jnp.where(inside, rolled(column, -at, 1), 0.0)
            stores.append((planes, (d, l, 2, tile_rows(k)), tile))
        return stores

    tile_loop(0, 10, 5, ring)
    for t in range(2):
        planes[d, 0, t, 0:8, :] = zero
        planes[d, 0, t, 72:80, :] = zero
        at = 176 + 64 * field + 32 * other + 16 * t
        above = message[at : at + 8, :]
        below = message[at + 8 : at + 16, :]
        planes[d, 2, t, 0:8, :] = above
        planes[d, 2, t, 72:80, :] = below
        planes[d, 1, t, 0:8, :] = rolled(above, 4, 0)
        planes[d, 1, t, 72:80, :] = rolled(below, -4, 0)


def place_deep(planes, deep_in, message):
    def body(k):
        return [
            (planes, (n, t, tile_rows(k, 8)), deep_in[n, t, tile_rows(k), :])
            for n in range(3)
            for t in range(2)
        ]

    tile_loop(0, 8, 4, body)

    def ring(k):
        return [
            (planes, (n, 2, tile_rows(k)), partner_ring(message, n, tile_rows(k)))
            for n in range(3)
        ]

    tile_loop(0, 10, 5, ring)
    for n in range(3):
        for t in range(2):
            at = 80 + 16 * (2 * n + t)
            planes[n, t, 0:8, :] = message[at : at + 8, :]
            planes[n, t, 72:80, :] = message[at + 8 : at + 16, :]


EVERY = (0, 1, 2, 3)


def shared_source(ref, *at):
    def source(l, t, rows, shared):
        if t not in shared:
            shared[t] = ref[(*at, t, rows)]
        return shared[t]

    return source


def layer_source(ref, first_layer, *at):
    def source(l, t, rows, shared):
        *head, last = at
        return ref[(*head, last + l - first_layer, t, rows)]

    return source


def thermal_sensor_kernel(
    place, layer_class, share, lateral, vertical, sink, own, deep_in, sensor_in, message,
    thermal, sensed, heat, weighted, early, cond, v_peak,
    v_own, v_other, s_own, s_other, planes, deep, block, sems,
):
    place_deep(deep, deep_in, message)
    plain = (layer_class, None, lateral, vertical, sink)
    with_share = (layer_class, share, lateral, vertical, sink)
    both = range(2)
    hot = [Solver(place, with_share, d, (v_own, v_other), cond) for d in both]
    sense = [Solver(place, plain, d, (s_own, s_other), cond) for d in both]
    weigh = [Solver(place, plain, d, (v_peak, None), cond) for d in both]
    prepare(hot, lambda d, k, t: (own if d == 0 else deep)[2, t, tile_rows(k), :])

    def layers_in(n, t, rows):
        return sensor_in[n, t, rows, :]

    for d in both:
        place_other(planes, layers_in, message, 0, d)
    own_power = [shared_source(own, d) for d in both]
    their_power = [shared_source(deep, 1 - d) for d in both]
    own_sensor = [layer_source(own, 0, 3 + 4 * d) for d in both]
    their_sensor = [layer_source(planes, 1, d, 0) for d in both]
    own_peak = [layer_source(weighted, 0, d, 0) for d in both]

    first(
        [(hot[d], 0, EVERY, own_power[d]) for d in both]
        + [(hot[d], 1, EVERY, their_power[d]) for d in both]
        + [(sense[d], 0, EVERY, own_sensor[d]) for d in both]
        + [(sense[d], 1, (1, 2, 3), their_sensor[d]) for d in both]
    )
    for b, reach in ((0, (2, 3)), (1, (3,))):
        sweep(
            b,
            [(hot[d], 0, EVERY, own_power[d], None) for d in both]
            + [(hot[d], 1, EVERY, their_power[d], None) for d in both]
            + [(sense[d], 0, EVERY, own_sensor[d], None) for d in both]
            + [(sense[d], 1, reach, their_sensor[d], None) for d in both],
        )

    def emit_own(d):
        def emit(l, t, k, total):
            peak = own[11 + 4 * d + l, t, tile_rows(k), :]
            stores = [(weighted, (d, l, t, tile_rows(k)), total * peak)]
            if t < 2:
                stores.append((v_own, (d, 1, l, t, tile_rows(k, 8)), total))
            return stores

        return emit

    def emit_other(d):
        return lambda l, t, k, total: [(heat, (d, l - 1, t, tile_rows(k)), total)]

    def emit_block(d):
        return lambda l, t, k, total: [(block, (d, l, t, tile_rows(k, -8)), total)]

    def emit_early(d):
        return lambda l, t, k, total: [(early, (d, t, tile_rows(k, -8)), total)]

    sweep(
        0,
        [(hot[d], 0, EVERY, own_power[d], emit_own(d)) for d in both]
        + [(hot[d], 1, (1, 2, 3), their_power[d], emit_other(d)) for d in both],
    )
    copies = []

    def send(source, out, d, l, t):
        to = out.at[d, l, :, pl.ds(128 * t, 128)]
        copies.append(pltpu.make_async_copy(source, to, sems.at[len(copies)]))
        copies[-1].start()

    for d in both:
        for l in EVERY:
            for t in range(2):
                send(v_own.at[d, 1, l, t, pl.ds(16, 64), :], thermal, d, l, t)
    sweep(
        0,
        [(sense[d], 0, EVERY, own_sensor[d], emit_block(d)) for d in both],
        core_only=True,
        unroll=4,
    )
    for d in both:
        for l in EVERY:
            for t in range(2):
                send(block.at[d, l, t], sensed, d, l, t)
    first([(weigh[d], 0, EVERY, own_peak[d]) for d in both], unroll=5)
    sweep(0, [(weigh[d], 0, (0, 1, 2), own_peak[d], None) for d in both], unroll=5)
    sweep(1, [(weigh[d], 0, (0, 1), own_peak[d], None) for d in both], unroll=5)
    sweep(
        0,
        [(weigh[d], 0, (0,), own_peak[d], emit_early(d)) for d in both],
        core_only=True,
        unroll=4,
    )
    for copy in copies:
        copy.wait()


def peak_kernel(
    place, layer_class, lateral, vertical, sink, peak_in, message, heat, weighted, early, cond,
    v_start, out, v_peak, v_other, planes, block, sems,
):
    plain = (layer_class, None, lateral, vertical, sink)
    both = range(2)
    copies = []

    def send(source, d, l, t):
        to = out.at[d, l, :, pl.ds(128 * t, 128)]
        copies.append(pltpu.make_async_copy(source, to, sems.at[len(copies)]))
        copies[-1].start()

    for d in both:
        for t in range(2):
            send(early.at[d, t], d, 0, t)
    solver = [Solver(place, plain, d, (v_peak, v_other), cond) for d in both]

    def layers_in(n, t, rows):
        return peak_in[n, t, rows, :]

    for d in both:
        place_other(planes, layers_in, message, 1, d)
    own_peak = [layer_source(weighted, 0, d, 0) for d in both]

    def their_peak(d):
        def source(l, t, rows, shared):
            return planes[d, l - 1, t, rows, :] * heat[d, l - 1, t, rows, :]

        return source

    def emit_block(d):
        return lambda l, t, k, total: [(block, (d, l - 1, t, tile_rows(k, -8)), total)]

    first([(solver[d], 1, (1, 2, 3), their_peak(d)) for d in both], unroll=5)
    sweep(
        0,
        [(solver[d], 0, (3,), own_peak[d], None) for d in both]
        + [(solver[d], 1, (2, 3), their_peak(d), None) for d in both],
        unroll=5,
    )
    sweep(
        1,
        [(solver[d], 0, (2, 3), own_peak[d], None) for d in both]
        + [(solver[d], 1, (3,), their_peak(d), None) for d in both],
        unroll=5,
    )
    for d in both:
        sweep(
            0,
            [(solver[d], 0, (1, 2, 3), own_peak[d], emit_block(d))],
            core_only=True,
            unroll=4,
        )
        for l in (1, 2, 3):
            for t in range(2):
                send(block.at[d, l - 1, t], d, l, t)
    for copy in copies:
        copy.wait()


PLANES = (19, 3, ROWS, 128)
FIELD = (2, 4, 64, 256)
V = (2, 2, 4, 3, ROWS + 16, 128)
OTHER = (2, 3, 3, ROWS, 128)
DEEP_PLANES = (3, 3, ROWS, 128)
KEPT = [
    (2, 3, 3, ROWS, 128),
    (2, 4, 3, ROWS, 128),
    (2, 2, 64, 128),
    (2, 3, 3, ROWS, 128),
    V,
]


def call(kernel, tables, arrays, outs, scratch=(), flops=0, aliases={}, hbm=0, hbm_out=0, vmem=16, name=None):
    shapes = [jax.ShapeDtypeStruct(shape, F32) for shape in outs]
    arrays = [
        pltpu.with_memory_space_constraint(x, pltpu.HBM) if i < hbm else x
        for i, x in enumerate(arrays)
    ]
    anywhere = pl.BlockSpec(memory_space=pltpu.HBM)
    return pl.pallas_call(
        kernel,
        out_shape=shapes,
        in_specs=[SMEM] * len(tables) + [anywhere] * hbm + [VMEM] * (len(arrays) - hbm),
        out_specs=[anywhere] * hbm_out + [VMEM] * (len(shapes) - hbm_out),
        scratch_shapes=[pltpu.VMEM(x, F32) if isinstance(x, tuple) else x for x in scratch],
        input_output_aliases={len(tables) + i: o for i, o in aliases.items()},
        compiler_params=pltpu.CompilerParams(vmem_limit_bytes=vmem << 20),
        cost_estimate=pl.CostEstimate(flops=flops, bytes_accessed=1024, transcendentals=0),
        name=name,
    )(*tables, *arrays)


def pairs(count, odd):
    if odd:
        return [(i, ((i - 1) ^ 1) + 1) for i in range(1, count - 1)]
    return [(i, i ^ 1) for i in range(count)]


def local(
    block_ids,
    block_power,
    layer_class,
    power_share,
    lateral_k,
    vertical_k,
    sink_conductance,
    bond_conductance,
    peak_factors,
    sensor_weight,
):
    nx, ny = lax.axis_size("gx"), lax.axis_size("gy")
    facing = [(i, nx - 1 - i) for i in range(nx)]
    place = jnp.stack([lax.axis_index("gx"), lax.axis_index("gy")]).astype(jnp.int32)
    own, col_a, col_b = call(
        gather_kernel,
        (place,),
        (block_power, block_ids, bond_conductance, sensor_weight, peak_factors),
        [PLANES, (64, 128), (64, 128)],
        [
            pltpu.SMEM((BLOCKS,), F32),
            pltpu.VMEM((2, 64, 256), jnp.int32),
            pltpu.SemaphoreType.DMA((36,)),
        ],
        hbm=5,
        name="gather",
    )
    col_a = lax.ppermute(col_a, "gy", pairs(ny, False))
    col_b = lax.ppermute(col_b, "gy", pairs(ny, True))
    (deep_out,) = call(
        deep_kernel, (), (own,), [(3, 2, 64, 128)], flops=10**11, name="deep_out"
    )
    deep_in = lax.ppermute(deep_out, "gx", facing)
    row_a, row_b = call(
        row_kernel, (place,), (own, col_a, col_b, deep_out), [(264, 128), (264, 128)], flops=10**11, name="rows"
    )
    layers = (6, 2, 64, 128)
    sensor_out, peak_out = call(
        layers_kernel, (), (own, row_a), [layers, layers], flops=10**11, name="layers_out"
    )
    row_a = lax.ppermute(row_a, "gx", pairs(nx, False))
    row_b = lax.ppermute(row_b, "gx", pairs(nx, True))
    sensor_in = lax.ppermute(sensor_out, "gx", facing)
    own, message = call(
        build_kernel,
        (place,),
        (own, col_a, col_b, row_a, row_b, deep_in),
        [PLANES, (304, 128)],
        aliases={0: 0},
        flops=10**11,
        name="build",
    )
    peak_out, _ = lax.optimization_barrier((peak_out, message))
    message = lax.ppermute(message, "gx", facing)
    peak_in = lax.ppermute(peak_out, "gx", facing)
    thermal, sensed, *kept = call(
        thermal_sensor_kernel,
        (place, layer_class, power_share, lateral_k, vertical_k, sink_conductance),
        (own, deep_in, sensor_in, message),
        [FIELD, FIELD] + KEPT,
        [V, V, V, V, OTHER, DEEP_PLANES, (2, 4, 2, 64, 128), pltpu.SemaphoreType.DMA((32,))],
        flops=10**11,
        hbm_out=2,
        vmem=24,
        name="thermal_sensor",
    )
    peak, _ = call(
        peak_kernel,
        (place, layer_class, lateral_k, vertical_k, sink_conductance),
        (peak_in, message, *kept),
        [FIELD, V],
        [V, OTHER, (2, 3, 2, 64, 128), pltpu.SemaphoreType.DMA((16,))],
        aliases={6: 1},
        hbm_out=1,
        name="peak",
    )
    return thermal, peak, sensed


def solution(mesh):
    return jax.shard_map(
        local,
        mesh=mesh,
        in_specs=(
            P(None, "gx", "gy"),
            P(),
            P(),
            P(),
            P(),
            P(),
            P(),
            P("gx", "gy"),
            P(None, None, "gx", "gy"),
            P(None, None, "gx", "gy"),
        ),
        out_specs=(P(None, None, "gx", "gy"),) * 3,
        check_vma=False,
    )
```

```python
import jax
import jax.numpy as jnp
from jax import lax
from jax.experimental import pallas as pl
from jax.experimental.pallas import tpu as pltpu
from jax.sharding import PartitionSpec as P


BLOCKS = 32
ROWS = 80
DEEP = 6
NEAR = 3
F32 = jnp.float32

VMEM = pl.BlockSpec(memory_space=pltpu.VMEM)
SMEM = pl.BlockSpec(memory_space=pltpu.SMEM)

STRIP_H = [DEEP] * 3 + [NEAR] * 16
STRIP_AT = [sum(STRIP_H[:n]) for n in range(19)]
PART_H = [DEEP] * 3 + [2, 1] * 4
PART_AT = [2 * sum(PART_H[:n]) for n in range(11)]


def lanes():
    return lax.broadcasted_iota(jnp.int32, (8, 128), 1)


def sublanes():
    return lax.broadcasted_iota(jnp.int32, (8, 128), 0)


def rolled(x, shift, axis):
    size = x.shape[axis]
    shift %= size
    return x if shift == 0 else pltpu.roll(x, shift, axis)


def mirrored(x):
    return jnp.take_along_axis(x, 7 - sublanes(), axis=0)


def ring_tile(from_right, from_left, n):
    h, at = STRIP_H[n], STRIP_AT[n]
    lane = lanes()
    return jnp.where(
        lane < h,
        rolled(from_right, -at, 1),
        jnp.where(lane >= 128 - h, rolled(from_left, 128 - h - at, 1), 0.0),
    )


def gather_kernel(
    place, block_power, ids, bond, sensor, peak, own, to_a, to_b, table, blocks, sems
):
    copies = [
        pltpu.make_async_copy(block_power, table, sems.at[0]),
        pltpu.make_async_copy(ids, blocks, sems.at[1]),
    ]
    for n in range(2, 19):
        for t in range(2):
            cut = pl.ds(128 * t, 128)
            if n == 2:
                source = bond.at[:, cut]
            else:
                field, m = (sensor, n - 3) if n < 11 else (peak, n - 11)
                source = field.at[m // 4, m % 4, :, cut]
            copies.append(
                pltpu.make_async_copy(source, own.at[n, t, pl.ds(8, 64), :], sems.at[len(copies)])
            )
    for copy in copies:
        copy.start()
    copies[0].wait()
    copies[1].wait()
    values = [table[n] for n in range(BLOCKS)]

    def look_up(k):
        stores = []
        for d in range(2):
            for t in range(2):
                index = blocks[d, tile_rows(k), 128 * t : 128 * t + 128]
                level = values
                bit = 1
                while len(level) > 1:
                    odd = (index & bit) != 0
                    level = [
                        jnp.where(odd, level[2 * n + 1], level[2 * n])
                        for n in range(len(level) // 2)
                    ]
                    bit *= 2
                stores.append((own, (d, t, tile_rows(k, 8)), level[0]))
        return stores

    tile_loop(0, 8, 2, look_up)
    for copy in copies[2:]:
        copy.wait()
    even = (place[1] & 1) == 0

    def pack(k):
        lane = lanes()
        stores = []
        right_edge = jnp.zeros((8, 128), F32)
        left_edge = jnp.zeros((8, 128), F32)
        for n in range(19):
            h, at = STRIP_H[n], STRIP_AT[n]
            here = (lane >= at) & (lane < at + h)
            tiles = [own[n, t, tile_rows(k, 8), :] for t in range(2)]
            left_edge = jnp.where(here, rolled(tiles[0], at, 1), left_edge)
            right_edge = jnp.where(here, rolled(tiles[1], at - (128 - h), 1), right_edge)
        stores.append((to_a, (tile_rows(k),), jnp.where(even, right_edge, left_edge)))
        stores.append((to_b, (tile_rows(k),), jnp.where(even, left_edge, right_edge)))
        return stores

    tile_loop(0, 8, 4, pack)


def sides(place, axis, from_a, from_b, rows):
    even = (place[axis] & 1) == 0
    a, b = from_a[rows, :], from_b[rows, :]
    return jnp.where(even, a, b), jnp.where(even, b, a)


def mirror_into(out, own, planes):
    def flip(k):
        return [
            (out, (slot, t, tile_rows(7 - k)), mirrored(own[n, t, tile_rows(k, 8), :]))
            for slot, n in enumerate(planes)
            for t in range(2)
        ]

    tile_loop(0, 8, 2, flip)


def deep_kernel(own, out):
    mirror_into(out, own, (0, 1, 2, 4, 8))


def layers_kernel(own, row_a, sensor_out, peak_out):
    mirror_into(sensor_out, own, (5, 6, 9, 10))
    mirror_into(peak_out, own, (12, 13, 14, 16, 17, 18))


def row_kernel(place, own, col_a, col_b, deep_out, to_a, to_b):
    even = (place[0] & 1) == 0
    row = sublanes()
    strips = []
    for first in (0, 56):
        rows = slice(first, first + 8)
        right, left = sides(place, 1, col_a, col_b, rows)

        def tile(n, t):
            if t < 2:
                return own[n, t, first + 8 : first + 16, :]
            return ring_tile(right, left, n)

        strip = []
        for t in range(3):
            for n in range(3):
                strip.append(tile(n, t))
            for m in range(8):
                x, y = tile(3 + 2 * m, t), tile(4 + 2 * m, t)
                if first == 0:
                    strip.append(jnp.where(row < 4, x, rolled(y, 4, 0)))
                else:
                    strip.append(jnp.where(row >= 4, x, rolled(y, -4, 0)))
        strips.append(strip)
    top, bottom = strips
    for n in range(33):
        rows = slice(8 * n, 8 * n + 8)
        to_a[rows, :] = jnp.where(even, bottom[n], top[n])
        to_b[rows, :] = jnp.where(even, top[n], bottom[n])


def build_kernel(place, start, col_a, col_b, row_a, row_b, deep_in, own, message):
    def core(k):
        right, left = sides(place, 1, col_a, col_b, tile_rows(k))
        return [(own, (n, 2, tile_rows(k, 8)), ring_tile(right, left, n)) for n in range(19)]

    tile_loop(0, 8, 4, core)
    for t in range(3):
        for n in range(11):
            at = 8 * (11 * t + n)
            below, above = sides(place, 0, row_a, row_b, slice(at, at + 8))
            if n < 3:
                own[n, t, 0:8, :] = above
                own[n, t, 72:80, :] = below
            else:
                m = 3 + 2 * (n - 3)
                own[m, t, 0:8, :] = above
                own[m, t, 72:80, :] = below
                own[m + 1, t, 0:8, :] = rolled(above, 4, 0)
                own[m + 1, t, 72:80, :] = rolled(below, -4, 0)

    planes = [0, 1, 2]
    for field in range(2):
        for d in range(2):
            planes += [3 + 8 * field + 4 * d + 3, 3 + 8 * field + 4 * d + 2]

    def pack(k):
        lane = lanes()
        column = jnp.zeros((8, 128), F32)
        for slot, n in enumerate(planes):
            h, at = PART_H[slot], PART_AT[slot]
            here = (lane >= at) & (lane < at + 2 * h)
            column = jnp.where(here, rolled(own[n, 2, tile_rows(k), :], at + h, 1), column)
        return [(message, (tile_rows(9 - k),), mirrored(column))]

    tile_loop(0, 10, 5, pack)
    row = sublanes()
    for n in range(3):
        for t in range(2):
            at = 80 + 16 * (2 * n + t)
            message[at : at + 8, :] = mirrored(own[n, t, 72:80, :])
            message[at + 8 : at + 16, :] = mirrored(own[n, t, 0:8, :])
    for field in range(2):
        for d in range(2):
            n = 3 + 8 * field + 4 * d
            for t in range(2):
                above = jnp.where(
                    row >= 4, own[n + 3, t, 0:8, :], rolled(own[n + 2, t, 0:8, :], 4, 0)
                )
                below = jnp.where(
                    row < 4, own[n + 3, t, 72:80, :], rolled(own[n + 2, t, 72:80, :], 4, 0)
                )
                at = 176 + 16 * (4 * field + 2 * d + t)
                message[at : at + 8, :] = mirrored(below)
                message[at + 8 : at + 16, :] = mirrored(above)


def partner_ring(message, slot, rows):
    h, at = PART_H[slot], PART_AT[slot]
    lane = lanes()
    return jnp.where(
        (lane < h) | (lane >= 128 - h), rolled(message[rows, :], -(at + h), 1), 0.0
    )


class Stores(list):
    def append(self, store):
        ref, index, value = store
        ref[index] = value

    def __iadd__(self, stores):
        for store in stores:
            self.append(store)
        return self


def tile_loop(start, stop, unroll, body):
    def step(j, _):
        stores = []
        for u in range(unroll):
            stores += body(start + unroll * j + u)
        for ref, index, value in stores:
            ref[index] = value
        return 0

    lax.fori_loop(0, (stop - start) // unroll, step, 0)


def tile_rows(k, add=0):
    return pl.ds(pl.multiple_of(8 * k + add, 8), 8)


class Solver:
    def __init__(self, place, tables, d, v, cond):
        self.place, self.d, self.v, self.cond = place, d, v, cond
        layer_class, share, lateral, vertical, sink = tables
        self.coef = []
        for side in range(2):
            die = d if side == 0 else 1 - d
            classes = [layer_class[die, l] for l in range(4)]
            coefs = []
            for l in range(4):
                g = lateral[classes[l]]
                up = vertical[classes[l]] if l < 3 else jnp.float32(0)
                down = vertical[classes[l - 1]] if l > 0 else jnp.float32(0)
                diagonal = 4 * g + up + down
                if l == 0:
                    diagonal = diagonal + sink[die]
                part = share[classes[l]] if share is not None else None
                if l < 3:
                    inverse = 1.0 / jnp.full((8, 128), diagonal, F32)
                    scale = inverse if part is None else inverse * part
                    coefs.append((scale, g * inverse, up * inverse, down * inverse))
                else:
                    coefs.append((diagonal, g, down, part))
            self.coef.append(coefs)
        gy = place[1]
        right = jnp.where(gy == 15, 0.0, 1.0).astype(F32)
        left = jnp.where(gy == 0, 0.0, 1.0).astype(F32)
        self.ring = jnp.where(lanes() < 64, right, left)

    def scaled(self, side, l, t, k, s):
        coef = self.coef[side][l]
        if l < 3:
            s = s * coef[0]
        else:
            if coef[3] is not None:
                s = s * coef[3]
            s = s * self.cond[self.d, 1 + side, t, tile_rows(k)]
        return s * self.ring if t == 2 else s


def prepare(solvers, bond_tile):
    def body(k):
        stores = []
        for solver in solvers:
            for t in range(3):
                bond = bond_tile(solver.d, k, t)
                stores.append((solver.cond, (solver.d, 0, t, tile_rows(k)), bond))
                for side in range(2):
                    value = 1.0 / (solver.coef[side][3][0] + bond)
                    stores.append((solver.cond, (solver.d, 1 + side, t, tile_rows(k)), value))
        return stores

    tile_loop(0, 10, 2, body)


def zero_outside(place, written):
    zero = jnp.zeros((8, 128), F32)
    for here, first in ((place[0] == 0, 8), (place[0] == 15, 80)):

        @pl.when(here)
        def _():
            for ref, at in written:
                for t in range(3):
                    ref[(*at, t, slice(first, first + 8))] = zero


def first(work, unroll=5):
    def body(k):
        stores = []
        for solver, side, layers, source in work:
            for t in range(3):
                shared = {}
                for l in layers:
                    value = solver.scaled(side, l, t, k, source(l, t, tile_rows(k), shared))
                    at = (solver.d, 0, l, t, tile_rows(k, 8))
                    stores.append((solver.v[side], at, value))
        return stores

    tile_loop(0, 10, unroll, body)
    written = [(o.v[side], (o.d, 0, l)) for o, side, layers, _ in work for l in layers]
    zero_outside(work[0][0].place, written)


def sweep(b, work, core_only=False, unroll=5):
    def body(k):
        stores = Stores()
        rows, to = tile_rows(k), tile_rows(k, 8)
        lane = lanes()
        first_lane, last_lane = lane == 0, lane == 127
        seen = {}

        for solver, side, layers, source, emit in work:
            v, d, cond = solver.v, solver.d, solver.cond

            def value(side, l, t):
                key = (id(v[side]), d, l, t)
                if key not in seen:
                    seen[key] = v[side][d, b, l, t, to, :]
                return seen[key]

            shared = {}
            for l in layers:
                coef = solver.coef[side][l]
                forward = [pltpu.roll(value(side, l, t), 1, 1) for t in range(3)]
                backward = [pltpu.roll(value(side, l, t), 127, 1) for t in range(3)]
                for t in range(2 if core_only else 3):
                    left = jnp.where(first_lane, forward[t - 1], forward[t])
                    right = jnp.where(last_lane, backward[(t + 1) % 3], backward[t])
                    around = (left + right) + (
                        v[side][d, b, l, t, pl.ds(8 * k + 7, 8), :]
                        + v[side][d, b, l, t, pl.ds(8 * k + 9, 8), :]
                    )
                    s = source(l, t, rows, shared)
                    if l < 3:
                        total = s * coef[0] + coef[1] * around
                        total = total + coef[2] * value(side, l + 1, t)
                        if l > 0:
                            total = total + coef[3] * value(side, l - 1, t)
                    else:
                        if coef[3] is not None:
                            s = s * coef[3]
                        total = (s + coef[1] * around) + coef[2] * value(side, 2, t)
                        total = total + cond[d, 0, t, rows] * value(1 - side, 3, t)
                        total = total * cond[d, 1 + side, t, rows]
                    if t == 2:
                        total = total * solver.ring
                    if emit is None:
                        stores.append((v[side], (d, 1 - b, l, t, to), total))
                    else:
                        stores += emit(l, t, k, total)
        return stores

    if core_only:
        tile_loop(1, 9, unroll, body)
    else:
        tile_loop(0, 10, unroll, body)
        written = [
            (o.v[side], (o.d, 1 - b, l))
            for o, side, layers, _, emit in work
            if emit is None
            for l in layers
        ]
        if written:
            zero_outside(work[0][0].place, written)


def place_other(planes, layers_in, message, field, d):
    other = 1 - d
    zero = jnp.zeros((8, 128), F32)

    def body(k):
        return [
            (planes, (d, l, t, tile_rows(k, 8)), layers_in(3 * other + l, t, tile_rows(k)))
            for l in range(3)
            for t in range(2)
        ]

    tile_loop(0, 8, 4, body)

    def ring(k):
        column = message[tile_rows(k), :]
        lane = lanes()
        stores = [(planes, (d, 0, 2, tile_rows(k)), zero)]
        for slot_in, l, h in ((0, 2, 2), (1, 1, 1)):
            at = PART_AT[3 + 4 * field + 2 * other + slot_in] + h
            inside = (lane < h) | (lane >= 128 - h)
            tile = jnp.where(inside, rolled(column, -at, 1), 0.0)
            stores.append((planes, (d, l, 2, tile_rows(k)), tile))
        return stores

    tile_loop(0, 10, 5, ring)
    for t in range(2):
        planes[d, 0, t, 0:8, :] = zero
        planes[d, 0, t, 72:80, :] = zero
        at = 176 + 64 * field + 32 * other + 16 * t
        above = message[at : at + 8, :]
        below = message[at + 8 : at + 16, :]
        planes[d, 2, t, 0:8, :] = above
        planes[d, 2, t, 72:80, :] = below
        planes[d, 1, t, 0:8, :] = rolled(above, 4, 0)
        planes[d, 1, t, 72:80, :] = rolled(below, -4, 0)


def place_deep(planes, deep_in, message):
    def body(k):
        return [
            (planes, (n, t, tile_rows(k, 8)), deep_in[n, t, tile_rows(k), :])
            for n in range(3)
            for t in range(2)
        ]

    tile_loop(0, 8, 4, body)

    def ring(k):
        return [
            (planes, (n, 2, tile_rows(k)), partner_ring(message, n, tile_rows(k)))
            for n in range(3)
        ]

    tile_loop(0, 10, 5, ring)
    for n in range(3):
        for t in range(2):
            at = 80 + 16 * (2 * n + t)
            planes[n, t, 0:8, :] = message[at : at + 8, :]
            planes[n, t, 72:80, :] = message[at + 8 : at + 16, :]


EVERY = (0, 1, 2, 3)


def shared_source(ref, *at):
    def source(l, t, rows, shared):
        if t not in shared:
            shared[t] = ref[(*at, t, rows)]
        return shared[t]

    return source


def layer_source(ref, first_layer, *at):
    def source(l, t, rows, shared):
        *head, last = at
        return ref[(*head, last + l - first_layer, t, rows)]

    return source


def thermal_sensor_kernel(
    place, layer_class, share, lateral, vertical, sink, own, deep_in, sensor_in, message,
    thermal, sensed, heat, weighted, early, cond, v_peak,
    v_own, v_other, s_own, s_other, planes, deep, block, sems,
):
    place_deep(deep, deep_in, message)
    plain = (layer_class, None, lateral, vertical, sink)
    with_share = (layer_class, share, lateral, vertical, sink)
    both = range(2)
    hot = [Solver(place, with_share, d, (v_own, v_other), cond) for d in both]
    sense = [Solver(place, plain, d, (s_own, s_other), cond) for d in both]
    weigh = [Solver(place, plain, d, (v_peak, None), cond) for d in both]
    prepare(hot, lambda d, k, t: (own if d == 0 else deep)[2, t, tile_rows(k), :])

    def layers_in(n, t, rows):
        die, l = divmod(n, 3)
        if l == 0:
            return deep_in[3 + die, t, rows, :]
        return sensor_in[2 * die + l - 1, t, rows, :]

    for d in both:
        place_other(planes, layers_in, message, 0, d)
    own_power = [shared_source(own, d) for d in both]
    their_power = [shared_source(deep, 1 - d) for d in both]
    own_sensor = [layer_source(own, 0, 3 + 4 * d) for d in both]
    their_sensor = [layer_source(planes, 1, d, 0) for d in both]
    own_peak = [layer_source(weighted, 0, d, 0) for d in both]

    first(
        [(hot[d], 0, EVERY, own_power[d]) for d in both]
        + [(hot[d], 1, EVERY, their_power[d]) for d in both]
        + [(sense[d], 0, EVERY, own_sensor[d]) for d in both]
        + [(sense[d], 1, (1, 2, 3), their_sensor[d]) for d in both]
    )
    for b, reach in ((0, (2, 3)), (1, (3,))):
        sweep(
            b,
            [(hot[d], 0, EVERY, own_power[d], None) for d in both]
            + [(hot[d], 1, EVERY, their_power[d], None) for d in both]
            + [(sense[d], 0, EVERY, own_sensor[d], None) for d in both]
            + [(sense[d], 1, reach, their_sensor[d], None) for d in both],
        )

    def emit_own(d):
        def emit(l, t, k, total):
            peak = own[11 + 4 * d + l, t, tile_rows(k), :]
            stores = [(weighted, (d, l, t, tile_rows(k)), total * peak)]
            if t < 2:
                stores.append((v_own, (d, 1, l, t, tile_rows(k, 8)), total))
            return stores

        return emit

    def emit_other(d):
        return lambda l, t, k, total: [(heat, (d, l - 1, t, tile_rows(k)), total)]

    def emit_block(d):
        return lambda l, t, k, total: [(block, (d, l, t, tile_rows(k, -8)), total)]

    def emit_early(d):
        return lambda l, t, k, total: [(early, (d, t, tile_rows(k, -8)), total)]

    sweep(
        0,
        [(hot[d], 0, EVERY, own_power[d], emit_own(d)) for d in both]
        + [(hot[d], 1, (1, 2, 3), their_power[d], emit_other(d)) for d in both],
    )
    copies = []

    def send(source, out, d, l, t):
        to = out.at[d, l, :, pl.ds(128 * t, 128)]
        copies.append(pltpu.make_async_copy(source, to, sems.at[len(copies)]))
        copies[-1].start()

    for d in both:
        for l in EVERY:
            for t in range(2):
                send(v_own.at[d, 1, l, t, pl.ds(16, 64), :], thermal, d, l, t)
    sweep(
        0,
        [(sense[d], 0, EVERY, own_sensor[d], emit_block(d)) for d in both],
        core_only=True,
        unroll=4,
    )
    for d in both:
        for l in EVERY:
            for t in range(2):
                send(block.at[d, l, t], sensed, d, l, t)
    first([(weigh[d], 0, EVERY, own_peak[d]) for d in both], unroll=5)
    sweep(0, [(weigh[d], 0, (0, 1, 2), own_peak[d], None) for d in both], unroll=5)
    sweep(1, [(weigh[d], 0, (0, 1), own_peak[d], None) for d in both], unroll=5)
    sweep(
        0,
        [(weigh[d], 0, (0,), own_peak[d], emit_early(d)) for d in both],
        core_only=True,
        unroll=4,
    )
    for copy in copies:
        copy.wait()


def peak_kernel(
    place, layer_class, lateral, vertical, sink, peak_in, message, heat, weighted, early, cond,
    v_start, out, v_peak, v_other, planes, block, sems,
):
    plain = (layer_class, None, lateral, vertical, sink)
    both = range(2)
    copies = []

    def send(source, d, l, t):
        to = out.at[d, l, :, pl.ds(128 * t, 128)]
        copies.append(pltpu.make_async_copy(source, to, sems.at[len(copies)]))
        copies[-1].start()

    for d in both:
        for t in range(2):
            send(early.at[d, t], d, 0, t)
    solver = [Solver(place, plain, d, (v_peak, v_other), cond) for d in both]

    def layers_in(n, t, rows):
        return peak_in[n, t, rows, :]

    for d in both:
        place_other(planes, layers_in, message, 1, d)
    own_peak = [layer_source(weighted, 0, d, 0) for d in both]

    def their_peak(d):
        def source(l, t, rows, shared):
            return planes[d, l - 1, t, rows, :] * heat[d, l - 1, t, rows, :]

        return source

    def emit_block(d):
        return lambda l, t, k, total: [(block, (d, l - 1, t, tile_rows(k, -8)), total)]

    first([(solver[d], 1, (1, 2, 3), their_peak(d)) for d in both], unroll=5)
    sweep(
        0,
        [(solver[d], 0, (3,), own_peak[d], None) for d in both]
        + [(solver[d], 1, (2, 3), their_peak(d), None) for d in both],
        unroll=5,
    )
    sweep(
        1,
        [(solver[d], 0, (2, 3), own_peak[d], None) for d in both]
        + [(solver[d], 1, (3,), their_peak(d), None) for d in both],
        unroll=5,
    )
    for d in both:
        sweep(
            0,
            [(solver[d], 0, (1, 2, 3), own_peak[d], emit_block(d))],
            core_only=True,
            unroll=4,
        )
        for l in (1, 2, 3):
            for t in range(2):
                send(block.at[d, l - 1, t], d, l, t)
    for copy in copies:
        copy.wait()


PLANES = (19, 3, ROWS, 128)
FIELD = (2, 4, 64, 256)
V = (2, 2, 4, 3, ROWS + 16, 128)
OTHER = (2, 3, 3, ROWS, 128)
DEEP_PLANES = (3, 3, ROWS, 128)
KEPT = [
    (2, 3, 3, ROWS, 128),
    (2, 4, 3, ROWS, 128),
    (2, 2, 64, 128),
    (2, 3, 3, ROWS, 128),
    V,
]


def call(kernel, tables, arrays, outs, scratch=(), flops=0, aliases={}, hbm=0, hbm_out=0, vmem=16, name=None):
    shapes = [jax.ShapeDtypeStruct(shape, F32) for shape in outs]
    arrays = [
        pltpu.with_memory_space_constraint(x, pltpu.HBM) if i < hbm else x
        for i, x in enumerate(arrays)
    ]
    anywhere = pl.BlockSpec(memory_space=pltpu.HBM)
    return pl.pallas_call(
        kernel,
        out_shape=shapes,
        in_specs=[SMEM] * len(tables) + [anywhere] * hbm + [VMEM] * (len(arrays) - hbm),
        out_specs=[anywhere] * hbm_out + [VMEM] * (len(shapes) - hbm_out),
        scratch_shapes=[pltpu.VMEM(x, F32) if isinstance(x, tuple) else x for x in scratch],
        input_output_aliases={len(tables) + i: o for i, o in aliases.items()},
        compiler_params=pltpu.CompilerParams(vmem_limit_bytes=vmem << 20),
        cost_estimate=pl.CostEstimate(flops=flops, bytes_accessed=1024, transcendentals=0),
        name=name,
    )(*tables, *arrays)


def pairs(count, odd):
    if odd:
        return [(i, ((i - 1) ^ 1) + 1) for i in range(1, count - 1)]
    return [(i, i ^ 1) for i in range(count)]


def local(
    block_ids,
    block_power,
    layer_class,
    power_share,
    lateral_k,
    vertical_k,
    sink_conductance,
    bond_conductance,
    peak_factors,
    sensor_weight,
):
    nx, ny = lax.axis_size("gx"), lax.axis_size("gy")
    facing = [(i, nx - 1 - i) for i in range(nx)]
    place = jnp.stack([lax.axis_index("gx"), lax.axis_index("gy")]).astype(jnp.int32)
    own, col_a, col_b = call(
        gather_kernel,
        (place,),
        (block_power, block_ids, bond_conductance, sensor_weight, peak_factors),
        [PLANES, (64, 128), (64, 128)],
        [
            pltpu.SMEM((BLOCKS,), F32),
            pltpu.VMEM((2, 64, 256), jnp.int32),
            pltpu.SemaphoreType.DMA((36,)),
        ],
        hbm=5,
        name="gather",
    )
    col_a = lax.ppermute(col_a, "gy", pairs(ny, False))
    col_b = lax.ppermute(col_b, "gy", pairs(ny, True))
    (deep_out,) = call(
        deep_kernel, (), (own,), [(5, 2, 64, 128)], flops=10**11, name="deep_out"
    )
    deep_in = lax.ppermute(deep_out, "gx", facing)
    row_a, row_b = call(
        row_kernel, (place,), (own, col_a, col_b, deep_out), [(264, 128), (264, 128)], flops=10**11, name="rows"
    )
    layers = (6, 2, 64, 128)
    sensor_out, peak_out = call(
        layers_kernel, (), (own, row_a), [(4, 2, 64, 128), layers], flops=10**11, name="layers_out"
    )
    row_a = lax.ppermute(row_a, "gx", pairs(nx, False))
    row_b = lax.ppermute(row_b, "gx", pairs(nx, True))
    sensor_in = lax.ppermute(sensor_out, "gx", facing)
    own, message = call(
        build_kernel,
        (place,),
        (own, col_a, col_b, row_a, row_b, deep_in),
        [PLANES, (304, 128)],
        aliases={0: 0},
        flops=10**11,
        name="build",
    )
    peak_out, _ = lax.optimization_barrier((peak_out, message))
    message = lax.ppermute(message, "gx", facing)
    peak_in = lax.ppermute(peak_out, "gx", facing)
    thermal, sensed, *kept = call(
        thermal_sensor_kernel,
        (place, layer_class, power_share, lateral_k, vertical_k, sink_conductance),
        (own, deep_in, sensor_in, message),
        [FIELD, FIELD] + KEPT,
        [V, V, V, V, OTHER, DEEP_PLANES, (2, 4, 2, 64, 128), pltpu.SemaphoreType.DMA((32,))],
        flops=10**11,
        hbm_out=2,
        vmem=24,
        name="thermal_sensor",
    )
    peak, _ = call(
        peak_kernel,
        (place, layer_class, lateral_k, vertical_k, sink_conductance),
        (peak_in, message, *kept),
        [FIELD, V],
        [V, OTHER, (2, 3, 2, 64, 128), pltpu.SemaphoreType.DMA((16,))],
        aliases={6: 1},
        hbm_out=1,
        name="peak",
    )
    return thermal, peak, sensed


def solution(mesh):
    return jax.shard_map(
        local,
        mesh=mesh,
        in_specs=(
            P(None, "gx", "gy"),
            P(),
            P(),
            P(),
            P(),
            P(),
            P(),
            P("gx", "gy"),
            P(None, None, "gx", "gy"),
            P(None, None, "gx", "gy"),
        ),
        out_specs=(P(None, None, "gx", "gy"),) * 3,
        check_vma=False,
    )
```

```python
import jax
import jax.numpy as jnp
from jax import lax
from jax.experimental import pallas as pl
from jax.experimental.pallas import tpu as pltpu
from jax.sharding import PartitionSpec as P


BLOCKS = 32
ROWS = 80
DEEP = 6
NEAR = 3
F32 = jnp.float32

VMEM = pl.BlockSpec(memory_space=pltpu.VMEM)
SMEM = pl.BlockSpec(memory_space=pltpu.SMEM)

STRIP_H = [DEEP] * 3 + [NEAR] * 16
STRIP_AT = [sum(STRIP_H[:n]) for n in range(19)]
PART_H = [DEEP] * 3 + [2, 1] * 4
PART_AT = [2 * sum(PART_H[:n]) for n in range(11)]


def lanes():
    return lax.broadcasted_iota(jnp.int32, (8, 128), 1)


def sublanes():
    return lax.broadcasted_iota(jnp.int32, (8, 128), 0)


def rolled(x, shift, axis):
    size = x.shape[axis]
    shift %= size
    return x if shift == 0 else pltpu.roll(x, shift, axis)


def mirrored(x):
    return jnp.take_along_axis(x, 7 - sublanes(), axis=0)


def ring_tile(from_right, from_left, n):
    h, at = STRIP_H[n], STRIP_AT[n]
    lane = lanes()
    return jnp.where(
        lane < h,
        rolled(from_right, -at, 1),
        jnp.where(lane >= 128 - h, rolled(from_left, 128 - h - at, 1), 0.0),
    )


def gather_kernel(
    place, block_power, ids, bond, sensor, peak, own, to_a, to_b, table, blocks, sems
):
    copies = [
        pltpu.make_async_copy(block_power, table, sems.at[0]),
        pltpu.make_async_copy(ids, blocks, sems.at[1]),
    ]
    for n in range(2, 19):
        for t in range(2):
            cut = pl.ds(128 * t, 128)
            if n == 2:
                source = bond.at[:, cut]
            else:
                field, m = (sensor, n - 3) if n < 11 else (peak, n - 11)
                source = field.at[m // 4, m % 4, :, cut]
            copies.append(
                pltpu.make_async_copy(source, own.at[n, t, pl.ds(8, 64), :], sems.at[len(copies)])
            )
    for copy in copies:
        copy.start()
    copies[0].wait()
    copies[1].wait()
    values = [table[n] for n in range(BLOCKS)]

    def look_up(k):
        stores = []
        for d in range(2):
            for t in range(2):
                index = blocks[d, tile_rows(k), 128 * t : 128 * t + 128]
                level = values
                bit = 1
                while len(level) > 1:
                    odd = (index & bit) != 0
                    level = [
                        jnp.where(odd, level[2 * n + 1], level[2 * n])
                        for n in range(len(level) // 2)
                    ]
                    bit *= 2
                stores.append((own, (d, t, tile_rows(k, 8)), level[0]))
        return stores

    tile_loop(0, 8, 2, look_up)
    for copy in copies[2:]:
        copy.wait()
    even = (place[1] & 1) == 0

    def pack(k):
        lane = lanes()
        stores = []
        right_edge = jnp.zeros((8, 128), F32)
        left_edge = jnp.zeros((8, 128), F32)
        for n in range(19):
            h, at = STRIP_H[n], STRIP_AT[n]
            here = (lane >= at) & (lane < at + h)
            tiles = [own[n, t, tile_rows(k, 8), :] for t in range(2)]
            left_edge = jnp.where(here, rolled(tiles[0], at, 1), left_edge)
            right_edge = jnp.where(here, rolled(tiles[1], at - (128 - h), 1), right_edge)
        stores.append((to_a, (tile_rows(k),), jnp.where(even, right_edge, left_edge)))
        stores.append((to_b, (tile_rows(k),), jnp.where(even, left_edge, right_edge)))
        return stores

    tile_loop(0, 8, 4, pack)


def sides(place, axis, from_a, from_b, rows):
    even = (place[axis] & 1) == 0
    a, b = from_a[rows, :], from_b[rows, :]
    return jnp.where(even, a, b), jnp.where(even, b, a)


def mirror_into(out, own, planes):
    def flip(k):
        return [
            (out, (slot, t, tile_rows(7 - k)), mirrored(own[n, t, tile_rows(k, 8), :]))
            for slot, n in enumerate(planes)
            for t in range(2)
        ]

    tile_loop(0, 8, 2, flip)


def deep_kernel(own, out):
    mirror_into(out, own, (0, 1, 2, 4, 8))


def layers_kernel(own, row_a, sensor_out, peak_out):
    mirror_into(sensor_out, own, (5, 6, 9, 10))
    mirror_into(peak_out, own, (12, 13, 14, 16, 17, 18))


def row_kernel(place, own, col_a, col_b, deep_out, to_a, to_b):
    even = (place[0] & 1) == 0
    row = sublanes()
    strips = []
    for first in (0, 56):
        rows = slice(first, first + 8)
        right, left = sides(place, 1, col_a, col_b, rows)

        def tile(n, t):
            if t < 2:
                return own[n, t, first + 8 : first + 16, :]
            return ring_tile(right, left, n)

        strip = []
        for t in range(3):
            for n in range(3):
                strip.append(tile(n, t))
            for m in range(8):
                x, y = tile(3 + 2 * m, t), tile(4 + 2 * m, t)
                if first == 0:
                    strip.append(jnp.where(row < 4, x, rolled(y, 4, 0)))
                else:
                    strip.append(jnp.where(row >= 4, x, rolled(y, -4, 0)))
        strips.append(strip)
    top, bottom = strips
    for n in range(33):
        rows = slice(8 * n, 8 * n + 8)
        to_a[rows, :] = jnp.where(even, bottom[n], top[n])
        to_b[rows, :] = jnp.where(even, top[n], bottom[n])


def build_kernel(place, start, col_a, col_b, row_a, row_b, deep_in, own, message):
    def core(k):
        right, left = sides(place, 1, col_a, col_b, tile_rows(k))
        return [(own, (n, 2, tile_rows(k, 8)), ring_tile(right, left, n)) for n in range(19)]

    tile_loop(0, 8, 4, core)
    for t in range(3):
        for n in range(11):
            at = 8 * (11 * t + n)
            below, above = sides(place, 0, row_a, row_b, slice(at, at + 8))
            if n < 3:
                own[n, t, 0:8, :] = above
                own[n, t, 72:80, :] = below
            else:
                m = 3 + 2 * (n - 3)
                own[m, t, 0:8, :] = above
                own[m, t, 72:80, :] = below
                own[m + 1, t, 0:8, :] = rolled(above, 4, 0)
                own[m + 1, t, 72:80, :] = rolled(below, -4, 0)

    planes = [0, 1, 2]
    for field in range(2):
        for d in range(2):
            planes += [3 + 8 * field + 4 * d + 3, 3 + 8 * field + 4 * d + 2]

    def pack(k):
        lane = lanes()
        column = jnp.zeros((8, 128), F32)
        for slot, n in enumerate(planes):
            h, at = PART_H[slot], PART_AT[slot]
            here = (lane >= at) & (lane < at + 2 * h)
            column = jnp.where(here, rolled(own[n, 2, tile_rows(k), :], at + h, 1), column)
        return [(message, (tile_rows(9 - k),), mirrored(column))]

    tile_loop(0, 10, 5, pack)
    row = sublanes()
    for n in range(3):
        for t in range(2):
            at = 80 + 16 * (2 * n + t)
            message[at : at + 8, :] = mirrored(own[n, t, 72:80, :])
            message[at + 8 : at + 16, :] = mirrored(own[n, t, 0:8, :])
    for field in range(2):
        n = 3 + 8 * field
        for t in range(2):
            above = [own[m, t, 0:8, :] for m in (n + 3, n + 2, n + 7, n + 6)]
            below = [own[m, t, 72:80, :] for m in (n + 3, n + 2, n + 7, n + 6)]
            up, down = above[0], below[0]
            for slot in (1, 2, 3):
                up = jnp.where(row >= 8 - 2 * slot, up, rolled(above[slot], -2 * slot, 0))
                down = jnp.where(row < 2 * slot, down, rolled(below[slot], 2 * slot, 0))
            at = 176 + 16 * (2 * field + t)
            message[at : at + 8, :] = mirrored(down)
            message[at + 8 : at + 16, :] = mirrored(up)


def partner_ring(message, slot, rows):
    h, at = PART_H[slot], PART_AT[slot]
    lane = lanes()
    return jnp.where(
        (lane < h) | (lane >= 128 - h), rolled(message[rows, :], -(at + h), 1), 0.0
    )


class Stores(list):
    def append(self, store):
        ref, index, value = store
        ref[index] = value

    def __iadd__(self, stores):
        for store in stores:
            self.append(store)
        return self


def tile_loop(start, stop, unroll, body):
    def step(j, _):
        stores = []
        for u in range(unroll):
            stores += body(start + unroll * j + u)
        for ref, index, value in stores:
            ref[index] = value
        return 0

    lax.fori_loop(0, (stop - start) // unroll, step, 0)


def tile_rows(k, add=0):
    return pl.ds(pl.multiple_of(8 * k + add, 8), 8)


class Solver:
    def __init__(self, place, tables, d, v, cond):
        self.place, self.d, self.v, self.cond = place, d, v, cond
        layer_class, share, lateral, vertical, sink = tables
        self.coef = []
        for side in range(2):
            die = d if side == 0 else 1 - d
            classes = [layer_class[die, l] for l in range(4)]
            coefs = []
            for l in range(4):
                g = lateral[classes[l]]
                up = vertical[classes[l]] if l < 3 else jnp.float32(0)
                down = vertical[classes[l - 1]] if l > 0 else jnp.float32(0)
                diagonal = 4 * g + up + down
                if l == 0:
                    diagonal = diagonal + sink[die]
                part = share[classes[l]] if share is not None else None
                if l < 3:
                    inverse = 1.0 / jnp.full((8, 128), diagonal, F32)
                    scale = inverse if part is None else inverse * part
                    coefs.append((scale, g * inverse, up * inverse, down * inverse))
                else:
                    coefs.append((diagonal, g, down, part))
            self.coef.append(coefs)
        gy = place[1]
        right = jnp.where(gy == 15, 0.0, 1.0).astype(F32)
        left = jnp.where(gy == 0, 0.0, 1.0).astype(F32)
        self.ring = jnp.where(lanes() < 64, right, left)

    def scaled(self, side, l, t, k, s):
        coef = self.coef[side][l]
        if l < 3:
            s = s * coef[0]
        else:
            if coef[3] is not None:
                s = s * coef[3]
            s = s * self.cond[self.d, 1 + side, t, tile_rows(k)]
        return s * self.ring if t == 2 else s


def prepare(solvers, bond_tile):
    def body(k):
        stores = []
        for solver in solvers:
            for t in range(3):
                bond = bond_tile(solver.d, k, t)
                stores.append((solver.cond, (solver.d, 0, t, tile_rows(k)), bond))
                for side in range(2):
                    value = 1.0 / (solver.coef[side][3][0] + bond)
                    stores.append((solver.cond, (solver.d, 1 + side, t, tile_rows(k)), value))
        return stores

    tile_loop(0, 10, 2, body)


def zero_outside(place, written):
    zero = jnp.zeros((8, 128), F32)
    for here, first in ((place[0] == 0, 8), (place[0] == 15, 80)):

        @pl.when(here)
        def _():
            for ref, at in written:
                for t in range(3):
                    ref[(*at, t, slice(first, first + 8))] = zero


def first(work, unroll=5):
    def body(k):
        stores = []
        for solver, side, layers, source in work:
            for t in range(3):
                shared = {}
                for l in layers:
                    value = solver.scaled(side, l, t, k, source(l, t, tile_rows(k), shared))
                    at = (solver.d, 0, l, t, tile_rows(k, 8))
                    stores.append((solver.v[side], at, value))
        return stores

    tile_loop(0, 10, unroll, body)
    written = [(o.v[side], (o.d, 0, l)) for o, side, layers, _ in work for l in layers]
    zero_outside(work[0][0].place, written)


def sweep(b, work, core_only=False, unroll=5):
    def body(k):
        stores = Stores()
        rows, to = tile_rows(k), tile_rows(k, 8)
        lane = lanes()
        first_lane, last_lane = lane == 0, lane == 127
        seen = {}

        for solver, side, layers, source, emit in work:
            v, d, cond = solver.v, solver.d, solver.cond

            def value(side, l, t):
                key = (id(v[side]), d, l, t)
                if key not in seen:
                    seen[key] = v[side][d, b, l, t, to, :]
                return seen[key]

            shared = {}
            for l in layers:
                coef = solver.coef[side][l]
                forward = [pltpu.roll(value(side, l, t), 1, 1) for t in range(3)]
                backward = [pltpu.roll(value(side, l, t), 127, 1) for t in range(3)]
                for t in range(2 if core_only else 3):
                    left = jnp.where(first_lane, forward[t - 1], forward[t])
                    right = jnp.where(last_lane, backward[(t + 1) % 3], backward[t])
                    around = (left + right) + (
                        v[side][d, b, l, t, pl.ds(8 * k + 7, 8), :]
                        + v[side][d, b, l, t, pl.ds(8 * k + 9, 8), :]
                    )
                    s = source(l, t, rows, shared)
                    if l < 3:
                        total = s * coef[0] + coef[1] * around
                        total = total + coef[2] * value(side, l + 1, t)
                        if l > 0:
                            total = total + coef[3] * value(side, l - 1, t)
                    else:
                        if coef[3] is not None:
                            s = s * coef[3]
                        total = (s + coef[1] * around) + coef[2] * value(side, 2, t)
                        total = total + cond[d, 0, t, rows] * value(1 - side, 3, t)
                        total = total * cond[d, 1 + side, t, rows]
                    if t == 2:
                        total = total * solver.ring
                    if emit is None:
                        stores.append((v[side], (d, 1 - b, l, t, to), total))
                    else:
                        stores += emit(l, t, k, total)
        return stores

    if core_only:
        tile_loop(1, 9, unroll, body)
    else:
        tile_loop(0, 10, unroll, body)
        written = [
            (o.v[side], (o.d, 1 - b, l))
            for o, side, layers, _, emit in work
            if emit is None
            for l in layers
        ]
        if written:
            zero_outside(work[0][0].place, written)


def place_other(planes, layers_in, message, field, d):
    other = 1 - d
    zero = jnp.zeros((8, 128), F32)

    def body(k):
        return [
            (planes, (d, l, t, tile_rows(k, 8)), layers_in(3 * other + l, t, tile_rows(k)))
            for l in range(3)
            for t in range(2)
        ]

    tile_loop(0, 8, 4, body)

    def ring(k):
        column = message[tile_rows(k), :]
        lane = lanes()
        stores = [(planes, (d, 0, 2, tile_rows(k)), zero)]
        for slot_in, l, h in ((0, 2, 2), (1, 1, 1)):
            at = PART_AT[3 + 4 * field + 2 * other + slot_in] + h
            inside = (lane < h) | (lane >= 128 - h)
            tile = jnp.where(inside, rolled(column, -at, 1), 0.0)
            stores.append((planes, (d, l, 2, tile_rows(k)), tile))
        return stores

    tile_loop(0, 10, 5, ring)
    for t in range(2):
        planes[d, 0, t, 0:8, :] = zero
        planes[d, 0, t, 72:80, :] = zero
        at = 176 + 16 * (2 * field + t)
        above = message[at : at + 8, :]
        below = message[at + 8 : at + 16, :]
        for l, slot in ((2, 2 * other), (1, 2 * other + 1)):
            planes[d, l, t, 0:8, :] = rolled(above, 2 * slot, 0)
            planes[d, l, t, 72:80, :] = rolled(below, -2 * slot, 0)


def place_deep(planes, deep_in, message):
    def body(k):
        return [
            (planes, (n, t, tile_rows(k, 8)), deep_in[n, t, tile_rows(k), :])
            for n in range(3)
            for t in range(2)
        ]

    tile_loop(0, 8, 4, body)

    def ring(k):
        return [
            (planes, (n, 2, tile_rows(k)), partner_ring(message, n, tile_rows(k)))
            for n in range(3)
        ]

    tile_loop(0, 10, 5, ring)
    for n in range(3):
        for t in range(2):
            at = 80 + 16 * (2 * n + t)
            planes[n, t, 0:8, :] = message[at : at + 8, :]
            planes[n, t, 72:80, :] = message[at + 8 : at + 16, :]


EVERY = (0, 1, 2, 3)


def shared_source(ref, *at):
    def source(l, t, rows, shared):
        if t not in shared:
            shared[t] = ref[(*at, t, rows)]
        return shared[t]

    return source


def layer_source(ref, first_layer, *at):
    def source(l, t, rows, shared):
        *head, last = at
        return ref[(*head, last + l - first_layer, t, rows)]

    return source


def thermal_sensor_kernel(
    place, layer_class, share, lateral, vertical, sink, own, deep_in, sensor_in, message,
    thermal, sensed, heat, weighted, early, cond, v_peak,
    v_own, v_other, s_own, s_other, planes, deep, block, sems,
):
    place_deep(deep, deep_in, message)
    plain = (layer_class, None, lateral, vertical, sink)
    with_share = (layer_class, share, lateral, vertical, sink)
    both = range(2)
    hot = [Solver(place, with_share, d, (v_own, v_other), cond) for d in both]
    sense = [Solver(place, plain, d, (s_own, s_other), cond) for d in both]
    weigh = [Solver(place, plain, d, (v_peak, None), cond) for d in both]
    prepare(hot, lambda d, k, t: (own if d == 0 else deep)[2, t, tile_rows(k), :])

    def layers_in(n, t, rows):
        die, l = divmod(n, 3)
        if l == 0:
            return deep_in[3 + die, t, rows, :]
        return sensor_in[2 * die + l - 1, t, rows, :]

    for d in both:
        place_other(planes, layers_in, message, 0, d)
    own_power = [shared_source(own, d) for d in both]
    their_power = [shared_source(deep, 1 - d) for d in both]
    own_sensor = [layer_source(own, 0, 3 + 4 * d) for d in both]
    their_sensor = [layer_source(planes, 1, d, 0) for d in both]
    own_peak = [layer_source(weighted, 0, d, 0) for d in both]

    first(
        [(hot[d], 0, EVERY, own_power[d]) for d in both]
        + [(hot[d], 1, EVERY, their_power[d]) for d in both]
        + [(sense[d], 0, EVERY, own_sensor[d]) for d in both]
        + [(sense[d], 1, (1, 2, 3), their_sensor[d]) for d in both]
    )
    for b, reach in ((0, (2, 3)), (1, (3,))):
        sweep(
            b,
            [(hot[d], 0, EVERY, own_power[d], None) for d in both]
            + [(hot[d], 1, EVERY, their_power[d], None) for d in both]
            + [(sense[d], 0, EVERY, own_sensor[d], None) for d in both]
            + [(sense[d], 1, reach, their_sensor[d], None) for d in both],
        )

    def emit_own(d):
        def emit(l, t, k, total):
            peak = own[11 + 4 * d + l, t, tile_rows(k), :]
            stores = [(weighted, (d, l, t, tile_rows(k)), total * peak)]
            if t < 2:
                stores.append((v_own, (d, 1, l, t, tile_rows(k, 8)), total))
            return stores

        return emit

    def emit_other(d):
        return lambda l, t, k, total: [(heat, (d, l - 1, t, tile_rows(k)), total)]

    def emit_block(d):
        return lambda l, t, k, total: [(block, (d, l, t, tile_rows(k, -8)), total)]

    def emit_early(d):
        return lambda l, t, k, total: [(early, (d, t, tile_rows(k, -8)), total)]

    sweep(
        0,
        [(hot[d], 0, EVERY, own_power[d], emit_own(d)) for d in both]
        + [(hot[d], 1, (1, 2, 3), their_power[d], emit_other(d)) for d in both],
    )
    copies = []

    def send(source, out, d, l, t):
        to = out.at[d, l, :, pl.ds(128 * t, 128)]
        copies.append(pltpu.make_async_copy(source, to, sems.at[len(copies)]))
        copies[-1].start()

    for d in both:
        for l in EVERY:
            for t in range(2):
                send(v_own.at[d, 1, l, t, pl.ds(16, 64), :], thermal, d, l, t)
    sweep(
        0,
        [(sense[d], 0, EVERY, own_sensor[d], emit_block(d)) for d in both],
        core_only=True,
        unroll=4,
    )
    for d in both:
        for l in EVERY:
            for t in range(2):
                send(block.at[d, l, t], sensed, d, l, t)
    first([(weigh[d], 0, EVERY, own_peak[d]) for d in both], unroll=5)
    sweep(0, [(weigh[d], 0, (0, 1, 2), own_peak[d], None) for d in both], unroll=5)
    sweep(1, [(weigh[d], 0, (0, 1), own_peak[d], None) for d in both], unroll=5)
    sweep(
        0,
        [(weigh[d], 0, (0,), own_peak[d], emit_early(d)) for d in both],
        core_only=True,
        unroll=4,
    )
    for copy in copies:
        copy.wait()


def peak_kernel(
    place, layer_class, lateral, vertical, sink, peak_in, message, heat, weighted, early, cond,
    v_start, out, v_peak, v_other, planes, block, sems,
):
    plain = (layer_class, None, lateral, vertical, sink)
    both = range(2)
    copies = []

    def send(source, d, l, t):
        to = out.at[d, l, :, pl.ds(128 * t, 128)]
        copies.append(pltpu.make_async_copy(source, to, sems.at[len(copies)]))
        copies[-1].start()

    for d in both:
        for t in range(2):
            send(early.at[d, t], d, 0, t)
    solver = [Solver(place, plain, d, (v_peak, v_other), cond) for d in both]

    def layers_in(n, t, rows):
        return peak_in[n, t, rows, :]

    for d in both:
        place_other(planes, layers_in, message, 1, d)
    own_peak = [layer_source(weighted, 0, d, 0) for d in both]

    def their_peak(d):
        def source(l, t, rows, shared):
            return planes[d, l - 1, t, rows, :] * heat[d, l - 1, t, rows, :]

        return source

    def emit_block(d):
        return lambda l, t, k, total: [(block, (d, l - 1, t, tile_rows(k, -8)), total)]

    first([(solver[d], 1, (1, 2, 3), their_peak(d)) for d in both], unroll=5)
    sweep(
        0,
        [(solver[d], 0, (3,), own_peak[d], None) for d in both]
        + [(solver[d], 1, (2, 3), their_peak(d), None) for d in both],
        unroll=5,
    )
    sweep(
        1,
        [(solver[d], 0, (2, 3), own_peak[d], None) for d in both]
        + [(solver[d], 1, (3,), their_peak(d), None) for d in both],
        unroll=5,
    )
    for d in both:
        sweep(
            0,
            [(solver[d], 0, (1, 2, 3), own_peak[d], emit_block(d))],
            core_only=True,
            unroll=4,
        )
        for l in (1, 2, 3):
            for t in range(2):
                send(block.at[d, l - 1, t], d, l, t)
    for copy in copies:
        copy.wait()


PLANES = (19, 3, ROWS, 128)
FIELD = (2, 4, 64, 256)
V = (2, 2, 4, 3, ROWS + 16, 128)
OTHER = (2, 3, 3, ROWS, 128)
DEEP_PLANES = (3, 3, ROWS, 128)
KEPT = [
    (2, 3, 3, ROWS, 128),
    (2, 4, 3, ROWS, 128),
    (2, 2, 64, 128),
    (2, 3, 3, ROWS, 128),
    V,
]


def call(kernel, tables, arrays, outs, scratch=(), flops=0, aliases={}, hbm=0, hbm_out=0, vmem=16, name=None):
    shapes = [jax.ShapeDtypeStruct(shape, F32) for shape in outs]
    arrays = [
        pltpu.with_memory_space_constraint(x, pltpu.HBM) if i < hbm else x
        for i, x in enumerate(arrays)
    ]
    anywhere = pl.BlockSpec(memory_space=pltpu.HBM)
    return pl.pallas_call(
        kernel,
        out_shape=shapes,
        in_specs=[SMEM] * len(tables) + [anywhere] * hbm + [VMEM] * (len(arrays) - hbm),
        out_specs=[anywhere] * hbm_out + [VMEM] * (len(shapes) - hbm_out),
        scratch_shapes=[pltpu.VMEM(x, F32) if isinstance(x, tuple) else x for x in scratch],
        input_output_aliases={len(tables) + i: o for i, o in aliases.items()},
        compiler_params=pltpu.CompilerParams(vmem_limit_bytes=vmem << 20),
        cost_estimate=pl.CostEstimate(flops=flops, bytes_accessed=1024, transcendentals=0),
        name=name,
    )(*tables, *arrays)


def pairs(count, odd):
    if odd:
        return [(i, ((i - 1) ^ 1) + 1) for i in range(1, count - 1)]
    return [(i, i ^ 1) for i in range(count)]


def local(
    block_ids,
    block_power,
    layer_class,
    power_share,
    lateral_k,
    vertical_k,
    sink_conductance,
    bond_conductance,
    peak_factors,
    sensor_weight,
):
    nx, ny = lax.axis_size("gx"), lax.axis_size("gy")
    facing = [(i, nx - 1 - i) for i in range(nx)]
    place = jnp.stack([lax.axis_index("gx"), lax.axis_index("gy")]).astype(jnp.int32)
    own, col_a, col_b = call(
        gather_kernel,
        (place,),
        (block_power, block_ids, bond_conductance, sensor_weight, peak_factors),
        [PLANES, (64, 128), (64, 128)],
        [
            pltpu.SMEM((BLOCKS,), F32),
            pltpu.VMEM((2, 64, 256), jnp.int32),
            pltpu.SemaphoreType.DMA((36,)),
        ],
        hbm=5,
        name="gather",
    )
    col_a = lax.ppermute(col_a, "gy", pairs(ny, False))
    col_b = lax.ppermute(col_b, "gy", pairs(ny, True))
    (deep_out,) = call(
        deep_kernel, (), (own,), [(5, 2, 64, 128)], flops=10**11, name="deep_out"
    )
    deep_in = lax.ppermute(deep_out, "gx", facing)
    row_a, row_b = call(
        row_kernel, (place,), (own, col_a, col_b, deep_out), [(264, 128), (264, 128)], flops=10**11, name="rows"
    )
    layers = (6, 2, 64, 128)
    sensor_out, peak_out = call(
        layers_kernel, (), (own, row_a), [(4, 2, 64, 128), layers], flops=10**11, name="layers_out"
    )
    row_a = lax.ppermute(row_a, "gx", pairs(nx, False))
    row_b = lax.ppermute(row_b, "gx", pairs(nx, True))
    sensor_in = lax.ppermute(sensor_out, "gx", facing)
    own, message = call(
        build_kernel,
        (place,),
        (own, col_a, col_b, row_a, row_b, deep_in),
        [PLANES, (240, 128)],
        aliases={0: 0},
        flops=10**11,
        name="build",
    )
    peak_out, _ = lax.optimization_barrier((peak_out, message))
    message = lax.ppermute(message, "gx", facing)
    peak_in = lax.ppermute(peak_out, "gx", facing)
    thermal, sensed, *kept = call(
        thermal_sensor_kernel,
        (place, layer_class, power_share, lateral_k, vertical_k, sink_conductance),
        (own, deep_in, sensor_in, message),
        [FIELD, FIELD] + KEPT,
        [V, V, V, V, OTHER, DEEP_PLANES, (2, 4, 2, 64, 128), pltpu.SemaphoreType.DMA((32,))],
        flops=10**11,
        hbm_out=2,
        vmem=24,
        name="thermal_sensor",
    )
    peak, _ = call(
        peak_kernel,
        (place, layer_class, lateral_k, vertical_k, sink_conductance),
        (peak_in, message, *kept),
        [FIELD, V],
        [V, OTHER, (2, 3, 2, 64, 128), pltpu.SemaphoreType.DMA((16,))],
        aliases={6: 1},
        hbm_out=1,
        name="peak",
    )
    return thermal, peak, sensed


def solution(mesh):
    return jax.shard_map(
        local,
        mesh=mesh,
        in_specs=(
            P(None, "gx", "gy"),
            P(),
            P(),
            P(),
            P(),
            P(),
            P(),
            P("gx", "gy"),
            P(None, None, "gx", "gy"),
            P(None, None, "gx", "gy"),
        ),
        out_specs=(P(None, None, "gx", "gy"),) * 3,
        check_vma=False,
    )
```

```python
import jax
import jax.numpy as jnp
from jax import lax
from jax.experimental import pallas as pl
from jax.experimental.pallas import tpu as pltpu
from jax.sharding import PartitionSpec as P


BLOCKS = 32
ROWS = 80
DEEP = 6
NEAR = 3
F32 = jnp.float32

VMEM = pl.BlockSpec(memory_space=pltpu.VMEM)
SMEM = pl.BlockSpec(memory_space=pltpu.SMEM)

STRIP_H = [DEEP] * 3 + [NEAR] * 16
STRIP_AT = [sum(STRIP_H[:n]) for n in range(19)]
PART_H = [DEEP] * 3 + [2, 1] * 4
PART_AT = [2 * sum(PART_H[:n]) for n in range(11)]


def lanes():
    return lax.broadcasted_iota(jnp.int32, (8, 128), 1)


def sublanes():
    return lax.broadcasted_iota(jnp.int32, (8, 128), 0)


def rolled(x, shift, axis):
    size = x.shape[axis]
    shift %= size
    return x if shift == 0 else pltpu.roll(x, shift, axis)


def mirrored(x):
    return jnp.take_along_axis(x, 7 - sublanes(), axis=0)


def ring_tile(from_right, from_left, n):
    h, at = STRIP_H[n], STRIP_AT[n]
    lane = lanes()
    return jnp.where(
        lane < h,
        rolled(from_right, -at, 1),
        jnp.where(lane >= 128 - h, rolled(from_left, 128 - h - at, 1), 0.0),
    )


def gather_kernel(
    place, block_power, ids, bond, sensor, peak, own, to_a, to_b, table, blocks, sems
):
    copies = [
        pltpu.make_async_copy(block_power, table, sems.at[0]),
        pltpu.make_async_copy(ids, blocks, sems.at[1]),
    ]
    for n in range(2, 19):
        for t in range(2):
            cut = pl.ds(128 * t, 128)
            if n == 2:
                source = bond.at[:, cut]
            else:
                field, m = (sensor, n - 3) if n < 11 else (peak, n - 11)
                source = field.at[m // 4, m % 4, :, cut]
            copies.append(
                pltpu.make_async_copy(source, own.at[n, t, pl.ds(8, 64), :], sems.at[len(copies)])
            )
    for copy in copies:
        copy.start()
    copies[0].wait()
    copies[1].wait()
    values = [table[n] for n in range(BLOCKS)]

    def look_up(k):
        stores = []
        for d in range(2):
            for t in range(2):
                index = blocks[d, tile_rows(k), 128 * t : 128 * t + 128]
                level = values
                bit = 1
                while len(level) > 1:
                    odd = (index & bit) != 0
                    level = [
                        jnp.where(odd, level[2 * n + 1], level[2 * n])
                        for n in range(len(level) // 2)
                    ]
                    bit *= 2
                stores.append((own, (d, t, tile_rows(k, 8)), level[0]))
        return stores

    tile_loop(0, 8, 2, look_up)
    for copy in copies[2:]:
        copy.wait()
    even = (place[1] & 1) == 0

    def pack(k):
        lane = lanes()
        stores = []
        right_edge = jnp.zeros((8, 128), F32)
        left_edge = jnp.zeros((8, 128), F32)
        for n in range(19):
            h, at = STRIP_H[n], STRIP_AT[n]
            here = (lane >= at) & (lane < at + h)
            tiles = [own[n, t, tile_rows(k, 8), :] for t in range(2)]
            left_edge = jnp.where(here, rolled(tiles[0], at, 1), left_edge)
            right_edge = jnp.where(here, rolled(tiles[1], at - (128 - h), 1), right_edge)
        stores.append((to_a, (tile_rows(k),), jnp.where(even, right_edge, left_edge)))
        stores.append((to_b, (tile_rows(k),), jnp.where(even, left_edge, right_edge)))
        return stores

    tile_loop(0, 8, 4, pack)


def sides(place, axis, from_a, from_b, rows):
    even = (place[axis] & 1) == 0
    a, b = from_a[rows, :], from_b[rows, :]
    return jnp.where(even, a, b), jnp.where(even, b, a)


def mirror_into(out, own, planes):
    def flip(k):
        return [
            (out, (slot, t, tile_rows(7 - k)), mirrored(own[n, t, tile_rows(k, 8), :]))
            for slot, n in enumerate(planes)
            for t in range(2)
        ]

    tile_loop(0, 8, 2, flip)


def deep_kernel(own, out):
    mirror_into(out, own, (0, 1, 2, 4))


def layers_kernel(own, row_a, sensor_out, peak_out):
    mirror_into(sensor_out, own, (5, 6, 8, 9, 10))
    mirror_into(peak_out, own, (12, 13, 14, 16, 17, 18))


def row_kernel(place, own, col_a, col_b, deep_out, to_a, to_b):
    even = (place[0] & 1) == 0
    row = sublanes()
    strips = []
    for first in (0, 56):
        rows = slice(first, first + 8)
        right, left = sides(place, 1, col_a, col_b, rows)

        def tile(n, t):
            if t < 2:
                return own[n, t, first + 8 : first + 16, :]
            return ring_tile(right, left, n)

        strip = []
        for t in range(3):
            for n in range(3):
                strip.append(tile(n, t))
            for m in range(8):
                x, y = tile(3 + 2 * m, t), tile(4 + 2 * m, t)
                if first == 0:
                    strip.append(jnp.where(row < 4, x, rolled(y, 4, 0)))
                else:
                    strip.append(jnp.where(row >= 4, x, rolled(y, -4, 0)))
        strips.append(strip)
    top, bottom = strips
    for n in range(33):
        rows = slice(8 * n, 8 * n + 8)
        to_a[rows, :] = jnp.where(even, bottom[n], top[n])
        to_b[rows, :] = jnp.where(even, top[n], bottom[n])


def build_kernel(place, start, col_a, col_b, row_a, row_b, deep_in, own, message):
    def core(k):
        right, left = sides(place, 1, col_a, col_b, tile_rows(k))
        return [(own, (n, 2, tile_rows(k, 8)), ring_tile(right, left, n)) for n in range(19)]

    tile_loop(0, 8, 4, core)
    for t in range(3):
        for n in range(11):
            at = 8 * (11 * t + n)
            below, above = sides(place, 0, row_a, row_b, slice(at, at + 8))
            if n < 3:
                own[n, t, 0:8, :] = above
                own[n, t, 72:80, :] = below
            else:
                m = 3 + 2 * (n - 3)
                own[m, t, 0:8, :] = above
                own[m, t, 72:80, :] = below
                own[m + 1, t, 0:8, :] = rolled(above, 4, 0)
                own[m + 1, t, 72:80, :] = rolled(below, -4, 0)

    planes = [0, 1, 2]
    for field in range(2):
        for d in range(2):
            planes += [3 + 8 * field + 4 * d + 3, 3 + 8 * field + 4 * d + 2]

    def pack(k):
        lane = lanes()
        column = jnp.zeros((8, 128), F32)
        for slot, n in enumerate(planes):
            h, at = PART_H[slot], PART_AT[slot]
            here = (lane >= at) & (lane < at + 2 * h)
            column = jnp.where(here, rolled(own[n, 2, tile_rows(k), :], at + h, 1), column)
        return [(message, (tile_rows(9 - k),), mirrored(column))]

    tile_loop(0, 10, 5, pack)
    row = sublanes()
    for n in range(3):
        for t in range(2):
            at = 80 + 16 * (2 * n + t)
            message[at : at + 8, :] = mirrored(own[n, t, 72:80, :])
            message[at + 8 : at + 16, :] = mirrored(own[n, t, 0:8, :])
    for field in range(2):
        n = 3 + 8 * field
        for t in range(2):
            above = [own[m, t, 0:8, :] for m in (n + 3, n + 2, n + 7, n + 6)]
            below = [own[m, t, 72:80, :] for m in (n + 3, n + 2, n + 7, n + 6)]
            up, down = above[0], below[0]
            for slot in (1, 2, 3):
                up = jnp.where(row >= 8 - 2 * slot, up, rolled(above[slot], -2 * slot, 0))
                down = jnp.where(row < 2 * slot, down, rolled(below[slot], 2 * slot, 0))
            at = 176 + 16 * (2 * field + t)
            message[at : at + 8, :] = mirrored(down)
            message[at + 8 : at + 16, :] = mirrored(up)


def partner_ring(message, slot, rows):
    h, at = PART_H[slot], PART_AT[slot]
    lane = lanes()
    return jnp.where(
        (lane < h) | (lane >= 128 - h), rolled(message[rows, :], -(at + h), 1), 0.0
    )


class Stores(list):
    def append(self, store):
        ref, index, value = store
        ref[index] = value

    def __iadd__(self, stores):
        for store in stores:
            self.append(store)
        return self


def tile_loop(start, stop, unroll, body):
    def step(j, _):
        stores = []
        for u in range(unroll):
            stores += body(start + unroll * j + u)
        for ref, index, value in stores:
            ref[index] = value
        return 0

    lax.fori_loop(0, (stop - start) // unroll, step, 0)


def tile_rows(k, add=0):
    return pl.ds(pl.multiple_of(8 * k + add, 8), 8)


class Solver:
    def __init__(self, place, tables, d, v, cond):
        self.place, self.d, self.v, self.cond = place, d, v, cond
        layer_class, share, lateral, vertical, sink = tables
        self.coef = []
        for side in range(2):
            die = d if side == 0 else 1 - d
            classes = [layer_class[die, l] for l in range(4)]
            coefs = []
            for l in range(4):
                g = lateral[classes[l]]
                up = vertical[classes[l]] if l < 3 else jnp.float32(0)
                down = vertical[classes[l - 1]] if l > 0 else jnp.float32(0)
                diagonal = 4 * g + up + down
                if l == 0:
                    diagonal = diagonal + sink[die]
                part = share[classes[l]] if share is not None else None
                if l < 3:
                    inverse = 1.0 / jnp.full((8, 128), diagonal, F32)
                    scale = inverse if part is None else inverse * part
                    coefs.append((scale, g * inverse, up * inverse, down * inverse))
                else:
                    coefs.append((diagonal, g, down, part))
            self.coef.append(coefs)
        gy = place[1]
        right = jnp.where(gy == 15, 0.0, 1.0).astype(F32)
        left = jnp.where(gy == 0, 0.0, 1.0).astype(F32)
        self.ring = jnp.where(lanes() < 64, right, left)

    def scaled(self, side, l, t, k, s):
        coef = self.coef[side][l]
        if l < 3:
            s = s * coef[0]
        else:
            if coef[3] is not None:
                s = s * coef[3]
            s = s * self.cond[self.d, 1 + side, t, tile_rows(k)]
        return s * self.ring if t == 2 else s


def prepare(solvers, bond_tile):
    def body(k):
        stores = []
        for solver in solvers:
            for t in range(3):
                bond = bond_tile(solver.d, k, t)
                stores.append((solver.cond, (solver.d, 0, t, tile_rows(k)), bond))
                for side in range(2):
                    value = 1.0 / (solver.coef[side][3][0] + bond)
                    stores.append((solver.cond, (solver.d, 1 + side, t, tile_rows(k)), value))
        return stores

    tile_loop(0, 10, 2, body)


def zero_outside(place, written):
    zero = jnp.zeros((8, 128), F32)
    for here, first in ((place[0] == 0, 8), (place[0] == 15, 80)):

        @pl.when(here)
        def _():
            for ref, at in written:
                for t in range(3):
                    ref[(*at, t, slice(first, first + 8))] = zero


def first(work, unroll=5):
    def body(k):
        stores = []
        for solver, side, layers, source in work:
            for t in range(3):
                shared = {}
                for l in layers:
                    value = solver.scaled(side, l, t, k, source(l, t, tile_rows(k), shared))
                    at = (solver.d, 0, l, t, tile_rows(k, 8))
                    stores.append((solver.v[side], at, value))
        return stores

    tile_loop(0, 10, unroll, body)
    written = [(o.v[side], (o.d, 0, l)) for o, side, layers, _ in work for l in layers]
    zero_outside(work[0][0].place, written)


def sweep(b, work, core_only=False, unroll=5):
    def body(k):
        stores = Stores()
        rows, to = tile_rows(k), tile_rows(k, 8)
        lane = lanes()
        first_lane, last_lane = lane == 0, lane == 127
        seen = {}

        for solver, side, layers, source, emit in work:
            v, d, cond = solver.v, solver.d, solver.cond

            def value(side, l, t):
                key = (id(v[side]), d, l, t)
                if key not in seen:
                    seen[key] = v[side][d, b, l, t, to, :]
                return seen[key]

            shared = {}
            for l in layers:
                coef = solver.coef[side][l]
                forward = [pltpu.roll(value(side, l, t), 1, 1) for t in range(3)]
                backward = [pltpu.roll(value(side, l, t), 127, 1) for t in range(3)]
                for t in range(2 if core_only else 3):
                    left = jnp.where(first_lane, forward[t - 1], forward[t])
                    right = jnp.where(last_lane, backward[(t + 1) % 3], backward[t])
                    around = (left + right) + (
                        v[side][d, b, l, t, pl.ds(8 * k + 7, 8), :]
                        + v[side][d, b, l, t, pl.ds(8 * k + 9, 8), :]
                    )
                    s = source(l, t, rows, shared)
                    if l < 3:
                        total = s * coef[0] + coef[1] * around
                        total = total + coef[2] * value(side, l + 1, t)
                        if l > 0:
                            total = total + coef[3] * value(side, l - 1, t)
                    else:
                        if coef[3] is not None:
                            s = s * coef[3]
                        total = (s + coef[1] * around) + coef[2] * value(side, 2, t)
                        total = total + cond[d, 0, t, rows] * value(1 - side, 3, t)
                        total = total * cond[d, 1 + side, t, rows]
                    if t == 2:
                        total = total * solver.ring
                    if emit is None:
                        stores.append((v[side], (d, 1 - b, l, t, to), total))
                    else:
                        stores += emit(l, t, k, total)
        return stores

    if core_only:
        tile_loop(1, 9, unroll, body)
    else:
        tile_loop(0, 10, unroll, body)
        written = [
            (o.v[side], (o.d, 1 - b, l))
            for o, side, layers, _, emit in work
            if emit is None
            for l in layers
        ]
        if written:
            zero_outside(work[0][0].place, written)


def place_other(planes, layers_in, message, field, d):
    other = 1 - d
    zero = jnp.zeros((8, 128), F32)

    def body(k):
        return [
            (planes, (d, l, t, tile_rows(k, 8)), layers_in(3 * other + l, t, tile_rows(k)))
            for l in range(3)
            for t in range(2)
        ]

    tile_loop(0, 8, 4, body)

    def ring(k):
        column = message[tile_rows(k), :]
        lane = lanes()
        stores = [(planes, (d, 0, 2, tile_rows(k)), zero)]
        for slot_in, l, h in ((0, 2, 2), (1, 1, 1)):
            at = PART_AT[3 + 4 * field + 2 * other + slot_in] + h
            inside = (lane < h) | (lane >= 128 - h)
            tile = jnp.where(inside, rolled(column, -at, 1), 0.0)
            stores.append((planes, (d, l, 2, tile_rows(k)), tile))
        return stores

    tile_loop(0, 10, 5, ring)
    for t in range(2):
        planes[d, 0, t, 0:8, :] = zero
        planes[d, 0, t, 72:80, :] = zero
        at = 176 + 16 * (2 * field + t)
        above = message[at : at + 8, :]
        below = message[at + 8 : at + 16, :]
        for l, slot in ((2, 2 * other), (1, 2 * other + 1)):
            planes[d, l, t, 0:8, :] = rolled(above, 2 * slot, 0)
            planes[d, l, t, 72:80, :] = rolled(below, -2 * slot, 0)


def place_deep(planes, deep_in, message):
    def body(k):
        return [
            (planes, (n, t, tile_rows(k, 8)), deep_in[n, t, tile_rows(k), :])
            for n in range(3)
            for t in range(2)
        ]

    tile_loop(0, 8, 4, body)

    def ring(k):
        return [
            (planes, (n, 2, tile_rows(k)), partner_ring(message, n, tile_rows(k)))
            for n in range(3)
        ]

    tile_loop(0, 10, 5, ring)
    for n in range(3):
        for t in range(2):
            at = 80 + 16 * (2 * n + t)
            planes[n, t, 0:8, :] = message[at : at + 8, :]
            planes[n, t, 72:80, :] = message[at + 8 : at + 16, :]


EVERY = (0, 1, 2, 3)


def shared_source(ref, *at):
    def source(l, t, rows, shared):
        if t not in shared:
            shared[t] = ref[(*at, t, rows)]
        return shared[t]

    return source


def layer_source(ref, first_layer, *at):
    def source(l, t, rows, shared):
        *head, last = at
        return ref[(*head, last + l - first_layer, t, rows)]

    return source


def thermal_sensor_kernel(
    place, layer_class, share, lateral, vertical, sink, own, deep_in, sensor_in, message,
    thermal, sensed, heat, weighted, early, cond, v_peak,
    v_own, v_other, s_own, s_other, planes, deep, block, sems,
):
    place_deep(deep, deep_in, message)
    plain = (layer_class, None, lateral, vertical, sink)
    with_share = (layer_class, share, lateral, vertical, sink)
    both = range(2)
    hot = [Solver(place, with_share, d, (v_own, v_other), cond) for d in both]
    sense = [Solver(place, plain, d, (s_own, s_other), cond) for d in both]
    weigh = [Solver(place, plain, d, (v_peak, None), cond) for d in both]
    prepare(hot, lambda d, k, t: (own if d == 0 else deep)[2, t, tile_rows(k), :])

    def layers_in(n, t, rows):
        if n == 0:
            return deep_in[3, t, rows, :]
        return sensor_in[n - 1, t, rows, :]

    for d in both:
        place_other(planes, layers_in, message, 0, d)
    own_power = [shared_source(own, d) for d in both]
    their_power = [shared_source(deep, 1 - d) for d in both]
    own_sensor = [layer_source(own, 0, 3 + 4 * d) for d in both]
    their_sensor = [layer_source(planes, 1, d, 0) for d in both]
    own_peak = [layer_source(weighted, 0, d, 0) for d in both]

    first(
        [(hot[d], 0, EVERY, own_power[d]) for d in both]
        + [(hot[d], 1, EVERY, their_power[d]) for d in both]
        + [(sense[d], 0, EVERY, own_sensor[d]) for d in both]
        + [(sense[d], 1, (1, 2, 3), their_sensor[d]) for d in both]
    )
    for b, reach in ((0, (2, 3)), (1, (3,))):
        sweep(
            b,
            [(hot[d], 0, EVERY, own_power[d], None) for d in both]
            + [(hot[d], 1, EVERY, their_power[d], None) for d in both]
            + [(sense[d], 0, EVERY, own_sensor[d], None) for d in both]
            + [(sense[d], 1, reach, their_sensor[d], None) for d in both],
        )

    def emit_own(d):
        def emit(l, t, k, total):
            peak = own[11 + 4 * d + l, t, tile_rows(k), :]
            stores = [(weighted, (d, l, t, tile_rows(k)), total * peak)]
            if t < 2:
                stores.append((v_own, (d, 1, l, t, tile_rows(k, 8)), total))
            return stores

        return emit

    def emit_other(d):
        return lambda l, t, k, total: [(heat, (d, l - 1, t, tile_rows(k)), total)]

    def emit_block(d):
        return lambda l, t, k, total: [(block, (d, l, t, tile_rows(k, -8)), total)]

    def emit_early(d):
        return lambda l, t, k, total: [(early, (d, t, tile_rows(k, -8)), total)]

    sweep(
        0,
        [(hot[d], 0, EVERY, own_power[d], emit_own(d)) for d in both]
        + [(hot[d], 1, (1, 2, 3), their_power[d], emit_other(d)) for d in both],
    )
    copies = []

    def send(source, out, d, l, t):
        to = out.at[d, l, :, pl.ds(128 * t, 128)]
        copies.append(pltpu.make_async_copy(source, to, sems.at[len(copies)]))
        copies[-1].start()

    for d in both:
        for l in EVERY:
            for t in range(2):
                send(v_own.at[d, 1, l, t, pl.ds(16, 64), :], thermal, d, l, t)
    sweep(
        0,
        [(sense[d], 0, EVERY, own_sensor[d], emit_block(d)) for d in both],
        core_only=True,
        unroll=4,
    )
    for d in both:
        for l in EVERY:
            for t in range(2):
                send(block.at[d, l, t], sensed, d, l, t)
    first([(weigh[d], 0, EVERY, own_peak[d]) for d in both], unroll=5)
    sweep(0, [(weigh[d], 0, (0, 1, 2), own_peak[d], None) for d in both], unroll=5)
    sweep(1, [(weigh[d], 0, (0, 1), own_peak[d], None) for d in both], unroll=5)
    sweep(
        0,
        [(weigh[d], 0, (0,), own_peak[d], emit_early(d)) for d in both],
        core_only=True,
        unroll=4,
    )
    for copy in copies:
        copy.wait()


def peak_kernel(
    place, layer_class, lateral, vertical, sink, peak_in, message, heat, weighted, early, cond,
    v_start, out, v_peak, v_other, planes, block, sems,
):
    plain = (layer_class, None, lateral, vertical, sink)
    both = range(2)
    copies = []

    def send(source, d, l, t):
        to = out.at[d, l, :, pl.ds(128 * t, 128)]
        copies.append(pltpu.make_async_copy(source, to, sems.at[len(copies)]))
        copies[-1].start()

    for d in both:
        for t in range(2):
            send(early.at[d, t], d, 0, t)
    solver = [Solver(place, plain, d, (v_peak, v_other), cond) for d in both]

    def layers_in(n, t, rows):
        return peak_in[n, t, rows, :]

    for d in both:
        place_other(planes, layers_in, message, 1, d)
    own_peak = [layer_source(weighted, 0, d, 0) for d in both]

    def their_peak(d):
        def source(l, t, rows, shared):
            return planes[d, l - 1, t, rows, :] * heat[d, l - 1, t, rows, :]

        return source

    def emit_block(d):
        return lambda l, t, k, total: [(block, (d, l - 1, t, tile_rows(k, -8)), total)]

    first([(solver[d], 1, (1, 2, 3), their_peak(d)) for d in both], unroll=5)
    sweep(
        0,
        [(solver[d], 0, (3,), own_peak[d], None) for d in both]
        + [(solver[d], 1, (2, 3), their_peak(d), None) for d in both],
        unroll=5,
    )
    sweep(
        1,
        [(solver[d], 0, (2, 3), own_peak[d], None) for d in both]
        + [(solver[d], 1, (3,), their_peak(d), None) for d in both],
        unroll=5,
    )
    for d in both:
        sweep(
            0,
            [(solver[d], 0, (1, 2, 3), own_peak[d], emit_block(d))],
            core_only=True,
            unroll=4,
        )
        for l in (1, 2, 3):
            for t in range(2):
                send(block.at[d, l - 1, t], d, l, t)
    for copy in copies:
        copy.wait()


PLANES = (19, 3, ROWS, 128)
FIELD = (2, 4, 64, 256)
V = (2, 2, 4, 3, ROWS + 16, 128)
OTHER = (2, 3, 3, ROWS, 128)
DEEP_PLANES = (3, 3, ROWS, 128)
KEPT = [
    (2, 3, 3, ROWS, 128),
    (2, 4, 3, ROWS, 128),
    (2, 2, 64, 128),
    (2, 3, 3, ROWS, 128),
    V,
]


def call(kernel, tables, arrays, outs, scratch=(), flops=0, aliases={}, hbm=0, hbm_out=0, vmem=16, name=None):
    shapes = [jax.ShapeDtypeStruct(shape, F32) for shape in outs]
    arrays = [
        pltpu.with_memory_space_constraint(x, pltpu.HBM) if i < hbm else x
        for i, x in enumerate(arrays)
    ]
    anywhere = pl.BlockSpec(memory_space=pltpu.HBM)
    return pl.pallas_call(
        kernel,
        out_shape=shapes,
        in_specs=[SMEM] * len(tables) + [anywhere] * hbm + [VMEM] * (len(arrays) - hbm),
        out_specs=[anywhere] * hbm_out + [VMEM] * (len(shapes) - hbm_out),
        scratch_shapes=[pltpu.VMEM(x, F32) if isinstance(x, tuple) else x for x in scratch],
        input_output_aliases={len(tables) + i: o for i, o in aliases.items()},
        compiler_params=pltpu.CompilerParams(vmem_limit_bytes=vmem << 20),
        cost_estimate=pl.CostEstimate(flops=flops, bytes_accessed=1024, transcendentals=0),
        name=name,
    )(*tables, *arrays)


def pairs(count, odd):
    if odd:
        return [(i, ((i - 1) ^ 1) + 1) for i in range(1, count - 1)]
    return [(i, i ^ 1) for i in range(count)]


def local(
    block_ids,
    block_power,
    layer_class,
    power_share,
    lateral_k,
    vertical_k,
    sink_conductance,
    bond_conductance,
    peak_factors,
    sensor_weight,
):
    nx, ny = lax.axis_size("gx"), lax.axis_size("gy")
    facing = [(i, nx - 1 - i) for i in range(nx)]
    place = jnp.stack([lax.axis_index("gx"), lax.axis_index("gy")]).astype(jnp.int32)
    own, col_a, col_b = call(
        gather_kernel,
        (place,),
        (block_power, block_ids, bond_conductance, sensor_weight, peak_factors),
        [PLANES, (64, 128), (64, 128)],
        [
            pltpu.SMEM((BLOCKS,), F32),
            pltpu.VMEM((2, 64, 256), jnp.int32),
            pltpu.SemaphoreType.DMA((36,)),
        ],
        hbm=5,
        name="gather",
    )
    col_a = lax.ppermute(col_a, "gy", pairs(ny, False))
    col_b = lax.ppermute(col_b, "gy", pairs(ny, True))
    (deep_out,) = call(
        deep_kernel, (), (own,), [(4, 2, 64, 128)], flops=10**11, name="deep_out"
    )
    deep_in = lax.ppermute(deep_out, "gx", facing)
    row_a, row_b = call(
        row_kernel, (place,), (own, col_a, col_b, deep_out), [(264, 128), (264, 128)], flops=10**11, name="rows"
    )
    layers = (6, 2, 64, 128)
    sensor_out, peak_out = call(
        layers_kernel, (), (own, row_a), [(5, 2, 64, 128), layers], flops=10**11, name="layers_out"
    )
    row_a = lax.ppermute(row_a, "gx", pairs(nx, False))
    row_b = lax.ppermute(row_b, "gx", pairs(nx, True))
    sensor_in = lax.ppermute(sensor_out, "gx", facing)
    own, message = call(
        build_kernel,
        (place,),
        (own, col_a, col_b, row_a, row_b, deep_in),
        [PLANES, (240, 128)],
        aliases={0: 0},
        flops=10**11,
        name="build",
    )
    peak_out, _ = lax.optimization_barrier((peak_out, message))
    message = lax.ppermute(message, "gx", facing)
    peak_in = lax.ppermute(peak_out, "gx", facing)
    thermal, sensed, *kept = call(
        thermal_sensor_kernel,
        (place, layer_class, power_share, lateral_k, vertical_k, sink_conductance),
        (own, deep_in, sensor_in, message),
        [FIELD, FIELD] + KEPT,
        [V, V, V, V, OTHER, DEEP_PLANES, (2, 4, 2, 64, 128), pltpu.SemaphoreType.DMA((32,))],
        flops=10**11,
        hbm_out=2,
        vmem=24,
        name="thermal_sensor",
    )
    peak, _ = call(
        peak_kernel,
        (place, layer_class, lateral_k, vertical_k, sink_conductance),
        (peak_in, message, *kept),
        [FIELD, V],
        [V, OTHER, (2, 3, 2, 64, 128), pltpu.SemaphoreType.DMA((16,))],
        aliases={6: 1},
        hbm_out=1,
        name="peak",
    )
    return thermal, peak, sensed


def solution(mesh):
    return jax.shard_map(
        local,
        mesh=mesh,
        in_specs=(
            P(None, "gx", "gy"),
            P(),
            P(),
            P(),
            P(),
            P(),
            P(),
            P("gx", "gy"),
            P(None, None, "gx", "gy"),
            P(None, None, "gx", "gy"),
        ),
        out_specs=(P(None, None, "gx", "gy"),) * 3,
        check_vma=False,
    )
```
